32 devices in a mesh: dp: 2 (over x), row: 4 (over z), col: 4 (over y, core).
Axes of the slice: x: 2, y: 2, z: 4, core: 2. Of those that a mesh axis runs over, the one named last changes fastest.
Arguments:
- layer_input: float32 [2, 1024, 256], P('dp', 'col', 'row'), may hold values from -6 to 6
- segment_ids: int32 [2, 1024], P('dp'), may hold values from 0 to 2, as said below
- head_projection_weights: float32 [2, 3, 256, 256], P(None, None, 'row', 'col'), may hold values from -0.375 to 0.375
- output_projection_weights: float32 [2, 256, 256], P(None, 'col', 'row'), may hold values from -1.5 to 1.5
- up_projection_weights: float32 [2, 256, 1024], P(None, 'row', 'col'), may hold values from -0.375 to 0.375
- down_projection_weights: float32 [2, 1024, 256], P(None, 'col', 'row'), may hold values from -0.1875 to 0.1875
- head_moment: float32 [2, 3, 256, 256], P(None, None, 'row', 'col'), may hold values from -6 to 6
- out_moment: float32 [2, 256, 256], P(None, 'col', 'row'), may hold values from -28 to 28
- up_moment: float32 [2, 256, 1024], P(None, 'row', 'col'), may hold values from -64 to 64
- down_moment: float32 [2, 1024, 256], P(None, 'col', 'row'), may hold values from -128 to 128
- norm_params: float32 [2, 4, 256], P(None, None, 'row')
- norm_first: float32 [2, 4, 256], P(None, None, 'row'), may hold values from -28 to 28
- norm_second: float32 [2, 4, 256], P(None, None, 'row'), may hold values from 2.048 to 8.192
- output_grad: float32 [2, 1024, 256], P('dp', 'col', 'row'), may hold values from -6 to 6
Outputs:
- layer_output: float32 [2, 1024, 256], P('dp', 'col', 'row')
- input_grad: float32 [2, 1024, 256], P('dp', 'col', 'row')
- head_updated: float32 [2, 3, 256, 256], P(None, None, 'row', 'col')
- out_updated: float32 [2, 256, 256], P(None, 'col', 'row')
- up_updated: float32 [2, 256, 1024], P(None, 'row', 'col')
- down_updated: float32 [2, 1024, 256], P(None, 'col', 'row')
- head_momentum: float32 [2, 3, 256, 256], P(None, None, 'row', 'col')
- out_momentum: float32 [2, 256, 256], P(None, 'col', 'row')
- up_momentum: float32 [2, 256, 1024], P(None, 'row', 'col')
- down_momentum: float32 [2, 1024, 256], P(None, 'col', 'row')
- first_moment: float32 [2, 4, 256], P(None, None, 'row')
- second_moment: float32 [2, 4, 256], P(None, None, 'row')
- norm_updated: float32 [2, 4, 256], P(None, None, 'row')
The draws below stay inside these ranges and needn't reach their ends.
Inputs may be any that keep to these rules, and one draw needn't show every extreme that they name: `segment_ids`: along each sequence the ids never fall, and each of 0, 1 and 2 occurs in every sequence.
All inputs are finite; a program needn't handle non-finite values.
Results may differ from the reference program's by a relative error of at most 0.0003.
Values sent between devices are 32-bit elements; how exact they have to be, the bound alone decides.
No kernel may reach another device: no remote copies, remote signals or barrier semaphores. Data moves between devices by JAX's collectives and lax.ppermute only.
A program may use at most 128 MiB of HBM per device.

```python
import math
import jax
import jax.numpy as jnp
from jax import lax

D = 256
FF = 1024
HEADS = 4
LEN = 1024
LAYERS = 2
NS_STEPS = 5
STEP = 10
HD = 64
SEQS = 2
TOKENS = 2048


def draw_segment_ids(key, part):
    key = jax.random.fold_in(key, 11)
    first_key, second_key = jax.random.split(key)
    first_cut = jax.random.randint(first_key, (SEQS, 1), 1, LEN // 4)
    second_cut = jax.random.randint(second_key, (SEQS, 1), 3 * LEN // 4 + 1, LEN)
    position = lax.broadcasted_iota(jnp.int32, (SEQS, LEN), 1)
    return (position >= first_cut).astype(jnp.int32) + (position >= second_cut).astype(jnp.int32)


def draw_norm_params(key, part):
    key = jax.random.fold_in(key, 23)
    noise = jax.random.normal(key, (LAYERS, 4, D), jnp.float32)
    selector = lax.broadcasted_iota(jnp.int32, (LAYERS, 4, D), 1) % 2 == 0
    return jnp.where(selector, 1.0 + 0.1 * noise, 0.3 * noise)


def levels(own_key, shape, shards, low, largest):
    level = 1.0
    for axis_at, parts in shards:
        steps = jax.random.uniform(jax.random.fold_in(jax.random.fold_in(own_key, 6), axis_at), (parts,), jnp.float32, low / len(shards), largest / len(shards))
        level = level * jnp.repeat(jnp.exp(steps), shape[axis_at] // parts).reshape((-1,) + (1,) * (len(shape) - 1 - axis_at))
    return level


def gaussian(own_key, dims, width, bound, cuts=(), kind=jnp.bfloat16):
    values = width * jax.random.normal(own_key, dims, jnp.float32)
    if cuts:
        values = values * levels(own_key, dims, cuts, -0.22, 0.18)
    return jnp.clip(values, -bound, bound).astype(kind)


def setup_inputs(seed: int = 0) -> dict:
    streams_of = jax.random.split(jax.random.key(seed), 15)
    return {
        "layer_input": gaussian(streams_of[0], (SEQS, LEN, D), 1.0, 6.0, ((0, 2), (1, 4), (2, 4)), jnp.float32),
        "segment_ids": draw_segment_ids(jax.random.fold_in(streams_of[14], 71), 0),
        "head_projection_weights": gaussian(streams_of[2], (LAYERS, 3, D, D), D ** -0.5, 0.375, ((2, 4), (3, 4)), jnp.float32),
        "output_projection_weights": gaussian(streams_of[3], (LAYERS, D, D), (D // 16) ** -0.5, 1.5, ((1, 4), (2, 4)), jnp.float32),
        "up_projection_weights": gaussian(streams_of[4], (LAYERS, D, FF), D ** -0.5, 0.375, ((1, 4), (2, 4)), jnp.float32),
        "down_projection_weights": gaussian(streams_of[5], (LAYERS, FF, D), FF ** -0.5, 0.1875, ((1, 4), (2, 4)), jnp.float32),
        "head_moment": gaussian(streams_of[6], (LAYERS, 3, D, D), (0.05 * TOKENS ** 0.5), 6.0, ((2, 4), (3, 4)), jnp.float32),
        "out_moment": gaussian(streams_of[7], (LAYERS, D, D), (0.1 * TOKENS ** 0.5), 28.0, ((1, 4), (2, 4)), jnp.float32),
        "up_moment": gaussian(streams_of[8], (LAYERS, D, FF), (0.25 * TOKENS ** 0.5), 64.0, ((1, 4), (2, 4)), jnp.float32),
        "down_moment": gaussian(streams_of[9], (LAYERS, FF, D), (0.5 * TOKENS ** 0.5), 128.0, ((1, 4), (2, 4)), jnp.float32),
        "norm_params": draw_norm_params(jax.random.fold_in(streams_of[14], 71), 0),
        "norm_first": gaussian(streams_of[11], (LAYERS, 4, D), (0.1 * TOKENS ** 0.5), 28.0, ((2, 4),), jnp.float32),
        "norm_second": jnp.clip(jnp.exp(math.log(8.192) - 1.3862944 * jax.random.uniform(streams_of[12], (LAYERS, 4, D), jnp.float32) ** levels(streams_of[12], (LAYERS, 4, D), ((2, 4),), -0.2, 0.2)), 2.048, 8.192),
        "output_grad": gaussian(streams_of[13], (SEQS, LEN, D), 1.0, 6.0, ((0, 2), (1, 4), (2, 4)), jnp.float32),
    }


@jax.custom_vjp
def low(v):
    return lax.optimization_barrier(v.astype(jnp.bfloat16)).astype(jnp.float32)

@jax.custom_vjp
def low_back(v):
    return v

def low_keep(v):
    return (low(v), None)

def low_pass(kept, grad):
    return (grad,)

def back_keep(v):
    return (v, None)

def back_low(kept, grad):
    return (low(grad),)
low.defvjp(low_keep, low_pass)
low_back.defvjp(back_keep, back_low)
highest_precision = lax.Precision.HIGHEST
norm_eps = 1e-05
newton_coefs = (3.4445, -4.775, 2.0315)
frob_eps = 1e-07
muon_decay = 0.95
muon_rate = 0.5
adam_first = 0.9
adam_second = 0.999
adam_eps = 1e-08
adam_rate = 0.2
masked_score = -1e+30

def matmul(left, right):
    return jnp.dot(left, right, precision=highest_precision, preferred_element_type=jnp.float32)

def layer_norm(values, gain, shift):
    center = values - lax.optimization_barrier(jnp.mean(values, axis=-1, keepdims=True))
    variance = lax.optimization_barrier(jnp.mean(center * center, axis=-1, keepdims=True))
    return center * lax.rsqrt(variance + norm_eps) * gain + shift

def attend(packed):
    queries, key_rows, value_rows, segments = packed
    split_queries = queries.reshape(LEN, HEADS, HD)
    split_keys = key_rows.reshape(LEN, HEADS, HD)
    split_values = value_rows.reshape(LEN, HEADS, HD)
    scores = jnp.einsum('qhd,khd->hqk', split_queries, split_keys, precision=highest_precision) * HD ** (-0.5)
    allowed = segments[:, None] == segments[None, :]
    scores = jnp.where(allowed[None, :, :], scores, masked_score)
    shares = jax.nn.softmax(scores, axis=-1)
    return jnp.einsum('hqk,khd->qhd', shares, split_values, precision=highest_precision).reshape(LEN, D)

def forward(layer_input, head_projection_weights, output_projection_weights, up_projection_weights, down_projection_weights, norm_params, segment_ids):
    hidden = layer_input
    for current_layer_index in range(LAYERS):
        flat = hidden.reshape(TOKENS, D)
        projected = [matmul(flat, head_projection_weights[current_layer_index, member]).reshape(SEQS, LEN, D) for member in range(3)]
        attended = lax.map(jax.checkpoint(attend), (projected[0], projected[1], projected[2], segment_ids))
        branch = matmul(attended.reshape(TOKENS, D), output_projection_weights[current_layer_index])
        middle = layer_norm(flat + branch, norm_params[current_layer_index, 0], norm_params[current_layer_index, 1])
        activated = jax.nn.gelu(matmul(middle, up_projection_weights[current_layer_index]), approximate=False)
        summed = middle + matmul(activated, down_projection_weights[current_layer_index])
        hidden = layer_norm(summed, norm_params[current_layer_index, 2], norm_params[current_layer_index, 3]).reshape(SEQS, LEN, D)
    return hidden

def orthogonal(matrix):
    height, breadth = matrix.shape
    current = matrix.T if height > breadth else matrix
    current = current / (jnp.sqrt(jnp.sum(current * current)) + frob_eps)
    for repeat in range(NS_STEPS):
        gram_matrix = jnp.dot(current, current.T, precision=highest_precision)
        polynomial = newton_coefs[1] * gram_matrix + newton_coefs[2] * jnp.dot(gram_matrix, gram_matrix, precision=highest_precision)
        current = newton_coefs[0] * current + jnp.dot(polynomial, current, precision=highest_precision)
    current = current.T if height > breadth else current
    return current * math.sqrt(max(height, breadth))

def muon_step(weight, moment, gradient, spread):
    renewed = muon_decay * moment + gradient
    return (weight - muon_rate * spread * orthogonal(renewed), renewed)

def reference(layer_input, segment_ids, head_projection_weights, output_projection_weights, up_projection_weights, down_projection_weights, head_moment, out_moment, up_moment, down_moment, norm_params, norm_first, norm_second, output_grad):

    def closure(inputs, head_mats, out_mats, up_mats, down_mats, params):
        return forward(inputs, head_mats, out_mats, up_mats, down_mats, params, segment_ids)
    layer_output, pullback = jax.vjp(closure, layer_input, head_projection_weights, output_projection_weights, up_projection_weights, down_projection_weights, norm_params)
    input_grad, head_grad, out_grad, up_grad, down_grad, norm_grad = pullback(output_grad)
    head_list, head_moms, out_list, out_moms = ([], [], [], [])
    up_list, up_moms, down_list, down_moms = ([], [], [], [])
    for current_layer_index in range(LAYERS):
        new_members, new_moments = ([], [])
        for member in range(3):
            updated, renewed = muon_step(head_projection_weights[current_layer_index, member], head_moment[current_layer_index, member], head_grad[current_layer_index, member], D ** (-0.5))
            new_members.append(updated)
            new_moments.append(renewed)
        head_list.append(jnp.stack(new_members))
        head_moms.append(jnp.stack(new_moments))
        updated, renewed = muon_step(output_projection_weights[current_layer_index], out_moment[current_layer_index], out_grad[current_layer_index], (D // 16) ** (-0.5))
        out_list.append(updated)
        out_moms.append(renewed)
        updated, renewed = muon_step(up_projection_weights[current_layer_index], up_moment[current_layer_index], up_grad[current_layer_index], D ** (-0.5))
        up_list.append(updated)
        up_moms.append(renewed)
        updated, renewed = muon_step(down_projection_weights[current_layer_index], down_moment[current_layer_index], down_grad[current_layer_index], FF ** (-0.5))
        down_list.append(updated)
        down_moms.append(renewed)
    first_moment = adam_first * norm_first + (1.0 - adam_first) * norm_grad
    second_moment = adam_second * norm_second + (1.0 - adam_second) * norm_grad * norm_grad
    corrected_first = first_moment / (1.0 - adam_first ** STEP)
    corrected_second = second_moment / (1.0 - adam_second ** STEP)
    norm_updated = norm_params - adam_rate * corrected_first / (jnp.sqrt(corrected_second) + adam_eps)
    return (layer_output, input_grad, jnp.stack(head_list), jnp.stack(out_list), jnp.stack(up_list), jnp.stack(down_list), jnp.stack(head_moms), jnp.stack(out_moms), jnp.stack(up_moms), jnp.stack(down_moms), first_moment, second_moment, norm_updated)
```

```python
import functools
import math

import jax
import jax.numpy as jnp
from jax import lax
from jax.experimental import pallas as pl
from jax.experimental.pallas import tpu as pltpu
from jax.sharding import PartitionSpec as P

D = 256
FF = 1024
LAYERS = 2
NS_STEPS = 5
STEP = 10
HD = 64
TILE = 128

norm_eps = 1e-05
newton_coefs = (3.4445, -4.775, 2.0315)
frob_eps = 1e-07
muon_decay = 0.95
muon_rate = 0.5
adam_first = 0.9
adam_second = 0.999
adam_eps = 1e-08
adam_rate = 0.2
masked_score = -1e30

f32 = jnp.float32
bf16 = jnp.bfloat16

NN = (((1,), (0,)), ((), ()))
NT = (((1,), (1,)), ((), ()))
TN = (((0,), (0,)), ((), ()))


def dot(a, b, dims=NN):
    return lax.dot_general(a, b, dims, precision=lax.Precision.HIGH, preferred_element_type=f32)


def dot1(a, b, dims=NN):
    return lax.dot_general(a, b, dims, preferred_element_type=f32)


def low_lanes(rows):
    return lax.broadcasted_iota(jnp.int32, (rows, TILE), 1) < HD


def swap(t):
    return pltpu.roll(t, HD, 1)


def dup_low(t):
    return jnp.where(low_lanes(t.shape[0]), t, swap(t))


def dup_high(t):
    return jnp.where(low_lanes(t.shape[0]), swap(t), t)


def halves(t):
    high = t.astype(bf16)
    return high, (t - high.astype(f32)).astype(bf16)


def mixed(t):
    high = t.astype(bf16).astype(f32)
    return jnp.where(low_lanes(t.shape[0]), high, t - high).astype(bf16)


def high_only(t):
    return jnp.where(low_lanes(t.shape[0]), t, 0.0).astype(bf16)


def left_stack(t):
    m = mixed(t)
    return jnp.concatenate([m, m], axis=1)


def right_stack(t):
    high, low = halves(t)
    return jnp.concatenate([high, low], axis=1)


def normalize(values):
    mean = jnp.sum(values, axis=-1, keepdims=True) * (1.0 / D)
    center = values - mean
    variance = jnp.sum(center * center, axis=-1, keepdims=True) * (1.0 / D)
    inverse = lax.rsqrt(variance + norm_eps)
    return center * inverse, inverse


def normalize_back(grad_out, normed, inverse, gain):
    scaled = grad_out * gain
    first = jnp.sum(scaled, axis=-1, keepdims=True) * (1.0 / D)
    second = jnp.sum(scaled * normed, axis=-1, keepdims=True) * (1.0 / D)
    grad_in = inverse * (scaled - first - normed * second)
    gain_grad = jnp.sum(grad_out * normed, axis=0, keepdims=True)
    shift_grad = jnp.sum(grad_out, axis=0, keepdims=True)
    return grad_in, gain_grad, shift_grad


def attention_forward_kernel(
    first, rows, cols, idx_ref, h_ref, pack_ref, ln_ref, segrow_ref, segcol_ref,
    h_out, wkv_out, wqo_out, kv_out, qx_out, att_out, lse_out, mid_out, n1_out, i1_out, *extra
):
    c = idx_ref[0]
    span = mid_out.shape[0]
    for j in range(cols):
        for r in range(rows):
            piece = pack_ref[r * cols + j, 0:HD, :]
            wkv_out[r * HD:(r + 1) * HD, j * TILE:(j + 1) * TILE] = piece[:, :TILE]
            wqo_out[r * HD:(r + 1) * HD, j * TILE:(j + 1) * TILE] = piece[:, TILE:]
    if first:
        for j in range(cols):
            block = jnp.concatenate(
                [pack_ref[r * cols + j, HD:2 * HD, :] for r in range(rows)], axis=0
            )
            h_out[j] = jnp.transpose(block)
        (params_out,) = extra
        tiles = []
        for t in range(rows // 2):
            a = pack_ref[(2 * t) * cols, 2 * HD:2 * HD + 8, 0:TILE]
            b = pack_ref[(2 * t + 1) * cols, 2 * HD:2 * HD + 8, 0:TILE]
            tiles.append(jnp.where(low_lanes(8), a, swap(b)))
        params_out[...] = jnp.concatenate(tiles, axis=1)
        gain, shift = params_out[0:1, :], params_out[1:2, :]
        h_src = h_out
    else:
        h_src = h_ref
        gain, shift = ln_ref[4:5, :], ln_ref[5:6, :]
    wkv = wkv_out[...]
    for j in range(cols):
        kv_out[j * span:(j + 1) * span, :] = dot(h_src[j], wkv)
    h_own = h_src[c]
    qx_out[...] = dot(h_own, wqo_out[...])
    lane = lax.broadcasted_iota(jnp.int32, (span, TILE), 1)
    allowed = segcol_ref[c] == segrow_ref[...]
    lse_all = jnp.zeros((span, TILE), f32)
    for j in range(cols):
        tile = slice(j * TILE, (j + 1) * TILE)
        kv = kv_out[:, tile]
        k_right = right_stack(dup_low(kv))
        v_dup = dup_high(kv)
        v_mix = mixed(v_dup)
        v_high = high_only(v_dup)
        q_left = left_stack(dup_low(qx_out[:, tile]) * (HD ** -0.5))
        scores = jnp.where(allowed, dot1(q_left, k_right, NT), masked_score)
        top = jnp.max(scores, axis=-1, keepdims=True)
        raised = jnp.exp(scores - top)
        total = jnp.sum(raised, axis=-1, keepdims=True)
        p_high, p_low = halves(raised)
        out = dot1(p_high, v_mix) + dot1(p_low, v_high)
        out = (out + swap(out)) / total
        att_out[:, tile] = jnp.where(low_lanes(span), 0.0, out)
        lse_all = jnp.where(lane == j, top + jnp.log(total), lse_all)
    lse_out[...] = jnp.transpose(lse_all)[0:8, :]
    branch = dot(att_out[...], wqo_out[...], NT)
    normed, inverse = normalize(h_own + branch)
    n1_out[...] = normed
    i1_out[...] = jnp.broadcast_to(inverse, (span, TILE))
    mid_out[...] = normed * gain + shift


def feed_forward_kernel(
    layer, rows, cols, up_at, pack_ref, mid_ref, ln_ref,
    h_out, up_out, dn_out, before_out, act_out, n2_out, i2_out
):
    span = mid_ref.shape[0]
    for j in range(cols):
        for r in range(rows):
            at = (slice(r * HD, (r + 1) * HD), slice(j * 2 * TILE, (j + 1) * 2 * TILE))
            up_out[at] = pack_ref[r * cols + j, up_at:up_at + HD, :]
            dn_out[at] = pack_ref[r * cols + j, up_at + HD:up_at + 2 * HD, :]
    mid = mid_ref[...]
    before = dot(mid, up_out[...])
    before_out[...] = before
    activated = 0.5 * before * (1.0 + lax.erf(before * 0.7071067811865476))
    act_out[...] = activated
    feed = dot(activated, dn_out[...], NT)
    normed, inverse = normalize(mid + feed)
    n2_out[...] = normed
    i2_out[...] = jnp.broadcast_to(inverse, (span, TILE))
    h_out[...] = normed * ln_ref[4 * layer + 2:4 * layer + 3, :] + ln_ref[4 * layer + 3:4 * layer + 4, :]


def backward_kernel(
    layer, last, rows, cols, og_at, idx_ref, dh_ref, ln_ref, segrow_ref, segcol_ref, h_ref, wkv_ref, wqo_ref,
    kv_ref, qx_ref, att_ref, lse_ref, n1_ref, i1_ref, up_ref, dn_ref, before_ref, act_ref, n2_ref,
    i2_ref, dh_out, grad_out, dkv, dqx, dbef, dv1_ref, dv2_ref, norm_ref
):
    c = idx_ref[0]
    role = idx_ref[1]
    span = n1_ref.shape[0]
    gains = [ln_ref[4 * layer + k:4 * layer + k + 1, :] for k in range(4)]
    if last:
        block = jnp.concatenate([dh_ref[r * cols + c, og_at:og_at + HD, :] for r in range(rows)], axis=0)
        dh = jnp.transpose(block)
    else:
        dh = dh_ref[0]
        for j in range(1, cols):
            dh = dh + dh_ref[j]
    dv2, gain2, shift2 = normalize_back(dh, n2_ref[...], i2_ref[:, 0:1], gains[2])
    dv2_ref[...] = dv2
    d_act = dot(dv2, dn_ref[...])
    before = before_ref[...]
    slope = (
        0.5 * (1.0 + lax.erf(before * 0.7071067811865476))
        + before * jnp.exp(-0.5 * before * before) * 0.3989422804014327
    )
    dbef[...] = d_act * slope
    d_mid = dv2 + dot(dbef[...], up_ref[...], NT)
    dv1, gain1, shift1 = normalize_back(d_mid, n1_ref[...], i1_ref[:, 0:1], gains[0])
    dv1_ref[...] = dv1
    norm_ref[...] = jnp.zeros_like(norm_ref)
    for k, row in enumerate((gain1, shift1, gain2, shift2)):
        norm_ref[k:k + 1, :] = row
    d_att = dot(dv1, wqo_ref[...])
    lane = lax.broadcasted_iota(jnp.int32, (span, TILE), 1)
    inner_all = jnp.zeros((span, TILE), f32)
    for j in range(cols):
        tile = slice(j * TILE, (j + 1) * TILE)
        inner = jnp.sum(d_att[:, tile] * att_ref[:, tile], axis=-1, keepdims=True)
        inner_all = jnp.where(lane == j, inner, inner_all)
    inner_rows = jnp.transpose(inner_all)
    seg_row = segrow_ref[pl.ds(c, 1), :]
    low = low_lanes(span)
    for j in range(cols):
        tile = slice(j * TILE, (j + 1) * TILE)
        q_dup = dup_low(qx_ref[:, tile]) * (HD ** -0.5)
        q_mix = mixed(q_dup)
        q_left = jnp.concatenate([q_mix, q_mix], axis=1)
        q_high = high_only(q_dup)
        do_dup = dup_high(d_att[:, tile])
        do_mix = mixed(do_dup)
        do_left = jnp.concatenate([do_mix, do_mix], axis=1)
        do_high = high_only(do_dup)
        lse_row = lse_ref[j:j + 1, :]
        inner_row = inner_rows[j:j + 1, :]
        dq_t = jnp.zeros((TILE, span), f32)
        for b in range(cols):
            keys = slice(b * span, (b + 1) * span)
            kv = kv_ref[keys, tile]
            k_dup = dup_low(kv)
            v_dup = dup_high(kv)
            scores = dot1(right_stack(k_dup), q_left, NT)
            shares = jnp.where(segcol_ref[b] == seg_row, jnp.exp(scores - lse_row), 0.0)
            d_shares = dot1(right_stack(v_dup), do_left, NT)
            d_scores = shares * (d_shares - inner_row)
            p_high, p_low = halves(shares)
            s_high, s_low = halves(d_scores)
            dv = dot1(p_high, do_mix) + dot1(p_low, do_high)
            dk = dot1(s_high, q_mix) + dot1(s_low, q_high)
            dkv[keys, tile] = jnp.where(low, dk + swap(dk), dv + swap(dv))
            k_t = jnp.transpose(k_dup)
            k_t_high = k_t.astype(bf16)
            upper = lax.broadcasted_iota(jnp.int32, (TILE, span), 0) < HD
            k_t_mix = jnp.where(upper, k_t_high.astype(f32), k_t - k_t_high.astype(f32)).astype(bf16)
            k_t_only = jnp.where(upper, k_t, 0.0).astype(bf16)
            dq_t = dq_t + dot1(k_t_mix, s_high) + dot1(k_t_only, s_low)
        dq = jnp.transpose(dq_t)
        dqx[:, tile] = jnp.where(low, (dq + swap(dq)) * (HD ** -0.5), 0.0)
    wkv = wkv_ref[...]
    for j in range(cols):
        dh_out[j] = dot(dkv[j * span:(j + 1) * span, :], wkv, NT)
    dh_out[c] += dot(dqx[...], wqo_ref[...], NT) + dv1_ref[...]

    @pl.when(role == 0)
    def _():
        mid = n1_ref[...] * gains[0] + gains[1]
        for j in range(cols):
            grad_out[j] = dot(mid, dbef[:, j * 2 * TILE:(j + 1) * 2 * TILE], TN)

    @pl.when(role == 1)
    def _():
        for j in range(cols):
            grad_out[j] = dot(dv2_ref[...], act_ref[:, j * 2 * TILE:(j + 1) * 2 * TILE], TN)

    @pl.when(role == 2)
    def _():
        total = dot(h_ref[0], dkv[0:span, :], TN)
        for b in range(1, cols):
            total += dot(h_ref[b], dkv[b * span:(b + 1) * span, :], TN)
        for j in range(cols):
            grad_out[j, :, 0:TILE] = total[:, j * TILE:(j + 1) * TILE]
            grad_out[j, :, TILE:] = jnp.zeros((D, TILE), f32)

    @pl.when(role == 3)
    def _():
        total = dot(h_ref[c], dqx[...], TN) + dot(dv1_ref[...], att_ref[...], TN)
        norms = jnp.transpose(norm_ref[...])
        for j in range(cols):
            grad_out[j, :, 0:TILE] = total[:, j * TILE:(j + 1) * TILE]
            grad_out[j, :, TILE:] = norms


def newton_schulz(blocks):
    sizes = [jnp.sum(x * x, keepdims=True) for x in blocks]
    blocks = [x / (jnp.sqrt(s) + frob_eps) for x, s in zip(blocks, sizes)]
    for _ in range(NS_STEPS):
        grams = [dot(x, x, NT) for x in blocks]
        squares = [dot(a, a) for a in grams]
        polys = [newton_coefs[1] * a + newton_coefs[2] * s for a, s in zip(grams, squares)]
        blocks = [newton_coefs[0] * x + dot(p, x) for p, x in zip(polys, blocks)]
    return blocks


def orthogonal_kernel(cols, idx_ref, m_ref, out_ref, work):
    c = idx_ref[0]
    role = idx_ref[1]

    @pl.when(role < 2)
    def _():
        x = jnp.concatenate([m_ref[j] for j in range(cols)], axis=1)
        (x,) = newton_schulz([x])
        for j in range(cols):
            work[j] = x[:, j * 2 * TILE:(j + 1) * 2 * TILE] * math.sqrt(FF)
        out_ref[...] = work[c]

    @pl.when(role >= 2)
    def _():
        low = low_lanes(D)
        tiles = [m_ref[j, :, 0:TILE] for j in range(cols)]
        lefts, rights = [], []
        for t in range(cols // 2):
            a, b = tiles[2 * t], tiles[2 * t + 1]
            lefts.append(jnp.where(low, a, swap(b)))
            rights.append(jnp.where(low, swap(a), b))
        left, right = newton_schulz(
            [jnp.concatenate(lefts, axis=1), jnp.concatenate(rights, axis=1)]
        )
        for t in range(cols // 2):
            a = left[:, t * TILE:(t + 1) * TILE] * math.sqrt(D)
            b = right[:, t * TILE:(t + 1) * TILE] * math.sqrt(D)
            work[2 * t, :, 0:TILE] = jnp.where(low, a, swap(b))
            work[2 * t + 1, :, 0:TILE] = jnp.where(low, swap(a), b)
        out_ref[:, 0:TILE] = work[c, :, 0:TILE]
        out_ref[:, TILE:] = jnp.zeros((D, TILE), f32)


def call(body, operands, outs, scratch=(), flops=0):
    specs = [pl.BlockSpec(memory_space=pltpu.SMEM if x.ndim == 1 else pltpu.VMEM) for x in operands]
    moved = sum(4 * math.prod(x.shape) for x in operands) + sum(4 * math.prod(s) for s in outs)
    return pl.pallas_call(
        body,
        out_shape=[jax.ShapeDtypeStruct(s, f32) for s in outs],
        in_specs=specs,
        out_specs=[pl.BlockSpec(memory_space=pltpu.VMEM) for _ in outs],
        scratch_shapes=[pltpu.VMEM(s, f32) for s in scratch],
        compiler_params=pltpu.CompilerParams(vmem_limit_bytes=50 * 2**20),
        cost_estimate=pl.CostEstimate(flops=flops, bytes_accessed=moved, transcendentals=0),
    )(*operands)


def on_device(
    layer_input,
    segment_ids,
    head_projection_weights,
    output_projection_weights,
    up_projection_weights,
    down_projection_weights,
    head_moment,
    out_moment,
    up_moment,
    down_moment,
    norm_params,
    norm_first,
    norm_second,
    output_grad,
):
    row = lax.axis_index("row").astype(jnp.int32)
    col = lax.axis_index("col").astype(jnp.int32)
    rows = lax.axis_size("row")
    cols = lax.axis_size("col")
    dps = lax.axis_size("dp")
    span = layer_input.shape[1]
    length = span * cols
    idx = jnp.stack([col, row])
    swap2 = lambda x: jnp.swapaxes(x, -1, -2)

    def attention_pack(heads, outs):
        return jnp.concatenate([heads[1], heads[2], heads[0], swap2(outs)], axis=1)

    params = jnp.pad(norm_params.reshape(8, HD), ((0, 0), (0, 2 * TILE - HD)))
    shards = (
        jnp.concatenate(
            [
                attention_pack(head_projection_weights[0], output_projection_weights[0]),
                swap2(layer_input[0]),
                params,
            ]
        ),
        jnp.concatenate([up_projection_weights[0], swap2(down_projection_weights[0])]),
        jnp.concatenate(
            [
                attention_pack(head_projection_weights[1], output_projection_weights[1]),
                up_projection_weights[1],
                swap2(down_projection_weights[1]),
                swap2(output_grad[0]),
            ]
        ),
    )
    pack_a, pack_f, pack_b = [lax.all_gather(s, ("row", "col"), axis=0) for s in shards]
    seg_row = segment_ids.reshape(1, length)
    seg_rows = segment_ids.reshape(cols, span)
    seg_col = segment_ids.reshape(cols, span, 1)

    moments = []
    for l in range(LAYERS):
        blank = jnp.zeros((HD, TILE), f32)
        heads = head_moment[l]
        moments.append(
            jnp.stack(
                [
                    up_moment[l],
                    swap2(down_moment[l]),
                    jnp.concatenate([heads[1], heads[2], blank], axis=1),
                    jnp.concatenate([heads[0], swap2(out_moment[l]), blank], axis=1),
                ]
            )
        )
    moments = lax.all_to_all(jnp.stack(moments, axis=1), "row", 0, 0, tiled=True)

    full = (cols, span, D)
    own = (span, D)
    wide = (span, FF)
    half = (D, cols * TILE)
    one = (span, TILE)
    kept = []
    hidden = jnp.zeros((8, TILE), f32)
    ln = jnp.zeros((8, TILE), f32)
    for l in range(LAYERS):
        first = l == 0
        outs = [full if first else (8, TILE), half, half, (length, cols * TILE), (span, cols * TILE),
                (span, cols * TILE), (8, span), own, own, one]
        if first:
            outs.append((8, D))
        got = call(
            functools.partial(attention_forward_kernel, first, rows, cols),
            [idx, hidden, pack_a if first else pack_b, ln, seg_row, seg_col],
            outs, flops=5 * 10**9,
        )
        h_full, wkv, wqo, kv, qx, att, lse, mid, n1, i1 = got[:10]
        if first:
            ln = got[10]
        else:
            h_full = hidden
        h_own, up, dn, before, act, n2, i2 = call(
            functools.partial(feed_forward_kernel, l, rows, cols, 0 if first else HD),
            [pack_f if first else pack_b, mid, ln],
            [own, (D, FF), (D, FF), wide, wide, own, one], flops=10**9,
        )
        kept.append((h_full, wkv, wqo, kv, qx, att, lse, n1, i1, up, dn, before, act, n2, i2))
        if l + 1 < LAYERS:
            hidden = lax.all_gather(h_own, "col", axis=0)
    layer_output = lax.dynamic_slice(h_own, (0, row * HD), (span, HD))[None]

    swap_pairs = [(0, 1), (1, 0)]
    reduced = [None] * LAYERS
    dh = pack_b
    for l in reversed(range(LAYERS)):
        last = l == LAYERS - 1
        dh_part, grads = call(
            functools.partial(backward_kernel, l, last, rows, cols, 3 * HD),
            [idx, dh, ln, seg_rows, seg_col] + list(kept[l]),
            [full, (cols, D, D)],
            [(length, cols * TILE), (span, cols * TILE), wide, own, own, (TILE, D)], flops=12 * 10**9,
        )
        dh = lax.all_to_all(dh_part, "col", 0, 0, tiled=True)
        mine = lax.psum_scatter(grads, "col", scatter_dimension=0, tiled=False)
        mine = mine + lax.ppermute(mine, "dp", swap_pairs) if dps == 2 else lax.psum(mine, "dp")
        mine = mine + muon_decay * moments[:, l].reshape(D, D)
        whole = lax.all_gather(mine, "col", axis=0)
        (direction,) = call(
            functools.partial(orthogonal_kernel, cols),
            [idx, whole], [(D, D)], [(cols, D, D)], flops=3 * 10**9,
        )
        sent = jnp.concatenate([mine.reshape(rows, HD, D), direction.reshape(rows, HD, D)], axis=1)
        reduced[l] = lax.all_to_all(sent, "row", 0, 0, tiled=True)
    dh = jnp.sum(dh, axis=0)
    input_grad = lax.dynamic_slice(dh, (0, row * HD), (span, HD))[None]

    head_new, out_new, up_new, down_new = [], [], [], []
    head_mom, out_mom, up_mom, down_mom, norm_sum = [], [], [], [], []
    for l in range(LAYERS):
        mom, step = reduced[l][:, :HD], reduced[l][:, HD:] * muon_rate
        parts = lambda x: (jnp.stack([x[3, :, :HD], x[2, :, :HD], x[2, :, HD:TILE]]), swap2(x[3, :, HD:TILE]))
        heads, outs = parts(mom)
        head_mom.append(heads)
        out_mom.append(outs)
        up_mom.append(mom[0])
        down_mom.append(swap2(mom[1]))
        norm_sum.append(swap2(mom[3, :, TILE:TILE + 4]))
        heads, outs = parts(step)
        head_new.append(head_projection_weights[l] - D ** -0.5 * heads)
        out_new.append(output_projection_weights[l] - (D // 16) ** -0.5 * outs)
        up_new.append(up_projection_weights[l] - D ** -0.5 * step[0])
        down_new.append(down_projection_weights[l] - FF ** -0.5 * swap2(step[1]))
    norm_sum = jnp.stack(norm_sum)
    first_moment = adam_first * norm_first + (1.0 - adam_first) * norm_sum
    second_moment = adam_second * norm_second + (1.0 - adam_second) * norm_sum * norm_sum
    corrected_first = first_moment / (1.0 - adam_first**STEP)
    corrected_second = second_moment / (1.0 - adam_second**STEP)
    norm_updated = norm_params - adam_rate * corrected_first / (
        jnp.sqrt(corrected_second) + adam_eps
    )
    return (
        layer_output,
        input_grad,
        jnp.stack(head_new),
        jnp.stack(out_new),
        jnp.stack(up_new),
        jnp.stack(down_new),
        jnp.stack(head_mom),
        jnp.stack(out_mom),
        jnp.stack(up_mom),
        jnp.stack(down_mom),
        first_moment,
        second_moment,
        norm_updated,
    )


def solution(mesh):
    placed = (
        P("dp", "col", "row"),
        P("dp", None),
        P(None, None, "row", "col"),
        P(None, "col", "row"),
        P(None, "row", "col"),
        P(None, "col", "row"),
        P(None, None, "row", "col"),
        P(None, "col", "row"),
        P(None, "row", "col"),
        P(None, "col", "row"),
        P(None, None, "row"),
        P(None, None, "row"),
        P(None, None, "row"),
        P("dp", "col", "row"),
    )
    return jax.shard_map(
        on_device,
        mesh=mesh,
        in_specs=placed,
        out_specs=(
            P("dp", "col", "row"),
            P("dp", "col", "row"),
            P(None, None, "row", "col"),
            P(None, "col", "row"),
            P(None, "row", "col"),
            P(None, "col", "row"),
            P(None, None, "row", "col"),
            P(None, "col", "row"),
            P(None, "row", "col"),
            P(None, "col", "row"),
            P(None, None, "row"),
            P(None, None, "row"),
            P(None, None, "row"),
        ),
        check_vma=False,
    )
```

```python
import functools
import math

import jax
import jax.numpy as jnp
from jax import lax
from jax.experimental import pallas as pl
from jax.experimental.pallas import tpu as pltpu
from jax.sharding import PartitionSpec as P

D = 256
FF = 1024
LAYERS = 2
NS_STEPS = 5
STEP = 10
HD = 64
TILE = 128

norm_eps = 1e-05
newton_coefs = (3.4445, -4.775, 2.0315)
frob_eps = 1e-07
muon_decay = 0.95
muon_rate = 0.5
adam_first = 0.9
adam_second = 0.999
adam_eps = 1e-08
adam_rate = 0.2
masked_score = -1e30

f32 = jnp.float32
bf16 = jnp.bfloat16

NN = (((1,), (0,)), ((), ()))
NT = (((1,), (1,)), ((), ()))
TN = (((0,), (0,)), ((), ()))


def dot(a, b, dims=NN):
    return lax.dot_general(a, b, dims, precision=lax.Precision.HIGH, preferred_element_type=f32)


def dot1(a, b, dims=NN):
    return lax.dot_general(a, b, dims, preferred_element_type=f32)


def low_lanes(rows):
    return lax.broadcasted_iota(jnp.int32, (rows, TILE), 1) < HD


def swap(t):
    return pltpu.roll(t, HD, 1)


def dup_low(t):
    return jnp.where(low_lanes(t.shape[0]), t, swap(t))


def dup_high(t):
    return jnp.where(low_lanes(t.shape[0]), swap(t), t)


def halves(t):
    high = t.astype(bf16)
    return high, (t - high.astype(f32)).astype(bf16)


def mixed(t):
    high = t.astype(bf16).astype(f32)
    return jnp.where(low_lanes(t.shape[0]), high, t - high).astype(bf16)


def high_only(t):
    return jnp.where(low_lanes(t.shape[0]), t, 0.0).astype(bf16)


def left_stack(t):
    m = mixed(t)
    return jnp.concatenate([m, m], axis=1)


def right_stack(t):
    high, low = halves(t)
    return jnp.concatenate([high, low], axis=1)


def normalize(values):
    mean = jnp.sum(values, axis=-1, keepdims=True) * (1.0 / D)
    center = values - mean
    variance = jnp.sum(center * center, axis=-1, keepdims=True) * (1.0 / D)
    inverse = lax.rsqrt(variance + norm_eps)
    return center * inverse, inverse


def normalize_back(grad_out, normed, inverse, gain):
    scaled = grad_out * gain
    first = jnp.sum(scaled, axis=-1, keepdims=True) * (1.0 / D)
    second = jnp.sum(scaled * normed, axis=-1, keepdims=True) * (1.0 / D)
    grad_in = inverse * (scaled - first - normed * second)
    gain_grad = jnp.sum(grad_out * normed, axis=0, keepdims=True)
    shift_grad = jnp.sum(grad_out, axis=0, keepdims=True)
    return grad_in, gain_grad, shift_grad


def pack_reader(gathered, rows, cols, refs, c, z):
    if gathered:
        return lambda r, k, lo, hi: refs[0][(z ^ r) * cols + (c ^ k), lo:hi, :]
    return lambda r, k, lo, hi: refs[k][r, lo:hi, :]


def attention_forward_kernel(
    first, rows, cols, idx_ref, seg_ref, segcol_ref, *refs
):
    c, z = idx_ref[0], idx_ref[1]
    if first:
        packs, refs = refs[:cols], refs[cols:]
    else:
        ln_ref, packs, h_refs, refs = refs[0], refs[1:2], refs[2:2 + cols], refs[2 + cols:]
    h_out, wkv_out, wqo_out, kv_out, qx_out, att_out, lse_out, mid_out, n1_out, i1_out, *extra = refs
    block = pack_reader(not first, rows, cols, packs, c, z)
    span = mid_out.shape[0]
    for j in range(cols):
        for r in range(rows):
            piece = block(r, j, 0, HD)
            wkv_out[r * HD:(r + 1) * HD, j * TILE:(j + 1) * TILE] = piece[:, :TILE]
            wqo_out[r * HD:(r + 1) * HD, j * TILE:(j + 1) * TILE] = piece[:, TILE:]
    if first:
        for j in range(cols):
            h_out[j] = jnp.transpose(
                jnp.concatenate([block(r, j, HD, 2 * HD) for r in range(rows)], axis=0)
            )
        (params_out,) = extra
        tiles = []
        for t in range(rows // 2):
            a = block(2 * t, 0, 2 * HD, 2 * HD + 8)[:, 0:TILE]
            b = block(2 * t + 1, 0, 2 * HD, 2 * HD + 8)[:, 0:TILE]
            tiles.append(jnp.where(low_lanes(8), a, swap(b)))
        params_out[...] = jnp.concatenate(tiles, axis=1)
        gain, shift = params_out[0:1, :], params_out[1:2, :]
    else:
        for j in range(cols):
            h_out[j] = h_refs[j][...]
        gain, shift = ln_ref[4:5, :], ln_ref[5:6, :]
    wkv = wkv_out[...]
    for j in range(cols):
        kv_out[j * span:(j + 1) * span, :] = dot(h_out[j], wkv)
    h_own = h_out[0]
    qx_out[...] = dot(h_own, wqo_out[...])
    lane = lax.broadcasted_iota(jnp.int32, (span, TILE), 1)
    seg_row = jnp.concatenate([seg_ref[pl.ds(c ^ k, 1), :] for k in range(cols)], axis=1)
    allowed = segcol_ref[c] == seg_row
    lse_all = jnp.zeros((span, TILE), f32)
    for j in range(cols):
        tile = slice(j * TILE, (j + 1) * TILE)
        kv = kv_out[:, tile]
        k_right = right_stack(dup_low(kv))
        v_dup = dup_high(kv)
        v_mix = mixed(v_dup)
        v_high = high_only(v_dup)
        q_left = left_stack(dup_low(qx_out[:, tile]) * (HD ** -0.5))
        scores = jnp.where(allowed, dot1(q_left, k_right, NT), masked_score)
        top = jnp.max(scores, axis=-1, keepdims=True)
        raised = jnp.exp(scores - top)
        total = jnp.sum(raised, axis=-1, keepdims=True)
        p_high, p_low = halves(raised)
        out = dot1(p_high, v_mix) + dot1(p_low, v_high)
        out = (out + swap(out)) / total
        att_out[:, tile] = jnp.where(low_lanes(span), 0.0, out)
        lse_all = jnp.where(lane == j, top + jnp.log(total), lse_all)
    lse_out[...] = jnp.transpose(lse_all)[0:8, :]
    branch = dot(att_out[...], wqo_out[...], NT)
    normed, inverse = normalize(h_own + branch)
    n1_out[...] = normed
    i1_out[...] = jnp.broadcast_to(inverse, (span, TILE))
    mid_out[...] = normed * gain + shift


def feed_forward_kernel(layer, rows, cols, up_at, idx_ref, mid_ref, ln_ref, *refs):
    first = layer == 0
    packs, refs = (refs[:cols], refs[cols:]) if first else (refs[:1], refs[1:])
    h_out, up_out, dn_out, before_out, act_out, n2_out, i2_out = refs
    block = pack_reader(not first, rows, cols, packs, idx_ref[0], idx_ref[1])
    span = mid_ref.shape[0]
    for j in range(cols):
        for r in range(rows):
            at = (slice(r * HD, (r + 1) * HD), slice(j * 2 * TILE, (j + 1) * 2 * TILE))
            up_out[at] = block(r, j, up_at, up_at + HD)
            dn_out[at] = block(r, j, up_at + HD, up_at + 2 * HD)
    mid = mid_ref[...]
    before = dot(mid, up_out[...])
    before_out[...] = before
    activated = 0.5 * before * (1.0 + lax.erf(before * 0.7071067811865476))
    act_out[...] = activated
    feed = dot(activated, dn_out[...], NT)
    normed, inverse = normalize(mid + feed)
    n2_out[...] = normed
    i2_out[...] = jnp.broadcast_to(inverse, (span, TILE))
    h_out[...] = normed * ln_ref[4 * layer + 2:4 * layer + 3, :] + ln_ref[4 * layer + 3:4 * layer + 4, :]


def backward_kernel(layer, last, rows, cols, og_at, idx_ref, ln_ref, seg_ref, segcol_ref, *refs):
    c, z = idx_ref[0], idx_ref[1]
    role = z
    dh_refs, refs = (refs[:1], refs[1:]) if last else (refs[:3], refs[3:])
    (h_ref, wkv_ref, wqo_ref, kv_ref, qx_ref, att_ref, lse_ref, n1_ref, i1_ref, up_ref, dn_ref,
     before_ref, act_ref, n2_ref, i2_ref, keep_out, send_out, *refs) = refs
    outs, (dkv, dqx, dbef, dv1_ref, dv2_ref, norm_ref) = refs[:-6], refs[-6:]

    def grad_at(k):
        if last:
            return outs[0].at[c ^ k]
        return outs[k % 2].at[k // 2]

    span = n1_ref.shape[0]
    gains = [ln_ref[4 * layer + k:4 * layer + k + 1, :] for k in range(4)]
    if last:
        dh = jnp.transpose(
            jnp.concatenate(
                [dh_refs[0][(z ^ r) * cols + c, og_at:og_at + HD, :] for r in range(rows)], axis=0
            )
        )
    else:
        dh = dh_refs[0][0] + dh_refs[1][0] + dh_refs[2][...]
    dv2, gain2, shift2 = normalize_back(dh, n2_ref[...], i2_ref[:, 0:1], gains[2])
    dv2_ref[...] = dv2
    d_act = dot(dv2, dn_ref[...])
    before = before_ref[...]
    slope = (
        0.5 * (1.0 + lax.erf(before * 0.7071067811865476))
        + before * jnp.exp(-0.5 * before * before) * 0.3989422804014327
    )
    dbef[...] = d_act * slope
    d_mid = dv2 + dot(dbef[...], up_ref[...], NT)
    dv1, gain1, shift1 = normalize_back(d_mid, n1_ref[...], i1_ref[:, 0:1], gains[0])
    dv1_ref[...] = dv1
    norm_ref[...] = jnp.zeros_like(norm_ref)
    for k, row in enumerate((gain1, shift1, gain2, shift2)):
        norm_ref[k:k + 1, :] = row
    d_att = dot(dv1, wqo_ref[...])
    lane = lax.broadcasted_iota(jnp.int32, (span, TILE), 1)
    inner_all = jnp.zeros((span, TILE), f32)
    for j in range(cols):
        tile = slice(j * TILE, (j + 1) * TILE)
        inner = jnp.sum(d_att[:, tile] * att_ref[:, tile], axis=-1, keepdims=True)
        inner_all = jnp.where(lane == j, inner, inner_all)
    inner_rows = jnp.transpose(inner_all)
    seg_row = seg_ref[pl.ds(c, 1), :]
    low = low_lanes(span)
    for j in range(cols):
        tile = slice(j * TILE, (j + 1) * TILE)
        q_dup = dup_low(qx_ref[:, tile]) * (HD ** -0.5)
        q_mix = mixed(q_dup)
        q_left = jnp.concatenate([q_mix, q_mix], axis=1)
        q_high = high_only(q_dup)
        do_dup = dup_high(d_att[:, tile])
        do_mix = mixed(do_dup)
        do_left = jnp.concatenate([do_mix, do_mix], axis=1)
        do_high = high_only(do_dup)
        lse_row = lse_ref[j:j + 1, :]
        inner_row = inner_rows[j:j + 1, :]
        dq_t = jnp.zeros((TILE, span), f32)
        for b in range(cols):
            keys = slice(b * span, (b + 1) * span)
            kv = kv_ref[keys, tile]
            k_dup = dup_low(kv)
            v_dup = dup_high(kv)
            scores = dot1(right_stack(k_dup), q_left, NT)
            shares = jnp.where(segcol_ref[c ^ b] == seg_row, jnp.exp(scores - lse_row), 0.0)
            d_shares = dot1(right_stack(v_dup), do_left, NT)
            d_scores = shares * (d_shares - inner_row)
            p_high, p_low = halves(shares)
            s_high, s_low = halves(d_scores)
            dv = dot1(p_high, do_mix) + dot1(p_low, do_high)
            dk = dot1(s_high, q_mix) + dot1(s_low, q_high)
            dkv[keys, tile] = jnp.where(low, dk + swap(dk), dv + swap(dv))
            k_t = jnp.transpose(k_dup)
            k_t_high = k_t.astype(bf16)
            upper = lax.broadcasted_iota(jnp.int32, (TILE, span), 0) < HD
            k_t_mix = jnp.where(upper, k_t_high.astype(f32), k_t - k_t_high.astype(f32)).astype(bf16)
            k_t_only = jnp.where(upper, k_t, 0.0).astype(bf16)
            dq_t = dq_t + dot1(k_t_mix, s_high) + dot1(k_t_only, s_low)
        dq = jnp.transpose(dq_t)
        dqx[:, tile] = jnp.where(low, (dq + swap(dq)) * (HD ** -0.5), 0.0)
    wkv = wkv_ref[...]
    for k in range(cols):
        part = dot(dkv[k * span:(k + 1) * span, :], wkv, NT)
        if k == 0:
            part = part + dot(dqx[...], wqo_ref[...], NT) + dv1_ref[...]
        (send_out if k % 2 else keep_out)[k // 2] = part

    @pl.when(role == 0)
    def _():
        mid = n1_ref[...] * gains[0] + gains[1]
        for k in range(cols):
            grad_at(k)[...] = dot(mid, dbef[:, k * 2 * TILE:(k + 1) * 2 * TILE], TN)

    @pl.when(role == 1)
    def _():
        for k in range(cols):
            grad_at(k)[...] = dot(dv2_ref[...], act_ref[:, k * 2 * TILE:(k + 1) * 2 * TILE], TN)

    @pl.when(role == 2)
    def _():
        total = dot(h_ref[0], dkv[0:span, :], TN)
        for b in range(1, cols):
            total += dot(h_ref[b], dkv[b * span:(b + 1) * span, :], TN)
        for k in range(cols):
            grad_at(k)[:, 0:TILE] = total[:, k * TILE:(k + 1) * TILE]
            grad_at(k)[:, TILE:] = jnp.zeros((D, TILE), f32)

    @pl.when(role == 3)
    def _():
        total = dot(h_ref[0], dqx[...], TN) + dot(dv1_ref[...], att_ref[...], TN)
        norms = jnp.transpose(norm_ref[...])
        for k in range(cols):
            grad_at(k)[:, 0:TILE] = total[:, k * TILE:(k + 1) * TILE]
            grad_at(k)[:, TILE:] = norms


def newton_schulz(blocks):
    sizes = [jnp.sum(x * x, keepdims=True) for x in blocks]
    blocks = [x / (jnp.sqrt(s) + frob_eps) for x, s in zip(blocks, sizes)]
    for _ in range(NS_STEPS):
        grams = [dot(x, x, NT) for x in blocks]
        squares = [dot(a, a) for a in grams]
        polys = [newton_coefs[1] * a + newton_coefs[2] * s for a, s in zip(grams, squares)]
        blocks = [newton_coefs[0] * x + dot(p, x) for p, x in zip(polys, blocks)]
    return blocks


def orthogonal_kernel(cols, whole, idx_ref, *refs):
    c, role = idx_ref[0], idx_ref[1]
    out_ref = refs[-1]

    def part(k):
        return refs[0][c ^ k] if whole else refs[k][...]

    @pl.when(role < 2)
    def _():
        (x,) = newton_schulz([jnp.concatenate([part(k) for k in range(cols)], axis=1)])
        out_ref[...] = x[:, 0:2 * TILE] * math.sqrt(FF)

    @pl.when(role >= 2)
    def _():
        low = low_lanes(D)
        tiles = [part(k)[:, 0:TILE] for k in range(cols)]
        lefts, rights = [], []
        for t in range(cols // 2):
            a, b = tiles[2 * t], tiles[2 * t + 1]
            lefts.append(jnp.where(low, a, swap(b)))
            rights.append(jnp.where(low, swap(a), b))
        left, right = newton_schulz(
            [jnp.concatenate(lefts, axis=1), jnp.concatenate(rights, axis=1)]
        )
        out_ref[:, 0:TILE] = jnp.where(low, left[:, 0:TILE], swap(right[:, 0:TILE])) * math.sqrt(D)
        out_ref[:, TILE:] = jnp.zeros((D, TILE), f32)


def call(body, operands, outs, scratch=(), flops=0):
    specs = [pl.BlockSpec(memory_space=pltpu.SMEM if x.ndim == 1 else pltpu.VMEM) for x in operands]
    moved = sum(4 * math.prod(x.shape) for x in operands) + sum(4 * math.prod(s) for s in outs)
    return pl.pallas_call(
        body,
        out_shape=[jax.ShapeDtypeStruct(s, f32) for s in outs],
        in_specs=specs,
        out_specs=[pl.BlockSpec(memory_space=pltpu.VMEM) for _ in outs],
        scratch_shapes=[pltpu.VMEM(s, f32) for s in scratch],
        compiler_params=pltpu.CompilerParams(vmem_limit_bytes=50 * 2**20),
        cost_estimate=pl.CostEstimate(flops=flops, bytes_accessed=moved, transcendentals=0),
    )(*operands)


def on_device(
    layer_input,
    segment_ids,
    head_projection_weights,
    output_projection_weights,
    up_projection_weights,
    down_projection_weights,
    head_moment,
    out_moment,
    up_moment,
    down_moment,
    norm_params,
    norm_first,
    norm_second,
    output_grad,
):
    row = lax.axis_index("row").astype(jnp.int32)
    col = lax.axis_index("col").astype(jnp.int32)
    rows = lax.axis_size("row")
    cols = lax.axis_size("col")
    dps = lax.axis_size("dp")
    span = layer_input.shape[1]
    length = span * cols
    idx = jnp.stack([col, row])
    swap2 = lambda x: jnp.swapaxes(x, -1, -2)

    def perm(x, axis, bit):
        return lax.ppermute(x, axis, [(i, i ^ bit) for i in range(lax.axis_size(axis))])

    def spread_cols(x):
        across = perm(x, "col", 2)
        return [x, perm(x, "col", 1), across, perm(across, "col", 1)]

    def spread_rows(parts):
        return jnp.stack([parts[0]] + [perm(parts[k], "row", k) for k in range(1, rows)])

    def attention_pack(heads, outs):
        return jnp.concatenate([heads[1], heads[2], heads[0], swap2(outs)], axis=1)

    params = jnp.pad(norm_params.reshape(8, HD), ((0, 0), (0, 2 * TILE - HD)))
    shard_a = jnp.concatenate(
        [
            attention_pack(head_projection_weights[0], output_projection_weights[0]),
            swap2(layer_input[0]),
            params,
        ]
    )
    shard_f = jnp.concatenate([up_projection_weights[0], swap2(down_projection_weights[0])])
    shard_b = jnp.concatenate(
        [
            attention_pack(head_projection_weights[1], output_projection_weights[1]),
            up_projection_weights[1],
            swap2(down_projection_weights[1]),
            swap2(output_grad[0]),
        ]
    )
    packs_a = spread_cols(spread_rows([shard_a] * rows))
    packs_f = spread_cols(spread_rows([shard_f] * rows))
    pack_b = lax.all_gather(shard_b, ("row", "col"), axis=0)
    seg_rows = segment_ids.reshape(cols, span)
    seg_col = segment_ids.reshape(cols, span, 1)

    order = row ^ jnp.arange(rows, dtype=jnp.int32)
    moments = []
    for l in range(LAYERS):
        blank = jnp.zeros((HD, TILE), f32)
        heads = head_moment[l]
        moments.append(
            jnp.stack(
                [
                    up_moment[l],
                    swap2(down_moment[l]),
                    jnp.concatenate([heads[1], heads[2], blank], axis=1),
                    jnp.concatenate([heads[0], swap2(out_moment[l]), blank], axis=1),
                ]
            )
        )
    moments = jnp.take(jnp.stack(moments, axis=1), order, axis=0)
    moments = spread_rows([moments[k] for k in range(rows)]) * muon_decay

    full = (cols, span, D)
    pair = (2, span, D)
    own = (span, D)
    wide = (span, FF)
    half = (D, cols * TILE)
    one = (span, TILE)
    kept = []
    for l in range(LAYERS):
        first = l == 0
        outs = [full, half, half, (length, cols * TILE), (span, cols * TILE),
                (span, cols * TILE), (8, span), own, own, one]
        if first:
            outs.append((8, D))
        got = call(
            functools.partial(attention_forward_kernel, first, rows, cols),
            [idx, seg_rows, seg_col] + (packs_a if first else [ln, pack_b] + hidden),
            outs, flops=5 * 10**9,
        )
        h_full, wkv, wqo, kv, qx, att, lse, mid, n1, i1 = got[:10]
        if first:
            ln = got[10]
        h_own, up, dn, before, act, n2, i2 = call(
            functools.partial(feed_forward_kernel, l, rows, cols, 0 if first else HD),
            [idx, mid, ln] + (packs_f if first else [pack_b]),
            [own, (D, FF), (D, FF), wide, wide, own, one], flops=10**9,
        )
        kept.append((h_full, wkv, wqo, kv, qx, att, lse, n1, i1, up, dn, before, act, n2, i2))
        if l + 1 < LAYERS:
            hidden = spread_cols(h_own)
    layer_output = h_own[:, :HD][None]

    def fold_core(keep, send):
        got = perm(send, "col", 1)
        return got, perm(keep[1] + got[1], "col", 2)

    reduced = [None] * LAYERS
    dh = [pack_b]
    for l in reversed(range(LAYERS)):
        last = l == LAYERS - 1
        keep, send, *grads = call(
            functools.partial(backward_kernel, l, last, rows, cols, 3 * HD),
            [idx, ln, seg_rows, seg_col] + dh + list(kept[l]),
            [pair, pair] + ([(cols, D, D)] if last else [(2, D, D), (2, D, D)]),
            [(length, cols * TILE), (span, cols * TILE), wide, own, own, (TILE, D)], flops=12 * 10**9,
        )
        if last:
            mine = lax.psum_scatter(grads[0], "col", scatter_dimension=0, tiled=False)
        else:
            got, across = fold_core(*grads)
            mine = grads[0][0] + got[0] + across
        got, across = fold_core(keep, send)
        dh = [keep, got, across]
        mine = mine + perm(mine, "dp", 1) if dps == 2 else lax.psum(mine, "dp")
        mine = mine + moments[:, l].reshape(D, D)
        parts = [lax.all_gather(mine, "col", axis=0)] if last else spread_cols(mine)
        (direction,) = call(
            functools.partial(orthogonal_kernel, cols, last),
            [idx] + parts, [(D, D)], flops=3 * 10**9,
        )
        blocks = [
            jnp.take(spread_rows(list(x.reshape(rows, HD, D))), order, axis=0)
            for x in (mine, direction)
        ]
        reduced[l] = blocks
    input_grad = (dh[0][0] + dh[1][0] + dh[2])[:, :HD][None]

    head_new, out_new, up_new, down_new = [], [], [], []
    head_mom, out_mom, up_mom, down_mom, norm_sum = [], [], [], [], []
    for l in range(LAYERS):
        mom, step = reduced[l][0], reduced[l][1] * muon_rate
        parts = lambda x: (jnp.stack([x[3, :, :HD], x[2, :, :HD], x[2, :, HD:TILE]]), swap2(x[3, :, HD:TILE]))
        heads, outs = parts(mom)
        head_mom.append(heads)
        out_mom.append(outs)
        up_mom.append(mom[0])
        down_mom.append(swap2(mom[1]))
        norm_sum.append(swap2(mom[3, :, TILE:TILE + 4]))
        heads, outs = parts(step)
        head_new.append(head_projection_weights[l] - D ** -0.5 * heads)
        out_new.append(output_projection_weights[l] - (D // 16) ** -0.5 * outs)
        up_new.append(up_projection_weights[l] - D ** -0.5 * step[0])
        down_new.append(down_projection_weights[l] - FF ** -0.5 * swap2(step[1]))
    norm_sum = jnp.stack(norm_sum)
    first_moment = adam_first * norm_first + (1.0 - adam_first) * norm_sum
    second_moment = adam_second * norm_second + (1.0 - adam_second) * norm_sum * norm_sum
    corrected_first = first_moment / (1.0 - adam_first**STEP)
    corrected_second = second_moment / (1.0 - adam_second**STEP)
    norm_updated = norm_params - adam_rate * corrected_first / (
        jnp.sqrt(corrected_second) + adam_eps
    )
    return (
        layer_output,
        input_grad,
        jnp.stack(head_new),
        jnp.stack(out_new),
        jnp.stack(up_new),
        jnp.stack(down_new),
        jnp.stack(head_mom),
        jnp.stack(out_mom),
        jnp.stack(up_mom),
        jnp.stack(down_mom),
        first_moment,
        second_moment,
        norm_updated,
    )


def solution(mesh):
    placed = (
        P("dp", "col", "row"),
        P("dp", None),
        P(None, None, "row", "col"),
        P(None, "col", "row"),
        P(None, "row", "col"),
        P(None, "col", "row"),
        P(None, None, "row", "col"),
        P(None, "col", "row"),
        P(None, "row", "col"),
        P(None, "col", "row"),
        P(None, None, "row"),
        P(None, None, "row"),
        P(None, None, "row"),
        P("dp", "col", "row"),
    )
    return jax.shard_map(
        on_device,
        mesh=mesh,
        in_specs=placed,
        out_specs=(
            P("dp", "col", "row"),
            P("dp", "col", "row"),
            P(None, None, "row", "col"),
            P(None, "col", "row"),
            P(None, "row", "col"),
            P(None, "col", "row"),
            P(None, None, "row", "col"),
            P(None, "col", "row"),
            P(None, "row", "col"),
            P(None, "col", "row"),
            P(None, None, "row"),
            P(None, None, "row"),
            P(None, None, "row"),
        ),
        check_vma=False,
    )
```

```python
import functools
import math

import jax
import jax.numpy as jnp
from jax import lax
from jax.experimental import pallas as pl
from jax.experimental.pallas import tpu as pltpu
from jax.sharding import PartitionSpec as P

D = 256
FF = 1024
LAYERS = 2
NS_STEPS = 5
STEP = 10
HD = 64
TILE = 128

norm_eps = 1e-05
newton_coefs = (3.4445, -4.775, 2.0315)
frob_eps = 1e-07
muon_decay = 0.95
muon_rate = 0.5
adam_first = 0.9
adam_second = 0.999
adam_eps = 1e-08
adam_rate = 0.2
masked_score = -1e30

f32 = jnp.float32
bf16 = jnp.bfloat16

NN = (((1,), (0,)), ((), ()))
NT = (((1,), (1,)), ((), ()))
TN = (((0,), (0,)), ((), ()))


def dot(a, b, dims=NN):
    return lax.dot_general(a, b, dims, precision=lax.Precision.HIGH, preferred_element_type=f32)


def dot1(a, b, dims=NN):
    return lax.dot_general(a, b, dims, preferred_element_type=f32)


def low_lanes(rows):
    return lax.broadcasted_iota(jnp.int32, (rows, TILE), 1) < HD


def swap(t):
    return pltpu.roll(t, HD, 1)


def dup_low(t):
    return jnp.where(low_lanes(t.shape[0]), t, swap(t))


def dup_high(t):
    return jnp.where(low_lanes(t.shape[0]), swap(t), t)


def halves(t):
    high = t.astype(bf16)
    return high, (t - high.astype(f32)).astype(bf16)


def mixed(t):
    high = t.astype(bf16).astype(f32)
    return jnp.where(low_lanes(t.shape[0]), high, t - high).astype(bf16)


def high_only(t):
    return jnp.where(low_lanes(t.shape[0]), t, 0.0).astype(bf16)


def left_stack(t):
    m = mixed(t)
    return jnp.concatenate([m, m], axis=1)


def right_stack(t):
    high, low = halves(t)
    return jnp.concatenate([high, low], axis=1)


def normalize(values):
    mean = jnp.sum(values, axis=-1, keepdims=True) * (1.0 / D)
    center = values - mean
    variance = jnp.sum(center * center, axis=-1, keepdims=True) * (1.0 / D)
    inverse = lax.rsqrt(variance + norm_eps)
    return center * inverse, inverse


def normalize_back(grad_out, normed, inverse, gain):
    scaled = grad_out * gain
    first = jnp.sum(scaled, axis=-1, keepdims=True) * (1.0 / D)
    second = jnp.sum(scaled * normed, axis=-1, keepdims=True) * (1.0 / D)
    grad_in = inverse * (scaled - first - normed * second)
    gain_grad = jnp.sum(grad_out * normed, axis=0, keepdims=True)
    shift_grad = jnp.sum(grad_out, axis=0, keepdims=True)
    return grad_in, gain_grad, shift_grad


def pack_reader(gathered, rows, cols, refs, c, z):
    if gathered:
        return lambda r, k, lo, hi: refs[0][(z ^ r) * cols + (c ^ k), lo:hi, :]
    return lambda r, k, lo, hi: refs[k][r, lo:hi, :]


def project_and_attend(c, h, wkv_ref, wqo_ref, seg_ref, segcol_ref, kv_ref, qx_ref, att_ref, lse_ref):
    cols = h.shape[0]
    span = h.shape[1]
    wkv = wkv_ref[...]
    for j in range(cols):
        kv_ref[j * span:(j + 1) * span, :] = dot(h[j], wkv)
    h_own = h[0]
    qx_ref[...] = dot(h_own, wqo_ref[...])
    lane = lax.broadcasted_iota(jnp.int32, (span, TILE), 1)
    seg_row = jnp.concatenate([seg_ref[pl.ds(c ^ k, 1), :] for k in range(cols)], axis=1)
    allowed = segcol_ref[c] == seg_row
    lse_all = jnp.zeros((span, TILE), f32)
    for j in range(cols):
        tile = slice(j * TILE, (j + 1) * TILE)
        kv = kv_ref[:, tile]
        k_right = right_stack(dup_low(kv))
        v_dup = dup_high(kv)
        v_mix = mixed(v_dup)
        v_high = high_only(v_dup)
        q_left = left_stack(dup_low(qx_ref[:, tile]) * (HD ** -0.5))
        scores = jnp.where(allowed, dot1(q_left, k_right, NT), masked_score)
        top = jnp.max(scores, axis=-1, keepdims=True)
        raised = jnp.exp(scores - top)
        total = jnp.sum(raised, axis=-1, keepdims=True)
        p_high, p_low = halves(raised)
        out = dot1(p_high, v_mix) + dot1(p_low, v_high)
        out = (out + swap(out)) / total
        att_ref[:, tile] = jnp.where(low_lanes(span), 0.0, out)
        lse_all = jnp.where(lane == j, top + jnp.log(total), lse_all)
    lse_ref[...] = jnp.transpose(lse_all)[0:8, :]
    return dot(att_ref[...], wqo_ref[...], NT), h_own


def place_attention(rows, cols, block, wkv_ref, wqo_ref):
    for j in range(cols):
        for r in range(rows):
            piece = block(r, j, 0, HD)
            wkv_ref[r * HD:(r + 1) * HD, j * TILE:(j + 1) * TILE] = piece[:, :TILE]
            wqo_ref[r * HD:(r + 1) * HD, j * TILE:(j + 1) * TILE] = piece[:, TILE:]


def place_feed(rows, cols, block, at, up_ref, dn_ref):
    for j in range(cols):
        for r in range(rows):
            to = (slice(r * HD, (r + 1) * HD), slice(j * 2 * TILE, (j + 1) * 2 * TILE))
            up_ref[to] = block(r, j, at, at + HD)
            dn_ref[to] = block(r, j, at + HD, at + 2 * HD)


def feed_forward(mid, up_ref, dn_ref, before_ref, act_ref):
    before = dot(mid, up_ref[...])
    before_ref[...] = before
    activated = 0.5 * before * (1.0 + lax.erf(before * 0.7071067811865476))
    act_ref[...] = activated
    return normalize(mid + dot(activated, dn_ref[...], NT))


def attention_kernel(rows, cols, idx_ref, seg_ref, segcol_ref, *refs):
    c, z = idx_ref[0], idx_ref[1]
    packs, refs = refs[:cols], refs[cols:]
    h_out, wkv_out, wqo_out, kv_out, qx_out, att_out, lse_out, mid_out, n1_out, i1_out, params_out = refs
    block = pack_reader(False, rows, cols, packs, c, z)
    span = mid_out.shape[0]
    place_attention(rows, cols, block, wkv_out, wqo_out)
    for j in range(cols):
        h_out[j] = jnp.transpose(
            jnp.concatenate([block(r, j, HD, 2 * HD) for r in range(rows)], axis=0)
        )
    tiles = []
    for t in range(rows // 2):
        a = block(2 * t, 0, 2 * HD, 2 * HD + 8)[:, 0:TILE]
        b = block(2 * t + 1, 0, 2 * HD, 2 * HD + 8)[:, 0:TILE]
        tiles.append(jnp.where(low_lanes(8), a, swap(b)))
    params_out[...] = jnp.concatenate(tiles, axis=1)
    branch, h_own = project_and_attend(
        c, h_out, wkv_out, wqo_out, seg_ref, segcol_ref, kv_out, qx_out, att_out, lse_out
    )
    normed, inverse = normalize(h_own + branch)
    n1_out[...] = normed
    i1_out[...] = jnp.broadcast_to(inverse, (span, TILE))
    mid_out[...] = normed * params_out[0:1, :] + params_out[1:2, :]


def feed_kernel(rows, cols, mid_ref, ln_ref, *refs):
    packs, refs = refs[:cols], refs[cols:]
    h_out, up_out, dn_out, before_out, act_out, n2_out, i2_out = refs
    block = pack_reader(False, rows, cols, packs, 0, 0)
    place_feed(rows, cols, block, 0, up_out, dn_out)
    normed, inverse = feed_forward(mid_ref[...], up_out, dn_out, before_out, act_out)
    n2_out[...] = normed
    i2_out[...] = jnp.broadcast_to(inverse, i2_out.shape)
    h_out[...] = normed * ln_ref[2:3, :] + ln_ref[3:4, :]


def backward(
    c, dh, gains, seg_ref, segcol_ref, wqo_ref, kv_ref, qx_ref, att_ref, lse_ref, n1, i1, up_ref, dn_ref,
    before_ref, n2, i2, dkv_ref, dqx_ref, dbef_ref, dv1_ref, dv2_ref, norm_ref
):
    span = n1.shape[0]
    cols = segcol_ref.shape[0]
    dv2, gain2, shift2 = normalize_back(dh, n2, i2, gains[2])
    dv2_ref[...] = dv2
    d_act = dot(dv2, dn_ref[...])
    before = before_ref[...]
    slope = (
        0.5 * (1.0 + lax.erf(before * 0.7071067811865476))
        + before * jnp.exp(-0.5 * before * before) * 0.3989422804014327
    )
    dbef_ref[...] = d_act * slope
    d_mid = dv2 + dot(dbef_ref[...], up_ref[...], NT)
    dv1, gain1, shift1 = normalize_back(d_mid, n1, i1, gains[0])
    dv1_ref[...] = dv1
    norm_ref[...] = jnp.zeros_like(norm_ref)
    for k, row in enumerate((gain1, shift1, gain2, shift2)):
        norm_ref[k:k + 1, :] = row
    d_att = dot(dv1, wqo_ref[...])
    lane = lax.broadcasted_iota(jnp.int32, (span, TILE), 1)
    inner_all = jnp.zeros((span, TILE), f32)
    for j in range(cols):
        tile = slice(j * TILE, (j + 1) * TILE)
        inner = jnp.sum(d_att[:, tile] * att_ref[:, tile], axis=-1, keepdims=True)
        inner_all = jnp.where(lane == j, inner, inner_all)
    inner_rows = jnp.transpose(inner_all)
    seg_row = seg_ref[pl.ds(c, 1), :]
    low = low_lanes(span)
    for j in range(cols):
        tile = slice(j * TILE, (j + 1) * TILE)
        q_dup = dup_low(qx_ref[:, tile]) * (HD ** -0.5)
        q_mix = mixed(q_dup)
        q_left = jnp.concatenate([q_mix, q_mix], axis=1)
        q_high = high_only(q_dup)
        do_dup = dup_high(d_att[:, tile])
        do_mix = mixed(do_dup)
        do_left = jnp.concatenate([do_mix, do_mix], axis=1)
        do_high = high_only(do_dup)
        lse_row = lse_ref[j:j + 1, :]
        inner_row = inner_rows[j:j + 1, :]
        dq_t = jnp.zeros((TILE, span), f32)
        for b in range(cols):
            keys = slice(b * span, (b + 1) * span)
            kv = kv_ref[keys, tile]
            k_dup = dup_low(kv)
            v_dup = dup_high(kv)
            scores = dot1(right_stack(k_dup), q_left, NT)
            shares = jnp.where(segcol_ref[c ^ b] == seg_row, jnp.exp(scores - lse_row), 0.0)
            d_shares = dot1(right_stack(v_dup), do_left, NT)
            d_scores = shares * (d_shares - inner_row)
            p_high, p_low = halves(shares)
            s_high, s_low = halves(d_scores)
            dv = dot1(p_high, do_mix) + dot1(p_low, do_high)
            dk = dot1(s_high, q_mix) + dot1(s_low, q_high)
            dkv_ref[keys, tile] = jnp.where(low, dk + swap(dk), dv + swap(dv))
            k_t = jnp.transpose(k_dup)
            k_t_high = k_t.astype(bf16)
            upper = lax.broadcasted_iota(jnp.int32, (TILE, span), 0) < HD
            k_t_mix = jnp.where(upper, k_t_high.astype(f32), k_t - k_t_high.astype(f32)).astype(bf16)
            k_t_only = jnp.where(upper, k_t, 0.0).astype(bf16)
            dq_t = dq_t + dot1(k_t_mix, s_high) + dot1(k_t_only, s_low)
        dq = jnp.transpose(dq_t)
        dqx_ref[:, tile] = jnp.where(low, (dq + swap(dq)) * (HD ** -0.5), 0.0)


def input_gradient(wkv_ref, wqo_ref, dkv_ref, dqx_ref, dv1_ref, keep_out, send_out):
    span = dv1_ref.shape[0]
    wkv = wkv_ref[...]
    for k in (1, 3, 0, 2):
        part = dot(dkv_ref[k * span:(k + 1) * span, :], wkv, NT)
        if k == 0:
            part = part + dot(dqx_ref[...], wqo_ref[...], NT) + dv1_ref[...]
        (send_out if k % 2 else keep_out)[k // 2] = part


def weight_gradients(
    role, cols, h_ref, mid_ref, act_ref, att_ref, dkv_ref, dqx_ref, dbef_ref, dv1_ref, dv2_ref, norm_ref,
    keep_out, send_out
):
    span = dv1_ref.shape[0]

    def grad_at(k):
        return (send_out if k % 2 else keep_out).at[k // 2]

    @pl.when(role == 0)
    def _():
        mid = mid_ref[...]
        for k in range(cols):
            grad_at(k)[...] = dot(mid, dbef_ref[:, k * 2 * TILE:(k + 1) * 2 * TILE], TN)

    @pl.when(role == 1)
    def _():
        for k in range(cols):
            grad_at(k)[...] = dot(dv2_ref[...], act_ref[:, k * 2 * TILE:(k + 1) * 2 * TILE], TN)

    @pl.when(role == 2)
    def _():
        total = dot(h_ref[0], dkv_ref[0:span, :], TN)
        for b in range(1, cols):
            total += dot(h_ref[b], dkv_ref[b * span:(b + 1) * span, :], TN)
        for k in range(cols):
            grad_at(k)[:, 0:TILE] = total[:, k * TILE:(k + 1) * TILE]
            grad_at(k)[:, TILE:] = jnp.zeros((D, TILE), f32)

    @pl.when(role == 3)
    def _():
        total = dot(h_ref[0], dqx_ref[...], TN) + dot(dv1_ref[...], att_ref[...], TN)
        norms = jnp.transpose(norm_ref[...])
        for k in range(cols):
            grad_at(k)[:, 0:TILE] = total[:, k * TILE:(k + 1) * TILE]
            grad_at(k)[:, TILE:] = norms


def top_layer_kernel(rows, cols, idx_ref, ln_ref, seg_ref, segcol_ref, pack_ref, *refs):
    c, z = idx_ref[0], idx_ref[1]
    h_refs, refs = refs[:cols], refs[cols:]
    (out_ref, h_full, mid_ref, act_ref, att_ref, dkv_ref, dqx_ref, dbef_ref, dv1_ref, dv2_ref, norm_ref,
     keep_out, send_out, wkv_ref, wqo_ref, kv_ref, qx_ref, lse_ref, up_ref, dn_ref, before_ref) = refs
    block = pack_reader(True, rows, cols, (pack_ref,), c, z)
    place_attention(rows, cols, block, wkv_ref, wqo_ref)
    place_feed(rows, cols, block, HD, up_ref, dn_ref)
    for j in range(cols):
        h_full[j] = h_refs[j][...]
    gains = [ln_ref[k:k + 1, :] for k in range(4, 8)]
    branch, h_own = project_and_attend(
        c, h_full, wkv_ref, wqo_ref, seg_ref, segcol_ref, kv_ref, qx_ref, att_ref, lse_ref
    )
    n1, i1 = normalize(h_own + branch)
    mid_ref[...] = n1 * gains[0] + gains[1]
    n2, i2 = feed_forward(mid_ref[...], up_ref, dn_ref, before_ref, act_ref)
    out_ref[...] = n2 * gains[2] + gains[3]
    dh = jnp.transpose(jnp.concatenate([block(r, 0, 3 * HD, 4 * HD) for r in range(rows)], axis=0))
    backward(
        c, dh, gains, seg_ref, segcol_ref, wqo_ref, kv_ref, qx_ref, att_ref, lse_ref, n1, i1, up_ref, dn_ref,
        before_ref, n2, i2, dkv_ref, dqx_ref, dbef_ref, dv1_ref, dv2_ref, norm_ref
    )
    input_gradient(wkv_ref, wqo_ref, dkv_ref, dqx_ref, dv1_ref, keep_out, send_out)


def top_gradients_kernel(cols, idx_ref, *refs):
    weight_gradients(idx_ref[1], cols, *refs)


def low_layer_kernel(cols, idx_ref, ln_ref, seg_ref, segcol_ref, *refs):
    (dh_keep, dh_got, dh_across, h_ref, mid_ref, act_ref, wqo_ref, kv_ref, qx_ref, att_ref, lse_ref, n1_ref,
     i1_ref, up_ref, dn_ref, before_ref, n2_ref, i2_ref, keep_out, send_out, dkv_ref, dqx_ref, dv1_ref,
     dbef_ref, dv2_ref, norm_ref) = refs
    dh = dh_keep[0] + dh_got[0] + dh_across[...]
    gains = [ln_ref[k:k + 1, :] for k in range(4)]
    backward(
        idx_ref[0], dh, gains, seg_ref, segcol_ref, wqo_ref, kv_ref, qx_ref, att_ref, lse_ref, n1_ref[...],
        i1_ref[:, 0:1], up_ref, dn_ref, before_ref, n2_ref[...], i2_ref[:, 0:1], dkv_ref, dqx_ref, dbef_ref,
        dv1_ref, dv2_ref, norm_ref
    )
    weight_gradients(
        idx_ref[1], cols, h_ref, mid_ref, act_ref, att_ref, dkv_ref, dqx_ref, dbef_ref, dv1_ref, dv2_ref,
        norm_ref, keep_out, send_out
    )


def low_input_kernel(*refs):
    input_gradient(*refs)


def newton_schulz(blocks):
    sizes = [jnp.sum(x * x, keepdims=True) for x in blocks]
    blocks = [x / (jnp.sqrt(s) + frob_eps) for x, s in zip(blocks, sizes)]
    for _ in range(NS_STEPS):
        grams = [dot(x, x, NT) for x in blocks]
        squares = [dot(a, a) for a in grams]
        polys = [newton_coefs[1] * a + newton_coefs[2] * s for a, s in zip(grams, squares)]
        blocks = [newton_coefs[0] * x + dot(p, x) for p, x in zip(polys, blocks)]
    return blocks


def orthogonal_kernel(cols, idx_ref, *refs):
    role = idx_ref[1]
    out_ref = refs[-1]

    def part(k):
        return refs[k][...]

    @pl.when(role < 2)
    def _():
        (x,) = newton_schulz([jnp.concatenate([part(k) for k in range(cols)], axis=1)])
        out_ref[...] = x[:, 0:2 * TILE] * math.sqrt(FF)

    @pl.when(role >= 2)
    def _():
        low = low_lanes(D)
        tiles = [part(k)[:, 0:TILE] for k in range(cols)]
        lefts, rights = [], []
        for t in range(cols // 2):
            a, b = tiles[2 * t], tiles[2 * t + 1]
            lefts.append(jnp.where(low, a, swap(b)))
            rights.append(jnp.where(low, swap(a), b))
        left, right = newton_schulz(
            [jnp.concatenate(lefts, axis=1), jnp.concatenate(rights, axis=1)]
        )
        out_ref[:, 0:TILE] = jnp.where(low, left[:, 0:TILE], swap(right[:, 0:TILE])) * math.sqrt(D)
        out_ref[:, TILE:] = jnp.zeros((D, TILE), f32)


def call(body, operands, outs, scratch=(), flops=0, vmem=50):
    specs = [pl.BlockSpec(memory_space=pltpu.SMEM if x.ndim == 1 else pltpu.VMEM) for x in operands]
    moved = sum(4 * math.prod(x.shape) for x in operands) + sum(4 * math.prod(s) for s in outs)
    return pl.pallas_call(
        body,
        out_shape=[jax.ShapeDtypeStruct(s, f32) for s in outs],
        in_specs=specs,
        out_specs=[pl.BlockSpec(memory_space=pltpu.VMEM) for _ in outs],
        scratch_shapes=[pltpu.VMEM(s, f32) for s in scratch],
        compiler_params=pltpu.CompilerParams(vmem_limit_bytes=vmem * 2**20),
        cost_estimate=pl.CostEstimate(flops=flops, bytes_accessed=moved, transcendentals=0),
    )(*operands)


def on_device(
    layer_input,
    segment_ids,
    head_projection_weights,
    output_projection_weights,
    up_projection_weights,
    down_projection_weights,
    head_moment,
    out_moment,
    up_moment,
    down_moment,
    norm_params,
    norm_first,
    norm_second,
    output_grad,
):
    row = lax.axis_index("row").astype(jnp.int32)
    col = lax.axis_index("col").astype(jnp.int32)
    rows = lax.axis_size("row")
    cols = lax.axis_size("col")
    dps = lax.axis_size("dp")
    span = layer_input.shape[1]
    length = span * cols
    idx = jnp.stack([col, row])
    swap2 = lambda x: jnp.swapaxes(x, -1, -2)

    def perm(x, axis, bit):
        return lax.ppermute(x, axis, [(i, i ^ bit) for i in range(lax.axis_size(axis))])

    def spread_cols(x):
        across = perm(x, "col", 2)
        return [x, perm(x, "col", 1), across, perm(across, "col", 1)]

    def spread_rows(parts):
        return jnp.stack([parts[0]] + [perm(parts[k], "row", k) for k in range(1, rows)])

    def attention_pack(heads, outs):
        return jnp.concatenate([heads[1], heads[2], heads[0], swap2(outs)], axis=1)

    params = jnp.pad(norm_params.reshape(8, HD), ((0, 0), (0, 2 * TILE - HD)))
    shard_a = jnp.concatenate(
        [
            attention_pack(head_projection_weights[0], output_projection_weights[0]),
            swap2(layer_input[0]),
            params,
        ]
    )
    shard_f = jnp.concatenate([up_projection_weights[0], swap2(down_projection_weights[0])])
    shard_b = jnp.concatenate(
        [
            attention_pack(head_projection_weights[1], output_projection_weights[1]),
            up_projection_weights[1],
            swap2(down_projection_weights[1]),
            swap2(output_grad[0]),
        ]
    )
    rows_a = spread_rows([shard_a] * rows)
    rows_f = spread_rows([shard_f] * rows)
    packs_a = spread_cols(rows_a)
    packs_f = spread_cols(rows_f)
    shard_b, _ = lax.optimization_barrier((shard_b, rows_a))
    pack_b = lax.all_gather(shard_b, ("row", "col"), axis=0)
    seg_rows = segment_ids.reshape(cols, span)
    seg_col = segment_ids.reshape(cols, span, 1)

    order = row ^ jnp.arange(rows, dtype=jnp.int32)
    moments = []
    for l in range(LAYERS):
        blank = jnp.zeros((HD, TILE), f32)
        heads = head_moment[l]
        moments.append(
            jnp.stack(
                [
                    up_moment[l],
                    swap2(down_moment[l]),
                    jnp.concatenate([heads[1], heads[2], blank], axis=1),
                    jnp.concatenate([heads[0], swap2(out_moment[l]), blank], axis=1),
                ]
            )
        )
    moments = jnp.take(jnp.stack(moments, axis=1), order, axis=0)
    moments = spread_rows([moments[k] for k in range(rows)]) * muon_decay

    full = (cols, span, D)
    pair = (2, span, D)
    own = (span, D)
    wide = (span, FF)
    half = (D, cols * TILE)
    keys = (length, cols * TILE)
    queries = (span, cols * TILE)
    one = (span, TILE)
    stats = (8, span)
    norms = (TILE, D)
    segs = [seg_rows, seg_col]

    h_full, wkv, wqo, kv, qx, att, lse, mid, n1, i1, ln = call(
        functools.partial(attention_kernel, rows, cols),
        [idx] + segs + packs_a,
        [full, half, half, keys, queries, queries, stats, own, own, one, (8, D)], flops=5 * 10**9, vmem=32,
    )
    mid, moments = lax.optimization_barrier((mid, moments))
    h_own, up, dn, before, act, n2, i2 = call(
        functools.partial(feed_kernel, rows, cols),
        [mid, ln] + packs_f,
        [own, (D, FF), (D, FF), wide, wide, own, one], flops=2 * 10**9, vmem=24,
    )
    hidden = spread_cols(h_own)
    top, *saved, keep, send = call(
        functools.partial(top_layer_kernel, rows, cols),
        [idx, ln] + segs + [pack_b] + hidden,
        [own, full, own, wide, queries, keys, queries, wide, own, own, norms, pair, pair],
        [half, half, keys, queries, stats, (D, FF), (D, FF), wide], flops=20 * 10**9, vmem=44,
    )
    layer_output = top[:, :HD][None]

    def fold_core(keep, send):
        got = perm(send, "col", 1)
        return got, perm(keep[1] + got[1], "col", 2)

    def momentum(keep, send, moment):
        got, across = fold_core(keep, send)
        mine = keep[0] + got[0] + across
        mine = mine + perm(mine, "dp", 1) if dps == 2 else lax.psum(mine, "dp")
        return mine + moment

    def direction(mine):
        (step,) = call(
            functools.partial(orthogonal_kernel, cols), [idx] + spread_cols(mine), [own], flops=4 * 10**9, vmem=24,
        )
        blocks = jnp.concatenate([mine.reshape(rows, HD, D), step.reshape(rows, HD, D)], axis=1)
        return jnp.take(spread_rows(list(blocks)), order, axis=0)

    got, across = fold_core(keep, send)
    grads_top = call(
        functools.partial(top_gradients_kernel, cols), [idx] + saved, [pair, pair], flops=2 * 10**9, vmem=24,
    )
    keep_g, send_g, dkv, dqx, dv1 = call(
        functools.partial(low_layer_kernel, cols),
        [idx, ln] + segs + [keep, got, across, h_full, mid, act, wqo, kv, qx, att, lse, n1, i1, up, dn, before, n2, i2],
        [pair, pair, keys, queries, own], [wide, own, norms], flops=12 * 10**9, vmem=44,
    )
    mine_top = momentum(*grads_top, moments[:, 1].reshape(D, D))
    mine_low = momentum(keep_g, send_g, moments[:, 0].reshape(D, D))
    keep, send = call(
        low_input_kernel, [wkv, wqo, dkv, dqx, dv1], [pair, pair], flops=2 * 10**9, vmem=24,
    )
    got, across = fold_core(keep, send)
    input_grad = (keep[0] + got[0] + across)[:, :HD][None]
    reduced = [direction(mine_low), direction(mine_top)]

    head_new, out_new, up_new, down_new = [], [], [], []
    head_mom, out_mom, up_mom, down_mom, norm_sum = [], [], [], [], []
    for l in range(LAYERS):
        mom, step = reduced[l][:, :HD], reduced[l][:, HD:] * muon_rate
        parts = lambda x: (jnp.stack([x[3, :, :HD], x[2, :, :HD], x[2, :, HD:TILE]]), swap2(x[3, :, HD:TILE]))
        heads, outs = parts(mom)
        head_mom.append(heads)
        out_mom.append(outs)
        up_mom.append(mom[0])
        down_mom.append(swap2(mom[1]))
        norm_sum.append(swap2(mom[3, :, TILE:TILE + 4]))
        heads, outs = parts(step)
        head_new.append(head_projection_weights[l] - D ** -0.5 * heads)
        out_new.append(output_projection_weights[l] - (D // 16) ** -0.5 * outs)
        up_new.append(up_projection_weights[l] - D ** -0.5 * step[0])
        down_new.append(down_projection_weights[l] - FF ** -0.5 * swap2(step[1]))
    norm_sum = jnp.stack(norm_sum)
    first_moment = adam_first * norm_first + (1.0 - adam_first) * norm_sum
    second_moment = adam_second * norm_second + (1.0 - adam_second) * norm_sum * norm_sum
    corrected_first = first_moment / (1.0 - adam_first**STEP)
    corrected_second = second_moment / (1.0 - adam_second**STEP)
    norm_updated = norm_params - adam_rate * corrected_first / (
        jnp.sqrt(corrected_second) + adam_eps
    )
    return (
        layer_output,
        input_grad,
        jnp.stack(head_new),
        jnp.stack(out_new),
        jnp.stack(up_new),
        jnp.stack(down_new),
        jnp.stack(head_mom),
        jnp.stack(out_mom),
        jnp.stack(up_mom),
        jnp.stack(down_mom),
        first_moment,
        second_moment,
        norm_updated,
    )


def solution(mesh):
    placed = (
        P("dp", "col", "row"),
        P("dp", None),
        P(None, None, "row", "col"),
        P(None, "col", "row"),
        P(None, "row", "col"),
        P(None, "col", "row"),
        P(None, None, "row", "col"),
        P(None, "col", "row"),
        P(None, "row", "col"),
        P(None, "col", "row"),
        P(None, None, "row"),
        P(None, None, "row"),
        P(None, None, "row"),
        P("dp", "col", "row"),
    )
    return jax.shard_map(
        on_device,
        mesh=mesh,
        in_specs=placed,
        out_specs=(
            P("dp", "col", "row"),
            P("dp", "col", "row"),
            P(None, None, "row", "col"),
            P(None, "col", "row"),
            P(None, "row", "col"),
            P(None, "col", "row"),
            P(None, None, "row", "col"),
            P(None, "col", "row"),
            P(None, "row", "col"),
            P(None, "col", "row"),
            P(None, None, "row"),
            P(None, None, "row"),
            P(None, None, "row"),
        ),
        check_vma=False,
    )
```

```python
import functools
import math

import jax
import jax.numpy as jnp
from jax import lax
from jax.experimental import pallas as pl
from jax.experimental.pallas import tpu as pltpu
from jax.sharding import PartitionSpec as P

D = 256
FF = 1024
LAYERS = 2
NS_STEPS = 5
STEP = 10
HD = 64
TILE = 128

norm_eps = 1e-05
newton_coefs = (3.4445, -4.775, 2.0315)
frob_eps = 1e-07
muon_decay = 0.95
muon_rate = 0.5
adam_first = 0.9
adam_second = 0.999
adam_eps = 1e-08
adam_rate = 0.2
masked_score = -1e30

f32 = jnp.float32
bf16 = jnp.bfloat16

NN = (((1,), (0,)), ((), ()))
NT = (((1,), (1,)), ((), ()))
TN = (((0,), (0,)), ((), ()))


def dot(a, b, dims=NN):
    return lax.dot_general(a, b, dims, precision=lax.Precision.HIGH, preferred_element_type=f32)


def dot1(a, b, dims=NN):
    return lax.dot_general(a, b, dims, preferred_element_type=f32)


def low_lanes(rows):
    return lax.broadcasted_iota(jnp.int32, (rows, TILE), 1) < HD


def swap(t):
    return pltpu.roll(t, HD, 1)


def dup_low(t):
    return jnp.where(low_lanes(t.shape[0]), t, swap(t))


def dup_high(t):
    return jnp.where(low_lanes(t.shape[0]), swap(t), t)


def halves(t):
    high = t.astype(bf16)
    return high, (t - high.astype(f32)).astype(bf16)


def mixed(t):
    high = t.astype(bf16).astype(f32)
    return jnp.where(low_lanes(t.shape[0]), high, t - high).astype(bf16)


def high_only(t):
    return jnp.where(low_lanes(t.shape[0]), t, 0.0).astype(bf16)


def left_stack(t):
    m = mixed(t)
    return jnp.concatenate([m, m], axis=1)


def right_stack(t):
    high, low = halves(t)
    return jnp.concatenate([high, low], axis=1)


def normalize(values):
    mean = jnp.sum(values, axis=-1, keepdims=True) * (1.0 / D)
    center = values - mean
    variance = jnp.sum(center * center, axis=-1, keepdims=True) * (1.0 / D)
    inverse = lax.rsqrt(variance + norm_eps)
    return center * inverse, inverse


def normalize_back(grad_out, normed, inverse, gain):
    scaled = grad_out * gain
    first = jnp.sum(scaled, axis=-1, keepdims=True) * (1.0 / D)
    second = jnp.sum(scaled * normed, axis=-1, keepdims=True) * (1.0 / D)
    grad_in = inverse * (scaled - first - normed * second)
    gain_grad = jnp.sum(grad_out * normed, axis=0, keepdims=True)
    shift_grad = jnp.sum(grad_out, axis=0, keepdims=True)
    return grad_in, gain_grad, shift_grad


def pack_reader(gathered, rows, cols, refs, c, z):
    if gathered:
        return lambda r, k, lo, hi: refs[0][(z ^ r) * cols + (c ^ k), lo:hi, :]
    return lambda r, k, lo, hi: refs[k][r, lo:hi, :]


def project_and_attend(c, h, wkv_ref, wqo_ref, seg_ref, segcol_ref, kv_ref, qx_ref, att_ref, lse_ref):
    cols = h.shape[0]
    span = h.shape[1]
    wkv = wkv_ref[...]
    for j in range(cols):
        kv_ref[j * span:(j + 1) * span, :] = dot(h[j], wkv)
    h_own = h[0]
    qx_ref[...] = dot(h_own, wqo_ref[...])
    lane = lax.broadcasted_iota(jnp.int32, (span, TILE), 1)
    seg_row = jnp.concatenate([seg_ref[pl.ds(c ^ k, 1), :] for k in range(cols)], axis=1)
    allowed = segcol_ref[c] == seg_row
    lse_all = jnp.zeros((span, TILE), f32)
    for j in range(cols):
        tile = slice(j * TILE, (j + 1) * TILE)
        kv = kv_ref[:, tile]
        k_right = right_stack(dup_low(kv))
        v_dup = dup_high(kv)
        v_mix = mixed(v_dup)
        v_high = high_only(v_dup)
        q_left = left_stack(dup_low(qx_ref[:, tile]) * (HD ** -0.5))
        scores = jnp.where(allowed, dot1(q_left, k_right, NT), masked_score)
        top = jnp.max(scores, axis=-1, keepdims=True)
        raised = jnp.exp(scores - top)
        total = jnp.sum(raised, axis=-1, keepdims=True)
        p_high, p_low = halves(raised)
        out = dot1(p_high, v_mix) + dot1(p_low, v_high)
        out = (out + swap(out)) / total
        att_ref[:, tile] = jnp.where(low_lanes(span), 0.0, out)
        lse_all = jnp.where(lane == j, top + jnp.log(total), lse_all)
    lse_ref[...] = jnp.transpose(lse_all)[0:8, :]
    return dot(att_ref[...], wqo_ref[...], NT), h_own


def place_attention(rows, cols, block, wkv_ref, wqo_ref):
    for j in range(cols):
        for r in range(rows):
            piece = block(r, j, 0, HD)
            wkv_ref[r * HD:(r + 1) * HD, j * TILE:(j + 1) * TILE] = piece[:, :TILE]
            wqo_ref[r * HD:(r + 1) * HD, j * TILE:(j + 1) * TILE] = piece[:, TILE:]


def place_feed(rows, cols, block, at, up_ref, dn_ref):
    for j in range(cols):
        for r in range(rows):
            to = (slice(r * HD, (r + 1) * HD), slice(j * 2 * TILE, (j + 1) * 2 * TILE))
            up_ref[to] = block(r, j, at, at + HD)
            dn_ref[to] = block(r, j, at + HD, at + 2 * HD)


def feed_forward(mid, up_ref, dn_ref, before_ref, act_ref):
    before = dot(mid, up_ref[...])
    before_ref[...] = before
    activated = 0.5 * before * (1.0 + lax.erf(before * 0.7071067811865476))
    act_ref[...] = activated
    return normalize(mid + dot(activated, dn_ref[...], NT))


def attention_kernel(rows, cols, idx_ref, seg_ref, segcol_ref, *refs):
    c, z = idx_ref[0], idx_ref[1]
    packs, refs = refs[:cols], refs[cols:]
    h_out, wkv_out, wqo_out, kv_out, qx_out, att_out, lse_out, mid_out, n1_out, i1_out, params_out = refs
    block = pack_reader(False, rows, cols, packs, c, z)
    span = mid_out.shape[0]
    place_attention(rows, cols, block, wkv_out, wqo_out)
    for j in range(cols):
        h_out[j] = jnp.transpose(
            jnp.concatenate([block(r, j, HD, 2 * HD) for r in range(rows)], axis=0)
        )
    tiles = []
    for t in range(rows // 2):
        a = block(2 * t, 0, 2 * HD, 2 * HD + 8)[:, 0:TILE]
        b = block(2 * t + 1, 0, 2 * HD, 2 * HD + 8)[:, 0:TILE]
        tiles.append(jnp.where(low_lanes(8), a, swap(b)))
    params_out[...] = jnp.concatenate(tiles, axis=1)
    branch, h_own = project_and_attend(
        c, h_out, wkv_out, wqo_out, seg_ref, segcol_ref, kv_out, qx_out, att_out, lse_out
    )
    normed, inverse = normalize(h_own + branch)
    n1_out[...] = normed
    i1_out[...] = jnp.broadcast_to(inverse, (span, TILE))
    mid_out[...] = normed * params_out[0:1, :] + params_out[1:2, :]


def feed_kernel(rows, cols, mid_ref, ln_ref, *refs):
    packs, refs = refs[:cols], refs[cols:]
    h_out, up_out, dn_out, before_out, act_out, n2_out, i2_out = refs
    block = pack_reader(False, rows, cols, packs, 0, 0)
    place_feed(rows, cols, block, 0, up_out, dn_out)
    normed, inverse = feed_forward(mid_ref[...], up_out, dn_out, before_out, act_out)
    n2_out[...] = normed
    i2_out[...] = jnp.broadcast_to(inverse, i2_out.shape)
    h_out[...] = normed * ln_ref[2:3, :] + ln_ref[3:4, :]


def backward(
    c, dh, gains, seg_ref, segcol_ref, wqo_ref, kv_ref, qx_ref, att_ref, lse_ref, n1, i1, up_ref, dn_ref,
    before_ref, n2, i2, dkv_ref, dqx_ref, dbef_ref, dv1_ref, dv2_ref, norm_ref
):
    span = n1.shape[0]
    cols = segcol_ref.shape[0]
    dv2, gain2, shift2 = normalize_back(dh, n2, i2, gains[2])
    dv2_ref[...] = dv2
    d_act = dot(dv2, dn_ref[...])
    before = before_ref[...]
    slope = (
        0.5 * (1.0 + lax.erf(before * 0.7071067811865476))
        + before * jnp.exp(-0.5 * before * before) * 0.3989422804014327
    )
    dbef_ref[...] = d_act * slope
    d_mid = dv2 + dot(dbef_ref[...], up_ref[...], NT)
    dv1, gain1, shift1 = normalize_back(d_mid, n1, i1, gains[0])
    dv1_ref[...] = dv1
    norm_ref[...] = jnp.zeros_like(norm_ref)
    for k, row in enumerate((gain1, shift1, gain2, shift2)):
        norm_ref[k:k + 1, :] = row
    d_att = dot(dv1, wqo_ref[...])
    lane = lax.broadcasted_iota(jnp.int32, (span, TILE), 1)
    inner_all = jnp.zeros((span, TILE), f32)
    for j in range(cols):
        tile = slice(j * TILE, (j + 1) * TILE)
        inner = jnp.sum(d_att[:, tile] * att_ref[:, tile], axis=-1, keepdims=True)
        inner_all = jnp.where(lane == j, inner, inner_all)
    inner_rows = jnp.transpose(inner_all)
    seg_row = seg_ref[pl.ds(c, 1), :]
    low = low_lanes(span)
    for j in range(cols):
        tile = slice(j * TILE, (j + 1) * TILE)
        q_dup = dup_low(qx_ref[:, tile]) * (HD ** -0.5)
        q_mix = mixed(q_dup)
        q_left = jnp.concatenate([q_mix, q_mix], axis=1)
        q_high = high_only(q_dup)
        do_dup = dup_high(d_att[:, tile])
        do_mix = mixed(do_dup)
        do_left = jnp.concatenate([do_mix, do_mix], axis=1)
        do_high = high_only(do_dup)
        lse_row = lse_ref[j:j + 1, :]
        inner_row = inner_rows[j:j + 1, :]
        dq_t = jnp.zeros((TILE, span), f32)
        for b in range(cols):
            keys = slice(b * span, (b + 1) * span)
            kv = kv_ref[keys, tile]
            k_dup = dup_low(kv)
            v_dup = dup_high(kv)
            scores = dot1(right_stack(k_dup), q_left, NT)
            shares = jnp.where(segcol_ref[c ^ b] == seg_row, jnp.exp(scores - lse_row), 0.0)
            d_shares = dot1(right_stack(v_dup), do_left, NT)
            d_scores = shares * (d_shares - inner_row)
            p_high, p_low = halves(shares)
            s_high, s_low = halves(d_scores)
            dv = dot1(p_high, do_mix) + dot1(p_low, do_high)
            dk = dot1(s_high, q_mix) + dot1(s_low, q_high)
            dkv_ref[keys, tile] = jnp.where(low, dk + swap(dk), dv + swap(dv))
            k_t = jnp.transpose(k_dup)
            k_t_high = k_t.astype(bf16)
            upper = lax.broadcasted_iota(jnp.int32, (TILE, span), 0) < HD
            k_t_mix = jnp.where(upper, k_t_high.astype(f32), k_t - k_t_high.astype(f32)).astype(bf16)
            k_t_only = jnp.where(upper, k_t, 0.0).astype(bf16)
            dq_t = dq_t + dot1(k_t_mix, s_high) + dot1(k_t_only, s_low)
        dq = jnp.transpose(dq_t)
        dqx_ref[:, tile] = jnp.where(low, (dq + swap(dq)) * (HD ** -0.5), 0.0)


def input_gradient(wkv_ref, wqo_ref, dkv_ref, dqx_ref, dv1_ref, keep_out, send_out):
    span = dv1_ref.shape[0]
    wkv = wkv_ref[...]
    for k in (1, 3, 0, 2):
        part = dot(dkv_ref[k * span:(k + 1) * span, :], wkv, NT)
        if k == 0:
            part = part + dot(dqx_ref[...], wqo_ref[...], NT) + dv1_ref[...]
        (send_out if k % 2 else keep_out)[k // 2] = part


def weight_gradients(
    role, cols, h_ref, mid_ref, act_ref, att_ref, dkv_ref, dqx_ref, dbef_ref, dv1_ref, dv2_ref, norm_ref, grad_at
):
    span = dv1_ref.shape[0]

    @pl.when(role == 0)
    def _():
        mid = mid_ref[...]
        for k in range(cols):
            grad_at(k)[...] = dot(mid, dbef_ref[:, k * 2 * TILE:(k + 1) * 2 * TILE], TN)

    @pl.when(role == 1)
    def _():
        for k in range(cols):
            grad_at(k)[...] = dot(dv2_ref[...], act_ref[:, k * 2 * TILE:(k + 1) * 2 * TILE], TN)

    @pl.when(role == 2)
    def _():
        total = dot(h_ref[0], dkv_ref[0:span, :], TN)
        for b in range(1, cols):
            total += dot(h_ref[b], dkv_ref[b * span:(b + 1) * span, :], TN)
        for k in range(cols):
            grad_at(k)[:, 0:TILE] = total[:, k * TILE:(k + 1) * TILE]
            grad_at(k)[:, TILE:] = jnp.zeros((D, TILE), f32)

    @pl.when(role == 3)
    def _():
        total = dot(h_ref[0], dqx_ref[...], TN) + dot(dv1_ref[...], att_ref[...], TN)
        norms = jnp.transpose(norm_ref[...])
        for k in range(cols):
            grad_at(k)[:, 0:TILE] = total[:, k * TILE:(k + 1) * TILE]
            grad_at(k)[:, TILE:] = norms


def top_layer_kernel(rows, cols, idx_ref, ln_ref, seg_ref, segcol_ref, pack_ref, *refs):
    c, z = idx_ref[0], idx_ref[1]
    late_refs, h_refs, refs = refs[:rows], refs[rows:rows + cols], refs[rows + cols:]
    (out_ref, h_full, mid_ref, act_ref, att_ref, dkv_ref, dqx_ref, dbef_ref, dv1_ref, dv2_ref, norm_ref,
     keep_out, send_out, wkv_ref, wqo_ref, kv_ref, qx_ref, lse_ref, up_ref, dn_ref, before_ref) = refs
    block = pack_reader(True, rows, cols, (pack_ref,), c, z)
    place_attention(rows, cols, block, wkv_ref, wqo_ref)
    place_feed(rows, cols, block, HD, up_ref, dn_ref)
    for j in range(cols):
        h_full[j] = h_refs[j][...]
    gains = [ln_ref[k:k + 1, :] for k in range(4, 8)]
    branch, h_own = project_and_attend(
        c, h_full, wkv_ref, wqo_ref, seg_ref, segcol_ref, kv_ref, qx_ref, att_ref, lse_ref
    )
    n1, i1 = normalize(h_own + branch)
    mid_ref[...] = n1 * gains[0] + gains[1]
    n2, i2 = feed_forward(mid_ref[...], up_ref, dn_ref, before_ref, act_ref)
    out_ref[...] = n2 * gains[2] + gains[3]
    dh = jnp.transpose(jnp.concatenate([ref[2 * HD:, :] for ref in late_refs], axis=0))
    backward(
        c, dh, gains, seg_ref, segcol_ref, wqo_ref, kv_ref, qx_ref, att_ref, lse_ref, n1, i1, up_ref, dn_ref,
        before_ref, n2, i2, dkv_ref, dqx_ref, dbef_ref, dv1_ref, dv2_ref, norm_ref
    )
    input_gradient(wkv_ref, wqo_ref, dkv_ref, dqx_ref, dv1_ref, keep_out, send_out)


def add_moment(idx_ref, late_refs, big, at):
    first = 0 if big else HD

    @pl.when(idx_ref[2] == 0)
    def _():
        for r, ref in enumerate(late_refs):
            at[r * HD:(r + 1) * HD, :] += ref[first:first + HD, :]


def top_gradients_kernel(rows, cols, idx_ref, *refs):
    z = idx_ref[1]
    late_refs, refs = refs[:rows], refs[rows:]
    keep_out, send_out = refs[-2:]
    weight_gradients(z, cols, *refs[:-2], lambda k: (send_out if k % 2 else keep_out).at[k // 2])
    for big in (True, False):

        @pl.when((z < 2) == big)
        def _():
            add_moment(idx_ref, late_refs, big, keep_out.at[0])


def low_layer_kernel(rows, cols, idx_ref, ln_ref, seg_ref, segcol_ref, *refs):
    late_refs, refs = refs[:rows], refs[rows:]
    z = idx_ref[1]
    (dh_keep, dh_got, dh_across, h_ref, mid_ref, act_ref, wqo_ref, kv_ref, qx_ref, att_ref, lse_ref, n1_ref,
     i1_ref, up_ref, dn_ref, before_ref, n2_ref, i2_ref, keep_out, send_out, dkv_ref, dqx_ref, dv1_ref,
     dbef_ref, dv2_ref, norm_ref) = refs
    dh = dh_keep[0] + dh_got[0] + dh_across[...]
    gains = [ln_ref[k:k + 1, :] for k in range(4)]
    backward(
        idx_ref[0], dh, gains, seg_ref, segcol_ref, wqo_ref, kv_ref, qx_ref, att_ref, lse_ref, n1_ref[...],
        i1_ref[:, 0:1], up_ref, dn_ref, before_ref, n2_ref[...], i2_ref[:, 0:1], dkv_ref, dqx_ref, dbef_ref,
        dv1_ref, dv2_ref, norm_ref
    )
    weight_gradients(
        z ^ 2, cols, h_ref, mid_ref, act_ref, att_ref, dkv_ref, dqx_ref, dbef_ref, dv1_ref, dv2_ref, norm_ref,
        lambda k: (send_out if k % 2 else keep_out).at[k // 2]
    )
    for big in (True, False):

        @pl.when((z >= 2) == big)
        def _():
            add_moment(idx_ref, late_refs, big, keep_out.at[0])


def low_input_kernel(*refs):
    input_gradient(*refs)


def newton_schulz(blocks):
    sizes = [jnp.sum(x * x, keepdims=True) for x in blocks]
    blocks = [x / (jnp.sqrt(s) + frob_eps) for x, s in zip(blocks, sizes)]
    for _ in range(NS_STEPS):
        grams = [dot(x, x, NT) for x in blocks]
        squares = [dot(a, a) for a in grams]
        polys = [newton_coefs[1] * a + newton_coefs[2] * s for a, s in zip(grams, squares)]
        blocks = [newton_coefs[0] * x + dot(p, x) for p, x in zip(polys, blocks)]
    return blocks


def orthogonal_kernel(cols, idx_ref, *refs):
    z = idx_ref[1]
    top_refs, low_refs = refs[:cols], refs[cols:2 * cols]
    big_out, small_out, big, small = refs[2 * cols:]

    @pl.when(z < 2)
    def _():
        for k in range(cols):
            big[:, k * 2 * TILE:(k + 1) * 2 * TILE] = top_refs[k][...]
            small[:, k * TILE:(k + 1) * TILE] = low_refs[k][:, 0:TILE]

    @pl.when(z >= 2)
    def _():
        for k in range(cols):
            big[:, k * 2 * TILE:(k + 1) * 2 * TILE] = low_refs[k][...]
            small[:, k * TILE:(k + 1) * TILE] = top_refs[k][:, 0:TILE]

    low = low_lanes(D)
    lefts, rights = [], []
    for t in range(cols // 2):
        a = small[:, 2 * t * TILE:(2 * t + 1) * TILE]
        b = small[:, (2 * t + 1) * TILE:(2 * t + 2) * TILE]
        lefts.append(jnp.where(low, a, swap(b)))
        rights.append(jnp.where(low, swap(a), b))
    wide, left, right = newton_schulz(
        [big[...], jnp.concatenate(lefts, axis=1), jnp.concatenate(rights, axis=1)]
    )
    big_out[...] = wide[:, 0:2 * TILE] * math.sqrt(FF)
    small_out[...] = jnp.where(low, left[:, 0:TILE], swap(right[:, 0:TILE])) * math.sqrt(D)


def first_pack_kernel(heads_ref, outs_ref, x_ref, params_ref, shard_out):
    shard_out[0:HD, 0:HD] = heads_ref[0, 1]
    shard_out[0:HD, HD:TILE] = heads_ref[0, 2]
    shard_out[0:HD, TILE:TILE + HD] = heads_ref[0, 0]
    shard_out[0:HD, TILE + HD:] = jnp.transpose(outs_ref[0])
    shard_out[HD:2 * HD, :] = x_ref[...]
    shard_out[2 * HD:, :] = jnp.zeros((8, 2 * TILE), f32)
    shard_out[2 * HD:, 0:HD] = params_ref[...]


def pack_kernel(
    rows, idx_ref, heads_ref, outs_ref, up_ref, dn_ref, og_ref, mh_ref, mo_ref, mu_ref, md_ref, f_out, b_out, *refs
):
    z = idx_ref[1]
    late_outs, moments = refs[:rows], refs[rows]
    f_out[0:HD, :] = up_ref[0]
    f_out[HD:, :] = dn_ref[0]
    b_out[0:HD, 0:HD] = heads_ref[1, 1]
    b_out[0:HD, HD:TILE] = heads_ref[1, 2]
    b_out[0:HD, TILE:TILE + HD] = heads_ref[1, 0]
    b_out[0:HD, TILE + HD:] = jnp.transpose(outs_ref[1])
    b_out[HD:2 * HD, :] = up_ref[1]
    b_out[2 * HD:, :] = dn_ref[1]
    for l in range(LAYERS):
        large, small = (0, 2) if l else (2, 0)
        moments[large, 0:HD, :] = mu_ref[l] * muon_decay
        moments[large + 1, 0:HD, :] = md_ref[l] * muon_decay
        moments[small, HD:, 0:HD] = mh_ref[l, 1] * muon_decay
        moments[small, HD:, HD:TILE] = mh_ref[l, 2] * muon_decay
        moments[small + 1, HD:, 0:HD] = mh_ref[l, 0] * muon_decay
        moments[small + 1, HD:, HD:TILE] = jnp.transpose(mo_ref[l]) * muon_decay
    for r in range(rows):
        moments[r, HD:, TILE:] = jnp.zeros((HD, TILE), f32)
    for k in range(rows):
        late_outs[k][0:2 * HD, :] = moments[z ^ k]
        late_outs[k][2 * HD:, :] = og_ref[...]


def update_kernel(
    rows, idx_ref, heads_ref, outs_ref, up_ref, dn_ref, params_ref, first_ref, second_ref, *refs
):
    z = idx_ref[1]
    mom_refs, step_refs, refs = refs[:rows], refs[rows:2 * rows], refs[2 * rows:]
    (heads_out, outs_out, up_out, dn_out, mh_out, mo_out, mu_out, md_out, first_out, second_out, params_out,
     mom, step) = refs
    for k in range(rows):
        mom[z ^ k] = mom_refs[k][...]
        step[z ^ k] = step_refs[k][...] * muon_rate
    for l in range(LAYERS):
        large, small = (0, 2) if l else (2, 0)
        mu_out[l] = mom[large, 0:HD, :]
        md_out[l] = mom[large + 1, 0:HD, :]
        up_out[l] = up_ref[l] - D ** -0.5 * step[large, :, 0:2 * TILE]
        dn_out[l] = dn_ref[l] - FF ** -0.5 * step[large + 1, :, 0:2 * TILE]
        kv, qo = mom[small, HD:, 0:TILE], mom[small + 1, HD:, 0:TILE]
        mh_out[l, 0] = qo[:, 0:HD]
        mh_out[l, 1] = kv[:, 0:HD]
        mh_out[l, 2] = swap(kv)[:, 0:HD]
        mo_out[l] = jnp.transpose(swap(qo))[0:HD, :]
        kv, qo = step[small, :, 2 * TILE:], step[small + 1, :, 2 * TILE:]
        heads_out[l, 0] = heads_ref[l, 0] - D ** -0.5 * qo[:, 0:HD]
        heads_out[l, 1] = heads_ref[l, 1] - D ** -0.5 * kv[:, 0:HD]
        heads_out[l, 2] = heads_ref[l, 2] - D ** -0.5 * swap(kv)[:, 0:HD]
        outs_out[l] = outs_ref[l] - (D // 16) ** -0.5 * jnp.transpose(swap(qo))[0:HD, :]
        grad = jnp.transpose(mom[small + 1, HD:, TILE:])[0:4, :]
        first = adam_first * first_ref[l] + (1.0 - adam_first) * grad
        second = adam_second * second_ref[l] + (1.0 - adam_second) * grad * grad
        first_out[l] = first
        second_out[l] = second
        params_out[l] = params_ref[l] - adam_rate * (first / (1.0 - adam_first**STEP)) / (
            jnp.sqrt(second / (1.0 - adam_second**STEP)) + adam_eps
        )


def call(body, operands, outs, scratch=(), flops=0, vmem=50):
    specs = [pl.BlockSpec(memory_space=pltpu.SMEM if x.ndim == 1 else pltpu.VMEM) for x in operands]
    moved = sum(4 * math.prod(x.shape) for x in operands) + sum(4 * math.prod(s) for s in outs)
    return pl.pallas_call(
        body,
        out_shape=[jax.ShapeDtypeStruct(s, f32) for s in outs],
        in_specs=specs,
        out_specs=[pl.BlockSpec(memory_space=pltpu.VMEM) for _ in outs],
        scratch_shapes=[pltpu.VMEM(s, f32) for s in scratch],
        compiler_params=pltpu.CompilerParams(vmem_limit_bytes=vmem * 2**20),
        cost_estimate=pl.CostEstimate(flops=flops, bytes_accessed=moved, transcendentals=0),
    )(*operands)


def on_device(
    layer_input,
    segment_ids,
    head_projection_weights,
    output_projection_weights,
    up_projection_weights,
    down_projection_weights,
    head_moment,
    out_moment,
    up_moment,
    down_moment,
    norm_params,
    norm_first,
    norm_second,
    output_grad,
):
    row = lax.axis_index("row").astype(jnp.int32)
    col = lax.axis_index("col").astype(jnp.int32)
    rows = lax.axis_size("row")
    cols = lax.axis_size("col")
    dps = lax.axis_size("dp")
    span = layer_input.shape[1]
    length = span * cols
    idx = jnp.stack([col, row, lax.axis_index("dp").astype(jnp.int32)])
    swap2 = lambda x: jnp.swapaxes(x, -1, -2)

    def perm(x, axis, bit):
        return lax.ppermute(x, axis, [(i, i ^ bit) for i in range(lax.axis_size(axis))])

    def spread_cols(x):
        across = perm(x, "col", 2)
        return [x, perm(x, "col", 1), across, perm(across, "col", 1)]

    def spread_rows(parts):
        return [parts[0]] + [perm(parts[k], "row", k) for k in range(1, rows)]

    heads, outs, ups = head_projection_weights, output_projection_weights, up_projection_weights
    downs = swap2(down_projection_weights)
    (shard_a,) = call(
        first_pack_kernel, [heads, outs, swap2(layer_input[0]), norm_params.reshape(8, HD)], [(2 * HD + 8, D)], vmem=8,
    )
    shard_f, shard_b, *late = call(
        functools.partial(pack_kernel, rows),
        [idx, heads, outs, ups, downs, swap2(output_grad[0]), head_moment, out_moment, up_moment, swap2(down_moment)],
        [(2 * HD, D), (3 * HD, D)] + [(3 * HD, D)] * rows, [(rows, 2 * HD, D)], vmem=8,
    )
    pieces = spread_rows([shard_a] * rows)
    mine_a = jnp.stack(pieces)
    packs_a = spread_cols(mine_a)
    shard_f, _ = lax.optimization_barrier((shard_f, packs_a[1]))
    rows_f = jnp.stack(spread_rows([shard_f] * rows))
    packs_f = spread_cols(rows_f)
    *late, _ = lax.optimization_barrier((*late, rows_f))
    late = spread_rows(late)
    shard_b, _ = lax.optimization_barrier((shard_b, mine_a))
    pack_b = lax.all_gather(shard_b, ("row", "col"), axis=0)
    seg_rows = segment_ids.reshape(cols, span)
    seg_col = segment_ids.reshape(cols, span, 1)

    full = (cols, span, D)
    pair = (2, span, D)
    own = (span, D)
    wide = (span, FF)
    half = (D, cols * TILE)
    keys = (length, cols * TILE)
    queries = (span, cols * TILE)
    one = (span, TILE)
    stats = (8, span)
    norms = (TILE, D)
    segs = [seg_rows, seg_col]

    h_full, wkv, wqo, kv, qx, att, lse, mid, n1, i1, ln = call(
        functools.partial(attention_kernel, rows, cols),
        [idx] + segs + packs_a,
        [full, half, half, keys, queries, queries, stats, own, own, one, (8, D)], flops=5 * 10**9, vmem=20,
    )
    h_own, up, dn, before, act, n2, i2 = call(
        functools.partial(feed_kernel, rows, cols),
        [mid, ln] + packs_f,
        [own, (D, FF), (D, FF), wide, wide, own, one], flops=2 * 10**9, vmem=12,
    )
    h_own, *late = lax.optimization_barrier((h_own, *late))
    hidden = spread_cols(h_own)
    top, *saved, keep, send = call(
        functools.partial(top_layer_kernel, rows, cols),
        [idx, ln] + segs + [pack_b] + late + hidden,
        [own, full, own, wide, queries, keys, queries, wide, own, own, norms, pair, pair],
        [half, half, keys, queries, stats, (D, FF), (D, FF), wide], flops=20 * 10**9, vmem=32,
    )
    layer_output = top[:, :HD][None]

    def fold_core(keep, send):
        got = perm(send, "col", 1)
        return got, perm(keep[1] + got[1], "col", 2)

    got, across = fold_core(keep, send)
    keep_t, send_t = call(
        functools.partial(top_gradients_kernel, rows, cols), [idx] + late + saved, [pair, pair],
        flops=2 * 10**9, vmem=10,
    )
    got_t = perm(send_t, "col", 1)
    half_t = keep_t[1] + got_t[1]
    got, half_t = lax.optimization_barrier((got, half_t))
    across_t = perm(half_t, "col", 2)
    keep_g, send_g, dkv, dqx, dv1 = call(
        functools.partial(low_layer_kernel, rows, cols),
        [idx, ln] + segs + late
        + [keep, got, across, h_full, mid, act, wqo, kv, qx, att, lse, n1, i1, up, dn, before, n2, i2],
        [pair, pair, keys, queries, own], [wide, own, norms], flops=12 * 10**9, vmem=20,
    )
    got, across = fold_core(keep_g, send_g)
    mine = keep_g[0] + got[0] + across
    top = keep_t[0] + got_t[0] + across_t
    top, mine = [
        lax.optimization_barrier(x + perm(x, "dp", 1) if dps == 2 else lax.psum(x, "dp")) for x in (top, mine)
    ]
    keep, send = call(
        low_input_kernel, [wkv, wqo, dkv, dqx, dv1], [pair, pair], flops=2 * 10**9, vmem=10,
    )
    got, across = fold_core(keep, send)
    input_grad = (keep[0] + got[0] + across)[:, :HD][None]

    tops, parts = spread_cols(top), spread_cols(mine)
    large, small = jnp.where(row < 2, top, mine), jnp.where(row < 2, mine, top)
    moms = jnp.concatenate([large.reshape(rows, HD, D), small.reshape(rows, HD, D)], axis=1)
    moms = spread_rows([moms[k] for k in range(rows)])
    large, small = call(
        functools.partial(orthogonal_kernel, cols), [idx] + tops + parts, [own, (D, TILE)],
        [(D, FF), (D, cols * TILE)], flops=8 * 10**9, vmem=24,
    )
    steps = jnp.concatenate([large.reshape(rows, HD, D), small.reshape(rows, HD, TILE)], axis=2)
    steps = spread_rows([steps[k] for k in range(rows)])
    three = (LAYERS, 4, HD)
    updates = list(call(
        functools.partial(update_kernel, rows),
        [idx, heads, outs, ups, downs, norm_params, norm_first, norm_second] + moms + steps,
        [heads.shape, outs.shape, ups.shape, downs.shape] * 2 + [three] * 3,
        [(rows, 2 * HD, D), (rows, HD, D + TILE)], vmem=8,
    ))
    for at in (3, 7):
        updates[at] = swap2(updates[at])
    return (layer_output, input_grad, *updates)


def solution(mesh):
    placed = (
        P("dp", "col", "row"),
        P("dp", None),
        P(None, None, "row", "col"),
        P(None, "col", "row"),
        P(None, "row", "col"),
        P(None, "col", "row"),
        P(None, None, "row", "col"),
        P(None, "col", "row"),
        P(None, "row", "col"),
        P(None, "col", "row"),
        P(None, None, "row"),
        P(None, None, "row"),
        P(None, None, "row"),
        P("dp", "col", "row"),
    )
    return jax.shard_map(
        on_device,
        mesh=mesh,
        in_specs=placed,
        out_specs=(
            P("dp", "col", "row"),
            P("dp", "col", "row"),
            P(None, None, "row", "col"),
            P(None, "col", "row"),
            P(None, "row", "col"),
            P(None, "col", "row"),
            P(None, None, "row", "col"),
            P(None, "col", "row"),
            P(None, "row", "col"),
            P(None, "col", "row"),
            P(None, None, "row"),
            P(None, None, "row"),
            P(None, None, "row"),
        ),
        check_vma=False,
    )
```

```python
import functools
import math

import jax
import jax.numpy as jnp
from jax import lax
from jax.experimental import pallas as pl
from jax.experimental.pallas import tpu as pltpu
from jax.sharding import PartitionSpec as P

D = 256
FF = 1024
LAYERS = 2
NS_STEPS = 5
STEP = 10
HD = 64
TILE = 128

norm_eps = 1e-05
newton_coefs = (3.4445, -4.775, 2.0315)
frob_eps = 1e-07
muon_decay = 0.95
muon_rate = 0.5
adam_first = 0.9
adam_second = 0.999
adam_eps = 1e-08
adam_rate = 0.2
masked_score = -1e30

f32 = jnp.float32
bf16 = jnp.bfloat16

NN = (((1,), (0,)), ((), ()))
NT = (((1,), (1,)), ((), ()))
TN = (((0,), (0,)), ((), ()))


def dot(a, b, dims=NN):
    return lax.dot_general(a, b, dims, precision=lax.Precision.HIGH, preferred_element_type=f32)


def dot1(a, b, dims=NN):
    return lax.dot_general(a, b, dims, preferred_element_type=f32)


def low_lanes(rows):
    return lax.broadcasted_iota(jnp.int32, (rows, TILE), 1) < HD


def swap(t):
    return pltpu.roll(t, HD, 1)


def dup_low(t):
    return jnp.where(low_lanes(t.shape[0]), t, swap(t))


def dup_high(t):
    return jnp.where(low_lanes(t.shape[0]), swap(t), t)


def halves(t):
    high = t.astype(bf16)
    return high, (t - high.astype(f32)).astype(bf16)


def mixed(t):
    high = t.astype(bf16).astype(f32)
    return jnp.where(low_lanes(t.shape[0]), high, t - high).astype(bf16)


def high_only(t):
    return jnp.where(low_lanes(t.shape[0]), t, 0.0).astype(bf16)


def left_stack(t):
    m = mixed(t)
    return jnp.concatenate([m, m], axis=1)


def right_stack(t):
    high, low = halves(t)
    return jnp.concatenate([high, low], axis=1)


def normalize(values):
    mean = jnp.sum(values, axis=-1, keepdims=True) * (1.0 / D)
    center = values - mean
    variance = jnp.sum(center * center, axis=-1, keepdims=True) * (1.0 / D)
    inverse = lax.rsqrt(variance + norm_eps)
    return center * inverse, inverse


def normalize_back(grad_out, normed, inverse, gain):
    scaled = grad_out * gain
    first = jnp.sum(scaled, axis=-1, keepdims=True) * (1.0 / D)
    second = jnp.sum(scaled * normed, axis=-1, keepdims=True) * (1.0 / D)
    grad_in = inverse * (scaled - first - normed * second)
    gain_grad = jnp.sum(grad_out * normed, axis=0, keepdims=True)
    shift_grad = jnp.sum(grad_out, axis=0, keepdims=True)
    return grad_in, gain_grad, shift_grad


def pack_reader(gathered, rows, cols, refs, c, z):
    if gathered:
        return lambda r, k, lo, hi: refs[0][(z ^ r) * cols + (c ^ k), lo:hi, :]
    return lambda r, k, lo, hi: refs[k][r, lo:hi, :]


def project_and_attend(c, h, wkv_ref, wqo_ref, seg_ref, segcol_ref, kv_ref, qx_ref, att_ref, lse_ref):
    cols = h.shape[0]
    span = h.shape[1]
    wkv = wkv_ref[...]
    for j in range(cols):
        kv_ref[j * span:(j + 1) * span, :] = dot(h[j], wkv)
    h_own = h[0]
    qx_ref[...] = dot(h_own, wqo_ref[...])
    lane = lax.broadcasted_iota(jnp.int32, (span, TILE), 1)
    seg_row = jnp.concatenate([seg_ref[pl.ds(c ^ k, 1), :] for k in range(cols)], axis=1)
    allowed = segcol_ref[c] == seg_row
    lse_all = jnp.zeros((span, TILE), f32)
    for j in range(cols):
        tile = slice(j * TILE, (j + 1) * TILE)
        kv = kv_ref[:, tile]
        k_right = right_stack(dup_low(kv))
        v_dup = dup_high(kv)
        v_mix = mixed(v_dup)
        v_high = high_only(v_dup)
        q_left = left_stack(dup_low(qx_ref[:, tile]) * (HD ** -0.5))
        scores = jnp.where(allowed, dot1(q_left, k_right, NT), masked_score)
        top = jnp.max(scores, axis=-1, keepdims=True)
        raised = jnp.exp(scores - top)
        total = jnp.sum(raised, axis=-1, keepdims=True)
        p_high, p_low = halves(raised)
        out = dot1(p_high, v_mix) + dot1(p_low, v_high)
        out = (out + swap(out)) / total
        att_ref[:, tile] = jnp.where(low_lanes(span), 0.0, out)
        lse_all = jnp.where(lane == j, top + jnp.log(total), lse_all)
    lse_ref[...] = jnp.transpose(lse_all)[0:8, :]
    return dot(att_ref[...], wqo_ref[...], NT), h_own


def place_attention(rows, cols, block, wkv_ref, wqo_ref):
    for j in range(cols):
        for r in range(rows):
            piece = block(r, j, 0, HD)
            wkv_ref[r * HD:(r + 1) * HD, j * TILE:(j + 1) * TILE] = piece[:, :TILE]
            wqo_ref[r * HD:(r + 1) * HD, j * TILE:(j + 1) * TILE] = piece[:, TILE:]


def place_feed(rows, cols, block, at, up_ref, dn_ref):
    for j in range(cols):
        for r in range(rows):
            to = (slice(r * HD, (r + 1) * HD), slice(j * 2 * TILE, (j + 1) * 2 * TILE))
            up_ref[to] = block(r, j, at, at + HD)
            dn_ref[to] = block(r, j, at + HD, at + 2 * HD)


def feed_forward(mid, up_ref, dn_ref, before_ref, act_ref):
    before = dot(mid, up_ref[...])
    before_ref[...] = before
    activated = 0.5 * before * (1.0 + lax.erf(before * 0.7071067811865476))
    act_ref[...] = activated
    return normalize(mid + dot(activated, dn_ref[...], NT))


def attention_kernel(rows, cols, idx_ref, seg_ref, segcol_ref, *refs):
    c, z = idx_ref[0], idx_ref[1]
    packs, refs = refs[:cols], refs[cols:]
    h_out, wkv_out, wqo_out, kv_out, qx_out, att_out, lse_out, mid_out, n1_out, i1_out, params_out = refs
    block = pack_reader(False, rows, cols, packs, c, z)
    span = mid_out.shape[0]
    place_attention(rows, cols, block, wkv_out, wqo_out)
    for j in range(cols):
        h_out[j] = jnp.transpose(
            jnp.concatenate([block(r, j, HD, 2 * HD) for r in range(rows)], axis=0)
        )
    tiles = []
    for t in range(rows // 2):
        a = block(2 * t, 0, 2 * HD, 2 * HD + 8)[:, 0:TILE]
        b = block(2 * t + 1, 0, 2 * HD, 2 * HD + 8)[:, 0:TILE]
        tiles.append(jnp.where(low_lanes(8), a, swap(b)))
    params_out[...] = jnp.concatenate(tiles, axis=1)
    branch, h_own = project_and_attend(
        c, h_out, wkv_out, wqo_out, seg_ref, segcol_ref, kv_out, qx_out, att_out, lse_out
    )
    normed, inverse = normalize(h_own + branch)
    n1_out[...] = normed
    i1_out[...] = jnp.broadcast_to(inverse, (span, TILE))
    mid_out[...] = normed * params_out[0:1, :] + params_out[1:2, :]


def feed_kernel(rows, cols, mid_ref, ln_ref, *refs):
    packs, refs = refs[:cols], refs[cols:]
    h_out, up_out, dn_out, before_out, act_out, n2_out, i2_out = refs
    block = pack_reader(False, rows, cols, packs, 0, 0)
    place_feed(rows, cols, block, 0, up_out, dn_out)
    normed, inverse = feed_forward(mid_ref[...], up_out, dn_out, before_out, act_out)
    n2_out[...] = normed
    i2_out[...] = jnp.broadcast_to(inverse, i2_out.shape)
    h_out[...] = normed * ln_ref[2:3, :] + ln_ref[3:4, :]


def backward(
    c, dh, gains, seg_ref, segcol_ref, wqo_ref, kv_ref, qx_ref, att_ref, lse_ref, n1, i1, up_ref, dn_ref,
    before_ref, n2, i2, dkv_ref, dqx_ref, dbef_ref, dv1_ref, dv2_ref, norm_ref
):
    span = n1.shape[0]
    cols = segcol_ref.shape[0]
    dv2, gain2, shift2 = normalize_back(dh, n2, i2, gains[2])
    dv2_ref[...] = dv2
    d_act = dot(dv2, dn_ref[...])
    before = before_ref[...]
    slope = (
        0.5 * (1.0 + lax.erf(before * 0.7071067811865476))
        + before * jnp.exp(-0.5 * before * before) * 0.3989422804014327
    )
    dbef_ref[...] = d_act * slope
    d_mid = dv2 + dot(dbef_ref[...], up_ref[...], NT)
    dv1, gain1, shift1 = normalize_back(d_mid, n1, i1, gains[0])
    dv1_ref[...] = dv1
    norm_ref[...] = jnp.zeros_like(norm_ref)
    for k, row in enumerate((gain1, shift1, gain2, shift2)):
        norm_ref[k:k + 1, :] = row
    d_att = dot(dv1, wqo_ref[...])
    lane = lax.broadcasted_iota(jnp.int32, (span, TILE), 1)
    inner_all = jnp.zeros((span, TILE), f32)
    for j in range(cols):
        tile = slice(j * TILE, (j + 1) * TILE)
        inner = jnp.sum(d_att[:, tile] * att_ref[:, tile], axis=-1, keepdims=True)
        inner_all = jnp.where(lane == j, inner, inner_all)
    inner_rows = jnp.transpose(inner_all)
    seg_row = seg_ref[pl.ds(c, 1), :]
    low = low_lanes(span)
    for j in range(cols):
        tile = slice(j * TILE, (j + 1) * TILE)
        q_dup = dup_low(qx_ref[:, tile]) * (HD ** -0.5)
        q_mix = mixed(q_dup)
        q_left = jnp.concatenate([q_mix, q_mix], axis=1)
        q_high = high_only(q_dup)
        do_dup = dup_high(d_att[:, tile])
        do_mix = mixed(do_dup)
        do_left = jnp.concatenate([do_mix, do_mix], axis=1)
        do_high = high_only(do_dup)
        lse_row = lse_ref[j:j + 1, :]
        inner_row = inner_rows[j:j + 1, :]
        dq_t = jnp.zeros((TILE, span), f32)
        for b in range(cols):
            keys = slice(b * span, (b + 1) * span)
            kv = kv_ref[keys, tile]
            k_dup = dup_low(kv)
            v_dup = dup_high(kv)
            scores = dot1(right_stack(k_dup), q_left, NT)
            shares = jnp.where(segcol_ref[c ^ b] == seg_row, jnp.exp(scores - lse_row), 0.0)
            d_shares = dot1(right_stack(v_dup), do_left, NT)
            d_scores = shares * (d_shares - inner_row)
            p_high, p_low = halves(shares)
            s_high, s_low = halves(d_scores)
            dv = dot1(p_high, do_mix) + dot1(p_low, do_high)
            dk = dot1(s_high, q_mix) + dot1(s_low, q_high)
            dkv_ref[keys, tile] = jnp.where(low, dk + swap(dk), dv + swap(dv))
            k_t = jnp.transpose(k_dup)
            k_t_high = k_t.astype(bf16)
            upper = lax.broadcasted_iota(jnp.int32, (TILE, span), 0) < HD
            k_t_mix = jnp.where(upper, k_t_high.astype(f32), k_t - k_t_high.astype(f32)).astype(bf16)
            k_t_only = jnp.where(upper, k_t, 0.0).astype(bf16)
            dq_t = dq_t + dot1(k_t_mix, s_high) + dot1(k_t_only, s_low)
        dq = jnp.transpose(dq_t)
        dqx_ref[:, tile] = jnp.where(low, (dq + swap(dq)) * (HD ** -0.5), 0.0)


def input_gradient(wkv_ref, wqo_ref, dkv_ref, dqx_ref, dv1_ref, keep_out, send_out):
    span = dv1_ref.shape[0]
    wkv = wkv_ref[...]
    for k in (1, 3, 0, 2):
        part = dot(dkv_ref[k * span:(k + 1) * span, :], wkv, NT)
        if k == 0:
            part = part + dot(dqx_ref[...], wqo_ref[...], NT) + dv1_ref[...]
        (send_out if k % 2 else keep_out)[k // 2] = part


def weight_gradients(
    role, cols, h_ref, mid_ref, act_ref, att_ref, dkv_ref, dqx_ref, dbef_ref, dv1_ref, dv2_ref, norm_ref, grad_at
):
    span = dv1_ref.shape[0]

    @pl.when(role == 0)
    def _():
        mid = mid_ref[...]
        for k in range(cols):
            grad_at(k)[...] = dot(mid, dbef_ref[:, k * 2 * TILE:(k + 1) * 2 * TILE], TN)

    @pl.when(role == 1)
    def _():
        for k in range(cols):
            grad_at(k)[...] = dot(dv2_ref[...], act_ref[:, k * 2 * TILE:(k + 1) * 2 * TILE], TN)

    @pl.when(role == 2)
    def _():
        total = dot(h_ref[0], dkv_ref[0:span, :], TN)
        for b in range(1, cols):
            total += dot(h_ref[b], dkv_ref[b * span:(b + 1) * span, :], TN)
        for k in range(cols):
            grad_at(k)[:, 0:TILE] = total[:, k * TILE:(k + 1) * TILE]
            grad_at(k)[:, TILE:] = jnp.zeros((D, TILE), f32)

    @pl.when(role == 3)
    def _():
        total = dot(h_ref[0], dqx_ref[...], TN) + dot(dv1_ref[...], att_ref[...], TN)
        norms = jnp.transpose(norm_ref[...])
        for k in range(cols):
            grad_at(k)[:, 0:TILE] = total[:, k * TILE:(k + 1) * TILE]
            grad_at(k)[:, TILE:] = norms


def top_layer_kernel(rows, cols, idx_ref, ln_ref, seg_ref, segcol_ref, pack_ref, *refs):
    c, z = idx_ref[0], idx_ref[1]
    late_refs, h_refs, refs = refs[:rows], refs[rows:rows + cols], refs[rows + cols:]
    (out_ref, h_full, mid_ref, act_ref, att_ref, dkv_ref, dqx_ref, dbef_ref, dv1_ref, dv2_ref, norm_ref,
     keep_out, send_out, wkv_ref, wqo_ref, kv_ref, qx_ref, lse_ref, up_ref, dn_ref, before_ref) = refs
    block = pack_reader(True, rows, cols, (pack_ref,), c, z)
    place_attention(rows, cols, block, wkv_ref, wqo_ref)
    place_feed(rows, cols, block, HD, up_ref, dn_ref)
    for j in range(cols):
        h_full[j] = h_refs[j][...]
    gains = [ln_ref[k:k + 1, :] for k in range(4, 8)]
    branch, h_own = project_and_attend(
        c, h_full, wkv_ref, wqo_ref, seg_ref, segcol_ref, kv_ref, qx_ref, att_ref, lse_ref
    )
    n1, i1 = normalize(h_own + branch)
    mid_ref[...] = n1 * gains[0] + gains[1]
    n2, i2 = feed_forward(mid_ref[...], up_ref, dn_ref, before_ref, act_ref)
    out_ref[...] = n2 * gains[2] + gains[3]
    dh = jnp.transpose(jnp.concatenate([ref[...] for ref in late_refs], axis=0))
    backward(
        c, dh, gains, seg_ref, segcol_ref, wqo_ref, kv_ref, qx_ref, att_ref, lse_ref, n1, i1, up_ref, dn_ref,
        before_ref, n2, i2, dkv_ref, dqx_ref, dbef_ref, dv1_ref, dv2_ref, norm_ref
    )
    input_gradient(wkv_ref, wqo_ref, dkv_ref, dqx_ref, dv1_ref, keep_out, send_out)


def add_moment(idx_ref, late_refs, big, at):
    first = 0 if big else HD

    @pl.when(idx_ref[2] == 0)
    def _():
        for r, ref in enumerate(late_refs):
            at[r * HD:(r + 1) * HD, :] += ref[first:first + HD, :]


def top_gradients_kernel(rows, cols, idx_ref, *refs):
    z = idx_ref[1]
    late_refs, refs = refs[:rows], refs[rows:]
    keep_out, send_out = refs[-2:]
    weight_gradients(z, cols, *refs[:-2], lambda k: (send_out if k % 2 else keep_out).at[k // 2])
    for big in (True, False):

        @pl.when((z < 2) == big)
        def _():
            add_moment(idx_ref, late_refs, big, keep_out.at[0])


def low_layer_kernel(rows, cols, idx_ref, ln_ref, seg_ref, segcol_ref, *refs):
    late_refs, refs = refs[:rows], refs[rows:]
    z = idx_ref[1]
    (dh_keep, dh_got, dh_across, h_ref, mid_ref, act_ref, wqo_ref, kv_ref, qx_ref, att_ref, lse_ref, n1_ref,
     i1_ref, up_ref, dn_ref, before_ref, n2_ref, i2_ref, keep_out, send_out, dkv_ref, dqx_ref, dv1_ref,
     dbef_ref, dv2_ref, norm_ref) = refs
    dh = dh_keep[0] + dh_got[0] + dh_across[...]
    gains = [ln_ref[k:k + 1, :] for k in range(4)]
    backward(
        idx_ref[0], dh, gains, seg_ref, segcol_ref, wqo_ref, kv_ref, qx_ref, att_ref, lse_ref, n1_ref[...],
        i1_ref[:, 0:1], up_ref, dn_ref, before_ref, n2_ref[...], i2_ref[:, 0:1], dkv_ref, dqx_ref, dbef_ref,
        dv1_ref, dv2_ref, norm_ref
    )
    weight_gradients(
        z ^ 2, cols, h_ref, mid_ref, act_ref, att_ref, dkv_ref, dqx_ref, dbef_ref, dv1_ref, dv2_ref, norm_ref,
        lambda k: (send_out if k % 2 else keep_out).at[k // 2]
    )
    for big in (True, False):

        @pl.when((z >= 2) == big)
        def _():
            add_moment(idx_ref, late_refs, big, keep_out.at[0])


def low_input_kernel(*refs):
    input_gradient(*refs)


def newton_schulz(blocks):
    sizes = [jnp.sum(x * x, keepdims=True) for x in blocks]
    blocks = [x / (jnp.sqrt(s) + frob_eps) for x, s in zip(blocks, sizes)]
    for _ in range(NS_STEPS):
        grams = [dot(x, x, NT) for x in blocks]
        squares = [dot(a, a) for a in grams]
        polys = [newton_coefs[1] * a + newton_coefs[2] * s for a, s in zip(grams, squares)]
        blocks = [newton_coefs[0] * x + dot(p, x) for p, x in zip(polys, blocks)]
    return blocks


def orthogonal_kernel(cols, idx_ref, *refs):
    z = idx_ref[1]
    top_refs, low_refs = refs[:cols], refs[cols:2 * cols]
    big_out, small_out, big, small = refs[2 * cols:]

    @pl.when(z < 2)
    def _():
        for k in range(cols):
            big[:, k * 2 * TILE:(k + 1) * 2 * TILE] = top_refs[k][...]
            small[:, k * TILE:(k + 1) * TILE] = low_refs[k][:, 0:TILE]

    @pl.when(z >= 2)
    def _():
        for k in range(cols):
            big[:, k * 2 * TILE:(k + 1) * 2 * TILE] = low_refs[k][...]
            small[:, k * TILE:(k + 1) * TILE] = top_refs[k][:, 0:TILE]

    low = low_lanes(D)
    lefts, rights = [], []
    for t in range(cols // 2):
        a = small[:, 2 * t * TILE:(2 * t + 1) * TILE]
        b = small[:, (2 * t + 1) * TILE:(2 * t + 2) * TILE]
        lefts.append(jnp.where(low, a, swap(b)))
        rights.append(jnp.where(low, swap(a), b))
    wide, left, right = newton_schulz(
        [big[...], jnp.concatenate(lefts, axis=1), jnp.concatenate(rights, axis=1)]
    )
    big_out[...] = wide[:, 0:2 * TILE] * math.sqrt(FF)
    small_out[...] = jnp.where(low, left[:, 0:TILE], swap(right[:, 0:TILE])) * math.sqrt(D)


def first_pack_kernel(heads_hbm, outs_hbm, x_hbm, params_hbm, shard_out, heads_ref, outs_ref, params_ref, sems):
    shard_out[2 * HD:, :] = jnp.zeros((8, 2 * TILE), f32)
    copies = [
        pltpu.make_async_copy(source, target, sems.at[i])
        for i, (source, target) in enumerate(
            (
                (heads_hbm.at[0], heads_ref),
                (outs_hbm.at[0], outs_ref),
                (params_hbm, params_ref),
                (x_hbm, shard_out.at[pl.ds(HD, HD)]),
            )
        )
    ]
    for copy in copies:
        copy.start()
    for copy in copies:
        copy.wait()
    shard_out[0:HD, 0:HD] = heads_ref[1]
    shard_out[0:HD, HD:TILE] = heads_ref[2]
    shard_out[0:HD, TILE:TILE + HD] = heads_ref[0]
    shard_out[0:HD, TILE + HD:] = jnp.transpose(outs_ref[...])
    shard_out[2 * HD:, 0:HD] = params_ref[...]


def pack_kernel(
    rows, idx_ref, heads_ref, outs_ref, up_ref, dn_ref, mh_ref, mo_ref, mu_ref, md_ref, f_out, b_out, *refs
):
    z = idx_ref[1]
    late_outs, moments = refs[:rows], refs[rows]
    f_out[0:HD, :] = up_ref[0]
    f_out[HD:, :] = dn_ref[0]
    b_out[0:HD, 0:HD] = heads_ref[1, 1]
    b_out[0:HD, HD:TILE] = heads_ref[1, 2]
    b_out[0:HD, TILE:TILE + HD] = heads_ref[1, 0]
    b_out[0:HD, TILE + HD:] = jnp.transpose(outs_ref[1])
    b_out[HD:2 * HD, :] = up_ref[1]
    b_out[2 * HD:, :] = dn_ref[1]
    for l in range(LAYERS):
        large, small = (0, 2) if l else (2, 0)
        moments[large, 0:HD, :] = mu_ref[l] * muon_decay
        moments[large + 1, 0:HD, :] = md_ref[l] * muon_decay
        moments[small, HD:, 0:HD] = mh_ref[l, 1] * muon_decay
        moments[small, HD:, HD:TILE] = mh_ref[l, 2] * muon_decay
        moments[small + 1, HD:, 0:HD] = mh_ref[l, 0] * muon_decay
        moments[small + 1, HD:, HD:TILE] = jnp.transpose(mo_ref[l]) * muon_decay
    for r in range(rows):
        moments[r, HD:, TILE:] = jnp.zeros((HD, TILE), f32)
    for k in range(rows):
        late_outs[k][...] = moments[z ^ k]


def update_kernel(
    rows, idx_ref, heads_ref, outs_ref, up_ref, dn_ref, params_ref, first_ref, second_ref, *refs
):
    z = idx_ref[1]
    mom_refs, step_refs, refs = refs[:rows], refs[rows:2 * rows], refs[2 * rows:]
    (heads_out, outs_out, up_out, dn_out, mh_out, mo_out, mu_out, md_out, first_out, second_out, params_out,
     mom, step) = refs
    for k in range(rows):
        mom[z ^ k] = mom_refs[k][...]
        step[z ^ k] = step_refs[k][...] * muon_rate
    for l in range(LAYERS):
        large, small = (0, 2) if l else (2, 0)
        mu_out[l] = mom[large, 0:HD, :]
        md_out[l] = mom[large + 1, 0:HD, :]
        up_out[l] = up_ref[l] - D ** -0.5 * step[large, :, 0:2 * TILE]
        dn_out[l] = dn_ref[l] - FF ** -0.5 * step[large + 1, :, 0:2 * TILE]
        kv, qo = mom[small, HD:, 0:TILE], mom[small + 1, HD:, 0:TILE]
        mh_out[l, 0] = qo[:, 0:HD]
        mh_out[l, 1] = kv[:, 0:HD]
        mh_out[l, 2] = swap(kv)[:, 0:HD]
        mo_out[l] = jnp.transpose(swap(qo))[0:HD, :]
        kv, qo = step[small, :, 2 * TILE:], step[small + 1, :, 2 * TILE:]
        heads_out[l, 0] = heads_ref[l, 0] - D ** -0.5 * qo[:, 0:HD]
        heads_out[l, 1] = heads_ref[l, 1] - D ** -0.5 * kv[:, 0:HD]
        heads_out[l, 2] = heads_ref[l, 2] - D ** -0.5 * swap(kv)[:, 0:HD]
        outs_out[l] = outs_ref[l] - (D // 16) ** -0.5 * jnp.transpose(swap(qo))[0:HD, :]
        grad = jnp.transpose(mom[small + 1, HD:, TILE:])[0:4, :]
        first = adam_first * first_ref[l] + (1.0 - adam_first) * grad
        second = adam_second * second_ref[l] + (1.0 - adam_second) * grad * grad
        first_out[l] = first
        second_out[l] = second
        params_out[l] = params_ref[l] - adam_rate * (first / (1.0 - adam_first**STEP)) / (
            jnp.sqrt(second / (1.0 - adam_second**STEP)) + adam_eps
        )


def call(body, operands, outs, scratch=(), flops=0, vmem=50):
    specs = [pl.BlockSpec(memory_space=pltpu.SMEM if x.ndim == 1 else pltpu.VMEM) for x in operands]
    moved = sum(4 * math.prod(x.shape) for x in operands) + sum(4 * math.prod(s) for s in outs)
    return pl.pallas_call(
        body,
        out_shape=[jax.ShapeDtypeStruct(s, f32) for s in outs],
        in_specs=specs,
        out_specs=[pl.BlockSpec(memory_space=pltpu.VMEM) for _ in outs],
        scratch_shapes=[pltpu.VMEM(s, f32) for s in scratch],
        compiler_params=pltpu.CompilerParams(vmem_limit_bytes=vmem * 2**20),
        cost_estimate=pl.CostEstimate(flops=flops, bytes_accessed=moved, transcendentals=0),
    )(*operands)


def fetched_call(body, idx, operands, outs, scratch):
    count, given = len(operands), len(outs) + len(scratch)

    def kernel(idx_ref, *refs):
        sources, rest, held, sems = refs[:count], refs[count:count + given], refs[count + given:-1], refs[-1]
        copies = [pltpu.make_async_copy(a, b, sems.at[i]) for i, (a, b) in enumerate(zip(sources, held))]
        for copy in copies:
            copy.start()
        for copy in copies:
            copy.wait()
        body(idx_ref, *held, *rest)

    return pl.pallas_call(
        kernel,
        out_shape=[jax.ShapeDtypeStruct(s, f32) for s in outs],
        in_specs=[pl.BlockSpec(memory_space=pltpu.SMEM)] + [pl.BlockSpec(memory_space=pltpu.HBM)] * count,
        out_specs=[pl.BlockSpec(memory_space=pltpu.VMEM) for _ in outs],
        scratch_shapes=[pltpu.VMEM(s, f32) for s in scratch]
        + [pltpu.VMEM(x.shape, f32) for x in operands] + [pltpu.SemaphoreType.DMA((count,))],
        compiler_params=pltpu.CompilerParams(vmem_limit_bytes=56 * 2**20),
    )(idx, *operands)


def on_device(
    layer_input,
    segment_ids,
    head_projection_weights,
    output_projection_weights,
    up_projection_weights,
    down_projection_weights,
    head_moment,
    out_moment,
    up_moment,
    down_moment,
    norm_params,
    norm_first,
    norm_second,
    output_grad,
):
    row = lax.axis_index("row").astype(jnp.int32)
    col = lax.axis_index("col").astype(jnp.int32)
    rows = lax.axis_size("row")
    cols = lax.axis_size("col")
    dps = lax.axis_size("dp")
    span = layer_input.shape[1]
    length = span * cols
    idx = jnp.stack([col, row, lax.axis_index("dp").astype(jnp.int32)])
    swap2 = lambda x: jnp.swapaxes(x, -1, -2)

    def perm(x, axis, bit):
        return lax.ppermute(x, axis, [(i, i ^ bit) for i in range(lax.axis_size(axis))])

    def spread_cols(x):
        across = perm(x, "col", 2)
        return [x, perm(x, "col", 1), across, perm(across, "col", 1)]

    def spread_rows(parts):
        return [parts[0]] + [perm(parts[k], "row", k) for k in range(1, rows)]

    heads, outs, ups = head_projection_weights, output_projection_weights, up_projection_weights
    downs = swap2(down_projection_weights)
    shard_a = pl.pallas_call(
        first_pack_kernel,
        out_shape=jax.ShapeDtypeStruct((2 * HD + 8, D), f32),
        in_specs=[pl.BlockSpec(memory_space=pltpu.HBM)] * 4,
        out_specs=pl.BlockSpec(memory_space=pltpu.VMEM),
        scratch_shapes=[
            pltpu.VMEM((3, HD, HD), f32), pltpu.VMEM((HD, HD), f32), pltpu.VMEM((8, HD), f32), pltpu.SemaphoreType.DMA((4,)),
        ],
        compiler_params=pltpu.CompilerParams(vmem_limit_bytes=60 * 2**20),
    )(heads, outs, swap2(layer_input[0]), norm_params.reshape(8, HD))
    og = swap2(output_grad[0])
    shard_f, shard_b, *moments = fetched_call(
        functools.partial(pack_kernel, rows),
        idx, [heads, outs, ups, downs, head_moment, out_moment, up_moment, swap2(down_moment)],
        [(2 * HD, D), (3 * HD, D)] + [(2 * HD, D)] * rows, [(rows, 2 * HD, D)],
    )
    pieces = spread_rows([shard_a] * rows)
    *pieces, shard_f = lax.optimization_barrier((*pieces, shard_f))
    mine_a = jnp.stack(pieces)
    across_a, core_a = perm(mine_a, "col", 2), perm(mine_a, "col", 1)
    shard_f, _ = lax.optimization_barrier((shard_f, core_a))
    mine_f = jnp.stack(spread_rows([shard_f] * rows))
    across_a, mine_f = lax.optimization_barrier((across_a, mine_f))
    packs_a = [mine_a, core_a, across_a, perm(across_a, "col", 1)]
    across_f = perm(mine_f, "col", 2)
    shard_b, _ = lax.optimization_barrier((shard_b, mine_a))
    pack_b = lax.all_gather(shard_b, ("row", "col"), axis=0)
    seg_rows = segment_ids.reshape(cols, span)
    seg_col = segment_ids.reshape(cols, span, 1)

    full = (cols, span, D)
    pair = (2, span, D)
    own = (span, D)
    wide = (span, FF)
    half = (D, cols * TILE)
    keys = (length, cols * TILE)
    queries = (span, cols * TILE)
    one = (span, TILE)
    stats = (8, span)
    norms = (TILE, D)
    segs = [seg_rows, seg_col]

    h_full, wkv, wqo, kv, qx, att, lse, mid, n1, i1, ln = call(
        functools.partial(attention_kernel, rows, cols),
        [idx] + segs + packs_a,
        [full, half, half, keys, queries, queries, stats, own, own, one, (8, D)], flops=5 * 10**9, vmem=12,
    )
    mid, across_f, og, *moments = lax.optimization_barrier((mid, across_f, og, *moments))
    packs_f = [mine_f, perm(mine_f, "col", 1), across_f, perm(across_f, "col", 1)]
    og = spread_rows([og] * rows)
    moments = spread_rows(moments)
    h_own, up, dn, before, act, n2, i2 = call(
        functools.partial(feed_kernel, rows, cols),
        [mid, ln] + packs_f,
        [own, (D, FF), (D, FF), wide, wide, own, one], flops=2 * 10**9, vmem=8,
    )
    hidden = spread_cols(h_own)
    top, *saved, keep, send = call(
        functools.partial(top_layer_kernel, rows, cols),
        [idx, ln] + segs + [pack_b] + og + hidden,
        [own, full, own, wide, queries, keys, queries, wide, own, own, norms, pair, pair],
        [half, half, keys, queries, stats, (D, FF), (D, FF), wide], flops=20 * 10**9, vmem=18,
    )
    layer_output = top[:, :HD][None]

    def fold_core(keep, send):
        got = perm(send, "col", 1)
        return got, perm(keep[1] + got[1], "col", 2)

    got, across = fold_core(keep, send)
    keep_t, send_t = call(
        functools.partial(top_gradients_kernel, rows, cols), [idx] + moments + saved, [pair, pair],
        flops=2 * 10**9, vmem=6,
    )
    got_t = perm(send_t, "col", 1)
    half_t = keep_t[1] + got_t[1]
    got, half_t = lax.optimization_barrier((got, half_t))
    across_t = perm(half_t, "col", 2)
    keep_g, send_g, dkv, dqx, dv1 = call(
        functools.partial(low_layer_kernel, rows, cols),
        [idx, ln] + segs + moments
        + [keep, got, across, h_full, mid, act, wqo, kv, qx, att, lse, n1, i1, up, dn, before, n2, i2],
        [pair, pair, keys, queries, own], [wide, own, norms], flops=12 * 10**9, vmem=12,
    )
    got, across = fold_core(keep_g, send_g)
    mine = keep_g[0] + got[0] + across
    top = keep_t[0] + got_t[0] + across_t
    top, mine = [
        lax.optimization_barrier(x + perm(x, "dp", 1) if dps == 2 else lax.psum(x, "dp")) for x in (top, mine)
    ]
    keep, send = call(
        low_input_kernel, [wkv, wqo, dkv, dqx, dv1], [pair, pair], flops=2 * 10**9, vmem=6,
    )
    got, across = fold_core(keep, send)
    input_grad = (keep[0] + got[0] + across)[:, :HD][None]

    tops, parts = spread_cols(top), spread_cols(mine)
    large, small = jnp.where(row < 2, top, mine), jnp.where(row < 2, mine, top)
    moms = jnp.concatenate([large.reshape(rows, HD, D), small.reshape(rows, HD, D)], axis=1)
    moms = spread_rows([moms[k] for k in range(rows)])
    large, small = call(
        functools.partial(orthogonal_kernel, cols), [idx] + tops + parts, [own, (D, TILE)],
        [(D, FF), (D, cols * TILE)], flops=8 * 10**9, vmem=16,
    )
    steps = jnp.concatenate([large.reshape(rows, HD, D), small.reshape(rows, HD, TILE)], axis=2)
    steps = spread_rows([steps[k] for k in range(rows)])
    three = (LAYERS, 4, HD)
    updates = list(call(
        functools.partial(update_kernel, rows),
        [idx, heads, outs, ups, downs, norm_params, norm_first, norm_second] + moms + steps,
        [heads.shape, outs.shape, ups.shape, downs.shape] * 2 + [three] * 3,
        [(rows, 2 * HD, D), (rows, HD, D + TILE)], vmem=8,
    ))
    for at in (3, 7):
        updates[at] = swap2(updates[at])
    return (layer_output, input_grad, *updates)


def solution(mesh):
    placed = (
        P("dp", "col", "row"),
        P("dp", None),
        P(None, None, "row", "col"),
        P(None, "col", "row"),
        P(None, "row", "col"),
        P(None, "col", "row"),
        P(None, None, "row", "col"),
        P(None, "col", "row"),
        P(None, "row", "col"),
        P(None, "col", "row"),
        P(None, None, "row"),
        P(None, None, "row"),
        P(None, None, "row"),
        P("dp", "col", "row"),
    )
    return jax.shard_map(
        on_device,
        mesh=mesh,
        in_specs=placed,
        out_specs=(
            P("dp", "col", "row"),
            P("dp", "col", "row"),
            P(None, None, "row", "col"),
            P(None, "col", "row"),
            P(None, "row", "col"),
            P(None, "col", "row"),
            P(None, None, "row", "col"),
            P(None, "col", "row"),
            P(None, "row", "col"),
            P(None, "col", "row"),
            P(None, None, "row"),
            P(None, None, "row"),
            P(None, None, "row"),
        ),
        check_vma=False,
    )
```

```python
import functools
import math

import jax
import jax.numpy as jnp
from jax import lax
from jax.experimental import pallas as pl
from jax.experimental.pallas import tpu as pltpu
from jax.sharding import PartitionSpec as P

D = 256
FF = 1024
LAYERS = 2
NS_STEPS = 5
STEP = 10
HD = 64
TILE = 128

norm_eps = 1e-05
newton_coefs = (3.4445, -4.775, 2.0315)
frob_eps = 1e-07
muon_decay = 0.95
muon_rate = 0.5
adam_first = 0.9
adam_second = 0.999
adam_eps = 1e-08
adam_rate = 0.2
masked_score = -1e30

f32 = jnp.float32
bf16 = jnp.bfloat16

NN = (((1,), (0,)), ((), ()))
NT = (((1,), (1,)), ((), ()))
TN = (((0,), (0,)), ((), ()))


def dot(a, b, dims=NN):
    return lax.dot_general(a, b, dims, precision=lax.Precision.HIGH, preferred_element_type=f32)


def dot1(a, b, dims=NN):
    return lax.dot_general(a, b, dims, preferred_element_type=f32)


def low_lanes(rows):
    return lax.broadcasted_iota(jnp.int32, (rows, TILE), 1) < HD


def swap(t):
    return pltpu.roll(t, HD, 1)


def dup_low(t):
    return jnp.where(low_lanes(t.shape[0]), t, swap(t))


def dup_high(t):
    return jnp.where(low_lanes(t.shape[0]), swap(t), t)


def halves(t):
    high = t.astype(bf16)
    return high, (t - high.astype(f32)).astype(bf16)


def mixed(t):
    high = t.astype(bf16).astype(f32)
    return jnp.where(low_lanes(t.shape[0]), high, t - high).astype(bf16)


def high_only(t):
    return jnp.where(low_lanes(t.shape[0]), t, 0.0).astype(bf16)


def left_stack(t):
    m = mixed(t)
    return jnp.concatenate([m, m], axis=1)


def right_stack(t):
    high, low = halves(t)
    return jnp.concatenate([high, low], axis=1)


def normalize(values):
    mean = jnp.sum(values, axis=-1, keepdims=True) * (1.0 / D)
    center = values - mean
    variance = jnp.sum(center * center, axis=-1, keepdims=True) * (1.0 / D)
    inverse = lax.rsqrt(variance + norm_eps)
    return center * inverse, inverse


def normalize_back(grad_out, normed, inverse, gain):
    scaled = grad_out * gain
    first = jnp.sum(scaled, axis=-1, keepdims=True) * (1.0 / D)
    second = jnp.sum(scaled * normed, axis=-1, keepdims=True) * (1.0 / D)
    grad_in = inverse * (scaled - first - normed * second)
    gain_grad = jnp.sum(grad_out * normed, axis=0, keepdims=True)
    shift_grad = jnp.sum(grad_out, axis=0, keepdims=True)
    return grad_in, gain_grad, shift_grad


def pack_reader(refs):
    return lambda r, k, lo, hi: refs[k][r, lo:hi, :]


def segment_row(seg_ref, chunk, span):
    return seg_ref[:, pl.ds(pl.multiple_of(chunk * span, span), span)].astype(f32)


def segment_column(seg_ref, chunk, span):
    return jnp.transpose(jnp.broadcast_to(segment_row(seg_ref, chunk, span), (TILE, span)))[:, 0:1]


def project_and_attend(c, h, wkv_ref, wqo_ref, seg_ref, kv_ref, qx_ref, att_ref, lse_ref):
    cols = h.shape[0]
    span = h.shape[1]
    wkv = wkv_ref[...]
    for j in range(cols):
        kv_ref[j * span:(j + 1) * span, :] = dot(h[j], wkv)
    h_own = h[0]
    qx_ref[...] = dot(h_own, wqo_ref[...])
    lane = lax.broadcasted_iota(jnp.int32, (span, TILE), 1)
    seg_row = jnp.concatenate([segment_row(seg_ref, c ^ k, span) for k in range(cols)], axis=1)
    allowed = segment_column(seg_ref, c, span) == seg_row
    lse_all = jnp.zeros((span, TILE), f32)
    for j in range(cols):
        tile = slice(j * TILE, (j + 1) * TILE)
        kv = kv_ref[:, tile]
        k_right = right_stack(dup_low(kv))
        v_dup = dup_high(kv)
        v_mix = mixed(v_dup)
        v_high = high_only(v_dup)
        q_left = left_stack(dup_low(qx_ref[:, tile]) * (HD ** -0.5))
        scores = jnp.where(allowed, dot1(q_left, k_right, NT), masked_score)
        top = jnp.max(scores, axis=-1, keepdims=True)
        raised = jnp.exp(scores - top)
        total = jnp.sum(raised, axis=-1, keepdims=True)
        p_high, p_low = halves(raised)
        out = dot1(p_high, v_mix) + dot1(p_low, v_high)
        out = (out + swap(out)) / total
        att_ref[:, tile] = jnp.where(low_lanes(span), 0.0, out)
        lse_all = jnp.where(lane == j, top + jnp.log(total), lse_all)
    lse_ref[...] = jnp.transpose(lse_all)[0:8, :]
    return dot(att_ref[...], wqo_ref[...], NT), h_own


def place_attention(rows, cols, block, wkv_ref, wqo_ref):
    for j in range(cols):
        for r in range(rows):
            piece = block(r, j, 0, HD)
            wkv_ref[r * HD:(r + 1) * HD, j * TILE:(j + 1) * TILE] = piece[:, :TILE]
            wqo_ref[r * HD:(r + 1) * HD, j * TILE:(j + 1) * TILE] = piece[:, TILE:]


def place_feed(rows, cols, block, at, up_ref, dn_ref):
    for j in range(cols):
        for r in range(rows):
            to = (slice(r * HD, (r + 1) * HD), slice(j * 2 * TILE, (j + 1) * 2 * TILE))
            up_ref[to] = block(r, j, at, at + HD)
            dn_ref[to] = block(r, j, at + HD, at + 2 * HD)


def feed_forward(mid, up_ref, dn_ref, before_ref, act_ref):
    before = dot(mid, up_ref[...])
    before_ref[...] = before
    activated = 0.5 * before * (1.0 + lax.erf(before * 0.7071067811865476))
    act_ref[...] = activated
    return normalize(mid + dot(activated, dn_ref[...], NT))


def attention_kernel(rows, cols, idx_ref, seg_ref, *refs):
    c = idx_ref[0]
    packs, refs = refs[:cols], refs[cols:]
    h_out, wkv_out, wqo_out, kv_out, qx_out, att_out, lse_out, mid_out, n1_out, i1_out, params_out = refs
    block = pack_reader(packs)
    span = mid_out.shape[0]
    place_attention(rows, cols, block, wkv_out, wqo_out)
    for j in range(cols):
        h_out[j] = jnp.transpose(
            jnp.concatenate([block(r, j, HD, 2 * HD) for r in range(rows)], axis=0)
        )
    tiles = []
    for t in range(rows // 2):
        a = block(2 * t, 0, 2 * HD, 2 * HD + 8)[:, 0:TILE]
        b = block(2 * t + 1, 0, 2 * HD, 2 * HD + 8)[:, 0:TILE]
        tiles.append(jnp.where(low_lanes(8), a, swap(b)))
    params_out[...] = jnp.concatenate(tiles, axis=1)
    branch, h_own = project_and_attend(
        c, h_out, wkv_out, wqo_out, seg_ref, kv_out, qx_out, att_out, lse_out
    )
    normed, inverse = normalize(h_own + branch)
    n1_out[...] = normed
    i1_out[...] = jnp.broadcast_to(inverse, (span, TILE))
    mid_out[...] = normed * params_out[0:1, :] + params_out[1:2, :]


def feed_kernel(rows, cols, mid_ref, ln_ref, *refs):
    packs, refs = refs[:cols], refs[cols:]
    h_out, up_out, dn_out, before_out, act_out, n2_out, i2_out = refs
    block = pack_reader(packs)
    place_feed(rows, cols, block, 0, up_out, dn_out)
    normed, inverse = feed_forward(mid_ref[...], up_out, dn_out, before_out, act_out)
    n2_out[...] = normed
    i2_out[...] = jnp.broadcast_to(inverse, i2_out.shape)
    h_out[...] = normed * ln_ref[2:3, :] + ln_ref[3:4, :]


def backward(
    c, dh, gains, seg_ref, wqo_ref, kv_ref, qx_ref, att_ref, lse_ref, n1, i1, up_ref, dn_ref,
    before_ref, n2, i2, dkv_ref, dqx_ref, dbef_ref, dv1_ref, dv2_ref, norm_ref
):
    span = n1.shape[0]
    cols = seg_ref.shape[1] // span
    dv2, gain2, shift2 = normalize_back(dh, n2, i2, gains[2])
    dv2_ref[...] = dv2
    d_act = dot(dv2, dn_ref[...])
    before = before_ref[...]
    slope = (
        0.5 * (1.0 + lax.erf(before * 0.7071067811865476))
        + before * jnp.exp(-0.5 * before * before) * 0.3989422804014327
    )
    dbef_ref[...] = d_act * slope
    d_mid = dv2 + dot(dbef_ref[...], up_ref[...], NT)
    dv1, gain1, shift1 = normalize_back(d_mid, n1, i1, gains[0])
    dv1_ref[...] = dv1
    norm_ref[...] = jnp.zeros_like(norm_ref)
    for k, row in enumerate((gain1, shift1, gain2, shift2)):
        norm_ref[k:k + 1, :] = row
    d_att = dot(dv1, wqo_ref[...])
    lane = lax.broadcasted_iota(jnp.int32, (span, TILE), 1)
    inner_all = jnp.zeros((span, TILE), f32)
    for j in range(cols):
        tile = slice(j * TILE, (j + 1) * TILE)
        inner = jnp.sum(d_att[:, tile] * att_ref[:, tile], axis=-1, keepdims=True)
        inner_all = jnp.where(lane == j, inner, inner_all)
    inner_rows = jnp.transpose(inner_all)
    seg_row = segment_row(seg_ref, c, span)
    seg_cols = [segment_column(seg_ref, c ^ b, span) for b in range(cols)]
    low = low_lanes(span)
    for j in range(cols):
        tile = slice(j * TILE, (j + 1) * TILE)
        q_dup = dup_low(qx_ref[:, tile]) * (HD ** -0.5)
        q_mix = mixed(q_dup)
        q_left = jnp.concatenate([q_mix, q_mix], axis=1)
        q_high = high_only(q_dup)
        do_dup = dup_high(d_att[:, tile])
        do_mix = mixed(do_dup)
        do_left = jnp.concatenate([do_mix, do_mix], axis=1)
        do_high = high_only(do_dup)
        lse_row = lse_ref[j:j + 1, :]
        inner_row = inner_rows[j:j + 1, :]
        dq_t = jnp.zeros((TILE, span), f32)
        for b in range(cols):
            keys = slice(b * span, (b + 1) * span)
            kv = kv_ref[keys, tile]
            k_dup = dup_low(kv)
            v_dup = dup_high(kv)
            scores = dot1(right_stack(k_dup), q_left, NT)
            shares = jnp.where(seg_cols[b] == seg_row, jnp.exp(scores - lse_row), 0.0)
            d_shares = dot1(right_stack(v_dup), do_left, NT)
            d_scores = shares * (d_shares - inner_row)
            p_high, p_low = halves(shares)
            s_high, s_low = halves(d_scores)
            dv = dot1(p_high, do_mix) + dot1(p_low, do_high)
            dk = dot1(s_high, q_mix) + dot1(s_low, q_high)
            dkv_ref[keys, tile] = jnp.where(low, dk + swap(dk), dv + swap(dv))
            k_t = jnp.transpose(k_dup)
            k_t_high = k_t.astype(bf16)
            upper = lax.broadcasted_iota(jnp.int32, (TILE, span), 0) < HD
            k_t_mix = jnp.where(upper, k_t_high.astype(f32), k_t - k_t_high.astype(f32)).astype(bf16)
            k_t_only = jnp.where(upper, k_t, 0.0).astype(bf16)
            dq_t = dq_t + dot1(k_t_mix, s_high) + dot1(k_t_only, s_low)
        dq = jnp.transpose(dq_t)
        dqx_ref[:, tile] = jnp.where(low, (dq + swap(dq)) * (HD ** -0.5), 0.0)


def input_gradient(wkv_ref, wqo_ref, dkv_ref, dqx_ref, dv1_ref, keep_out, send_out):
    span = dv1_ref.shape[0]
    wkv = wkv_ref[...]
    for k in (1, 3, 0, 2):
        part = dot(dkv_ref[k * span:(k + 1) * span, :], wkv, NT)
        if k == 0:
            part = part + dot(dqx_ref[...], wqo_ref[...], NT) + dv1_ref[...]
        (send_out if k % 2 else keep_out)[k // 2] = part


def weight_gradients(
    role, cols, h_ref, mid_ref, act_ref, att_ref, dkv_ref, dqx_ref, dbef_ref, dv1_ref, dv2_ref, norm_ref, grad_at
):
    span = dv1_ref.shape[0]

    @pl.when(role == 0)
    def _():
        mid = mid_ref[...]
        for k in range(cols):
            grad_at(k)[...] = dot(mid, dbef_ref[:, k * 2 * TILE:(k + 1) * 2 * TILE], TN)

    @pl.when(role == 1)
    def _():
        for k in range(cols):
            grad_at(k)[...] = dot(dv2_ref[...], act_ref[:, k * 2 * TILE:(k + 1) * 2 * TILE], TN)

    @pl.when(role == 2)
    def _():
        total = dot(h_ref[0], dkv_ref[0:span, :], TN)
        for b in range(1, cols):
            total += dot(h_ref[b], dkv_ref[b * span:(b + 1) * span, :], TN)
        for k in range(cols):
            grad_at(k)[:, 0:TILE] = total[:, k * TILE:(k + 1) * TILE]
            grad_at(k)[:, TILE:] = jnp.zeros((D, TILE), f32)

    @pl.when(role == 3)
    def _():
        total = dot(h_ref[0], dqx_ref[...], TN) + dot(dv1_ref[...], att_ref[...], TN)
        norms = jnp.transpose(norm_ref[...])
        for k in range(cols):
            grad_at(k)[:, 0:TILE] = total[:, k * TILE:(k + 1) * TILE]
            grad_at(k)[:, TILE:] = norms


def top_layer_kernel(rows, cols, idx_ref, ln_ref, seg_ref, *refs):
    c = idx_ref[0]
    packs, refs = refs[:cols], refs[cols:]
    late_refs, h_refs, refs = refs[:rows], refs[rows:rows + cols], refs[rows + cols:]
    (out_ref, h_full, mid_ref, act_ref, att_ref, dkv_ref, dqx_ref, dbef_ref, dv1_ref, dv2_ref, norm_ref,
     keep_out, send_out, wkv_ref, wqo_ref, kv_ref, qx_ref, lse_ref, up_ref, dn_ref, before_ref) = refs
    block = pack_reader(packs)
    place_attention(rows, cols, block, wkv_ref, wqo_ref)
    place_feed(rows, cols, block, HD, up_ref, dn_ref)
    for j in range(cols):
        h_full[j] = h_refs[j][...]
    gains = [ln_ref[k:k + 1, :] for k in range(4, 8)]
    branch, h_own = project_and_attend(
        c, h_full, wkv_ref, wqo_ref, seg_ref, kv_ref, qx_ref, att_ref, lse_ref
    )
    n1, i1 = normalize(h_own + branch)
    mid_ref[...] = n1 * gains[0] + gains[1]
    n2, i2 = feed_forward(mid_ref[...], up_ref, dn_ref, before_ref, act_ref)
    out_ref[...] = n2 * gains[2] + gains[3]
    dh = jnp.transpose(jnp.concatenate([ref[...] for ref in late_refs], axis=0))
    backward(
        c, dh, gains, seg_ref, wqo_ref, kv_ref, qx_ref, att_ref, lse_ref, n1, i1, up_ref, dn_ref,
        before_ref, n2, i2, dkv_ref, dqx_ref, dbef_ref, dv1_ref, dv2_ref, norm_ref
    )
    input_gradient(wkv_ref, wqo_ref, dkv_ref, dqx_ref, dv1_ref, keep_out, send_out)


def add_moment(idx_ref, late_refs, big, at):
    first = 0 if big else HD

    @pl.when(idx_ref[2] == 0)
    def _():
        for r, ref in enumerate(late_refs):
            at[r * HD:(r + 1) * HD, :] += ref[first:first + HD, :]


def top_gradients_kernel(rows, cols, idx_ref, *refs):
    z = idx_ref[1]
    late_refs, refs = refs[:rows], refs[rows:]
    keep_out, send_out = refs[-2:]
    weight_gradients(z, cols, *refs[:-2], lambda k: (send_out if k % 2 else keep_out).at[k // 2])
    for big in (True, False):

        @pl.when((z < 2) == big)
        def _():
            add_moment(idx_ref, late_refs, big, keep_out.at[0])


def low_layer_kernel(rows, cols, idx_ref, ln_ref, seg_ref, *refs):
    late_refs, refs = refs[:rows], refs[rows:]
    z = idx_ref[1]
    (dh_keep, dh_got, dh_across, h_ref, mid_ref, act_ref, wqo_ref, kv_ref, qx_ref, att_ref, lse_ref, n1_ref,
     i1_ref, up_ref, dn_ref, before_ref, n2_ref, i2_ref, keep_out, send_out, dkv_ref, dqx_ref, dv1_ref,
     dbef_ref, dv2_ref, norm_ref) = refs
    dh = dh_keep[0] + dh_got[0] + dh_across[...]
    gains = [ln_ref[k:k + 1, :] for k in range(4)]
    backward(
        idx_ref[0], dh, gains, seg_ref, wqo_ref, kv_ref, qx_ref, att_ref, lse_ref, n1_ref[...],
        i1_ref[:, 0:1], up_ref, dn_ref, before_ref, n2_ref[...], i2_ref[:, 0:1], dkv_ref, dqx_ref, dbef_ref,
        dv1_ref, dv2_ref, norm_ref
    )
    weight_gradients(
        z ^ 2, cols, h_ref, mid_ref, act_ref, att_ref, dkv_ref, dqx_ref, dbef_ref, dv1_ref, dv2_ref, norm_ref,
        lambda k: (send_out if k % 2 else keep_out).at[k // 2]
    )
    for big in (True, False):

        @pl.when((z >= 2) == big)
        def _():
            add_moment(idx_ref, late_refs, big, keep_out.at[0])


def low_input_kernel(*refs):
    input_gradient(*refs)


def symmetric(high, low, dims):
    return dot1(high, high, dims) + (dot1(high, low, dims) + dot1(low, high, dims))


def newton_schulz(blocks):
    sizes = [jnp.sum(x * x, keepdims=True) for x in blocks]
    blocks = [x / (jnp.sqrt(s) + frob_eps) for x, s in zip(blocks, sizes)]
    for _ in range(NS_STEPS):
        parts = [halves(x) for x in blocks]
        grams = [symmetric(h, l, NT) for h, l in parts]
        squares = [symmetric(*halves(a), NN) for a in grams]
        polys = [halves(newton_coefs[1] * a + newton_coefs[2] * s) for a, s in zip(grams, squares)]
        blocks = [
            newton_coefs[0] * x + (dot1(ph, h) + dot1(ph, l) + dot1(pl_, h))
            for x, (h, l), (ph, pl_) in zip(blocks, parts, polys)
        ]
    return blocks


def orthogonal_kernel(cols, idx_ref, *refs):
    z = idx_ref[1]
    top_refs, low_refs = refs[:cols], refs[cols:2 * cols]
    big_out, small_out, big, small = refs[2 * cols:]

    @pl.when(z < 2)
    def _():
        for k in range(cols):
            big[:, k * 2 * TILE:(k + 1) * 2 * TILE] = top_refs[k][...]
            small[:, k * TILE:(k + 1) * TILE] = low_refs[k][:, 0:TILE]

    @pl.when(z >= 2)
    def _():
        for k in range(cols):
            big[:, k * 2 * TILE:(k + 1) * 2 * TILE] = low_refs[k][...]
            small[:, k * TILE:(k + 1) * TILE] = top_refs[k][:, 0:TILE]

    low = low_lanes(D)
    lefts, rights = [], []
    for t in range(cols // 2):
        a = small[:, 2 * t * TILE:(2 * t + 1) * TILE]
        b = small[:, (2 * t + 1) * TILE:(2 * t + 2) * TILE]
        lefts.append(jnp.where(low, a, swap(b)))
        rights.append(jnp.where(low, swap(a), b))
    wide, left, right = newton_schulz(
        [big[...], jnp.concatenate(lefts, axis=1), jnp.concatenate(rights, axis=1)]
    )
    big_out[...] = wide[:, 0:2 * TILE] * math.sqrt(FF)
    small_out[...] = jnp.where(low, left[:, 0:TILE], swap(right[:, 0:TILE])) * math.sqrt(D)


def first_pack_kernel(heads_hbm, outs_hbm, x_hbm, params_hbm, shard_out, heads_ref, outs_ref, params_ref, sems):
    shard_out[2 * HD:, :] = jnp.zeros((8, 2 * TILE), f32)
    copies = [
        pltpu.make_async_copy(source, target, sems.at[i])
        for i, (source, target) in enumerate(
            (
                (heads_hbm.at[0], heads_ref),
                (outs_hbm.at[0], outs_ref),
                (params_hbm, params_ref),
                (x_hbm, shard_out.at[pl.ds(HD, HD)]),
            )
        )
    ]
    for copy in copies:
        copy.start()
    for copy in copies:
        copy.wait()
    shard_out[0:HD, 0:HD] = heads_ref[1]
    shard_out[0:HD, HD:TILE] = heads_ref[2]
    shard_out[0:HD, TILE:TILE + HD] = heads_ref[0]
    shard_out[0:HD, TILE + HD:] = jnp.transpose(outs_ref[...])
    shard_out[2 * HD:, 0:HD] = params_ref[...]


def pack_kernel(
    rows, idx_ref, heads_ref, outs_ref, up_ref, dn_ref, mh_ref, mo_ref, mu_ref, md_ref, f_out, b_out, *refs
):
    z = idx_ref[1]
    late_outs, moments = refs[:rows], refs[rows]
    f_out[0:HD, :] = up_ref[0]
    f_out[HD:, :] = dn_ref[0]
    b_out[0:HD, 0:HD] = heads_ref[1, 1]
    b_out[0:HD, HD:TILE] = heads_ref[1, 2]
    b_out[0:HD, TILE:TILE + HD] = heads_ref[1, 0]
    b_out[0:HD, TILE + HD:] = jnp.transpose(outs_ref[1])
    b_out[HD:2 * HD, :] = up_ref[1]
    b_out[2 * HD:, :] = dn_ref[1]
    for l in range(LAYERS):
        large, small = (0, 2) if l else (2, 0)
        moments[large, 0:HD, :] = mu_ref[l] * muon_decay
        moments[large + 1, 0:HD, :] = md_ref[l] * muon_decay
        moments[small, HD:, 0:HD] = mh_ref[l, 1] * muon_decay
        moments[small, HD:, HD:TILE] = mh_ref[l, 2] * muon_decay
        moments[small + 1, HD:, 0:HD] = mh_ref[l, 0] * muon_decay
        moments[small + 1, HD:, HD:TILE] = jnp.transpose(mo_ref[l]) * muon_decay
    for r in range(rows):
        moments[r, HD:, TILE:] = jnp.zeros((HD, TILE), f32)
    for k in range(rows):
        late_outs[k][...] = moments[z ^ k]


def update_kernel(
    rows, idx_ref, heads_ref, outs_ref, up_ref, dn_ref, params_ref, first_ref, second_ref, *refs
):
    z = idx_ref[1]
    mom_refs, step_refs, refs = refs[:rows], refs[rows:2 * rows], refs[2 * rows:]
    (heads_out, outs_out, up_out, dn_out, mh_out, mo_out, mu_out, md_out, first_out, second_out, params_out,
     mom, step) = refs
    for k in range(rows):
        mom[z ^ k] = mom_refs[k][...]
        step[z ^ k] = step_refs[k][...] * muon_rate
    for l in range(LAYERS):
        large, small = (0, 2) if l else (2, 0)
        mu_out[l] = mom[large, 0:HD, :]
        md_out[l] = mom[large + 1, 0:HD, :]
        up_out[l] = up_ref[l] - D ** -0.5 * step[large, :, 0:2 * TILE]
        dn_out[l] = dn_ref[l] - FF ** -0.5 * step[large + 1, :, 0:2 * TILE]
        kv, qo = mom[small, HD:, 0:TILE], mom[small + 1, HD:, 0:TILE]
        mh_out[l, 0] = qo[:, 0:HD]
        mh_out[l, 1] = kv[:, 0:HD]
        mh_out[l, 2] = swap(kv)[:, 0:HD]
        mo_out[l] = jnp.transpose(swap(qo))[0:HD, :]
        kv, qo = step[small, :, 2 * TILE:], step[small + 1, :, 2 * TILE:]
        heads_out[l, 0] = heads_ref[l, 0] - D ** -0.5 * qo[:, 0:HD]
        heads_out[l, 1] = heads_ref[l, 1] - D ** -0.5 * kv[:, 0:HD]
        heads_out[l, 2] = heads_ref[l, 2] - D ** -0.5 * swap(kv)[:, 0:HD]
        outs_out[l] = outs_ref[l] - (D // 16) ** -0.5 * jnp.transpose(swap(qo))[0:HD, :]
        grad = jnp.transpose(mom[small + 1, HD:, TILE:])[0:4, :]
        first = adam_first * first_ref[l] + (1.0 - adam_first) * grad
        second = adam_second * second_ref[l] + (1.0 - adam_second) * grad * grad
        first_out[l] = first
        second_out[l] = second
        params_out[l] = params_ref[l] - adam_rate * (first / (1.0 - adam_first**STEP)) / (
            jnp.sqrt(second / (1.0 - adam_second**STEP)) + adam_eps
        )


def call(body, operands, outs, scratch=(), flops=0, vmem=50):
    specs = [pl.BlockSpec(memory_space=pltpu.SMEM if x.ndim == 1 else pltpu.VMEM) for x in operands]
    moved = sum(4 * math.prod(x.shape) for x in operands) + sum(4 * math.prod(s) for s in outs)
    return pl.pallas_call(
        body,
        out_shape=[jax.ShapeDtypeStruct(s, f32) for s in outs],
        in_specs=specs,
        out_specs=[pl.BlockSpec(memory_space=pltpu.VMEM) for _ in outs],
        scratch_shapes=[pltpu.VMEM(s, f32) for s in scratch],
        compiler_params=pltpu.CompilerParams(vmem_limit_bytes=vmem * 2**20),
        cost_estimate=pl.CostEstimate(flops=flops, bytes_accessed=moved if flops else 0, transcendentals=0),
    )(*operands)


def fetched_call(body, idx, operands, outs, scratch):
    count, given = len(operands), len(outs) + len(scratch)

    def kernel(idx_ref, *refs):
        sources, rest, held, sems = refs[:count], refs[count:count + given], refs[count + given:-1], refs[-1]
        copies = [pltpu.make_async_copy(a, b, sems.at[i]) for i, (a, b) in enumerate(zip(sources, held))]
        for copy in copies:
            copy.start()
        for copy in copies:
            copy.wait()
        body(idx_ref, *held, *rest)

    return pl.pallas_call(
        kernel,
        out_shape=[jax.ShapeDtypeStruct(s, f32) for s in outs],
        in_specs=[pl.BlockSpec(memory_space=pltpu.SMEM)] + [pl.BlockSpec(memory_space=pltpu.HBM)] * count,
        out_specs=[pl.BlockSpec(memory_space=pltpu.VMEM) for _ in outs],
        scratch_shapes=[pltpu.VMEM(s, f32) for s in scratch]
        + [pltpu.VMEM(x.shape, f32) for x in operands] + [pltpu.SemaphoreType.DMA((count,))],
        compiler_params=pltpu.CompilerParams(vmem_limit_bytes=56 * 2**20),
    )(idx, *operands)


def on_device(
    layer_input,
    segment_ids,
    head_projection_weights,
    output_projection_weights,
    up_projection_weights,
    down_projection_weights,
    head_moment,
    out_moment,
    up_moment,
    down_moment,
    norm_params,
    norm_first,
    norm_second,
    output_grad,
):
    row = lax.axis_index("row").astype(jnp.int32)
    col = lax.axis_index("col").astype(jnp.int32)
    rows = lax.axis_size("row")
    cols = lax.axis_size("col")
    dps = lax.axis_size("dp")
    span = layer_input.shape[1]
    length = span * cols
    idx = jnp.stack([col, row, lax.axis_index("dp").astype(jnp.int32)])
    swap2 = lambda x: jnp.swapaxes(x, -1, -2)

    def perm(x, axis, bit):
        return lax.ppermute(x, axis, [(i, i ^ bit) for i in range(lax.axis_size(axis))])

    def spread_cols(x):
        across = perm(x, "col", 2)
        return [x, perm(x, "col", 1), across, perm(across, "col", 1)]

    def spread_rows(parts):
        return [parts[0]] + [perm(parts[k], "row", k) for k in range(1, rows)]

    heads, outs, ups = head_projection_weights, output_projection_weights, up_projection_weights
    downs = swap2(down_projection_weights)
    shard_a = pl.pallas_call(
        first_pack_kernel,
        out_shape=jax.ShapeDtypeStruct((2 * HD + 8, D), f32),
        in_specs=[pl.BlockSpec(memory_space=pltpu.HBM)] * 4,
        out_specs=pl.BlockSpec(memory_space=pltpu.VMEM),
        scratch_shapes=[
            pltpu.VMEM((3, HD, HD), f32), pltpu.VMEM((HD, HD), f32), pltpu.VMEM((8, HD), f32), pltpu.SemaphoreType.DMA((4,)),
        ],
        compiler_params=pltpu.CompilerParams(vmem_limit_bytes=60 * 2**20),
    )(heads, outs, swap2(layer_input[0]), norm_params.reshape(8, HD))
    og = swap2(output_grad[0])
    shard_f, shard_b, *moments = fetched_call(
        functools.partial(pack_kernel, rows),
        idx, [heads, outs, ups, downs, head_moment, out_moment, up_moment, swap2(down_moment)],
        [(2 * HD, D), (3 * HD, D)] + [(2 * HD, D)] * rows, [(rows, 2 * HD, D)],
    )
    pieces = spread_rows([shard_a] * rows)
    *pieces, shard_f = lax.optimization_barrier((*pieces, shard_f))
    mine_a = jnp.stack(pieces)
    across_a, core_a = perm(mine_a, "col", 2), perm(mine_a, "col", 1)
    shard_f, _ = lax.optimization_barrier((shard_f, core_a))
    pieces_f = spread_rows([shard_f] * rows)
    mine_f = jnp.stack(pieces_f)
    across_a, mine_f = lax.optimization_barrier((across_a, mine_f))
    packs_a = [mine_a, core_a, across_a, perm(across_a, "col", 1)]
    across_f = perm(mine_f, "col", 2)
    shard_b, _ = lax.optimization_barrier((shard_b, pieces_f[1]))
    pieces_b = spread_rows([shard_b] * rows)

    full = (cols, span, D)
    pair = (2, span, D)
    own = (span, D)
    wide = (span, FF)
    half = (D, cols * TILE)
    keys = (length, cols * TILE)
    queries = (span, cols * TILE)
    one = (span, TILE)
    stats = (8, span)
    norms = (TILE, D)
    segs = [segment_ids]

    h_full, wkv, wqo, kv, qx, att, lse, mid, n1, i1, ln = call(
        functools.partial(attention_kernel, rows, cols),
        [idx] + segs + packs_a,
        [full, half, half, keys, queries, queries, stats, own, own, one, (8, D)], flops=5 * 10**9, vmem=12,
    )
    mid, across_f, og, *rest = lax.optimization_barrier((mid, across_f, og, *moments, *pieces_b))
    moments, pieces_b = rest[:rows], rest[rows:]
    packs_f = [mine_f, perm(mine_f, "col", 1), across_f, perm(across_f, "col", 1)]
    og = spread_rows([og] * rows)
    moments = spread_rows(moments)
    h_own, up, dn, before, act, n2, i2 = call(
        functools.partial(feed_kernel, rows, cols),
        [mid, ln] + packs_f,
        [own, (D, FF), (D, FF), wide, wide, own, one], flops=2 * 10**9, vmem=8,
    )
    h_own, *og = lax.optimization_barrier((h_own, *og))
    hidden = spread_cols(h_own)
    mine_b = jnp.stack(pieces_b)
    across_b = perm(mine_b, "col", 2)
    across_b, hidden[2] = lax.optimization_barrier((across_b, hidden[2]))
    packs_b = [mine_b, perm(mine_b, "col", 1), across_b, perm(across_b, "col", 1)]
    top, *saved, keep, send = call(
        functools.partial(top_layer_kernel, rows, cols),
        [idx, ln] + segs + packs_b + og + hidden,
        [own, full, own, wide, queries, keys, queries, wide, own, own, norms, pair, pair],
        [half, half, keys, queries, stats, (D, FF), (D, FF), wide], flops=20 * 10**9, vmem=18,
    )
    layer_output = top[:, :HD][None]

    def fold_core(keep, send):
        got = perm(send, "col", 1)
        return got, perm(keep[1] + got[1], "col", 2)

    got, across = fold_core(keep, send)
    keep_t, send_t = call(
        functools.partial(top_gradients_kernel, rows, cols), [idx] + moments + saved, [pair, pair],
        flops=2 * 10**9, vmem=6,
    )
    got_t = perm(send_t, "col", 1)
    half_t = keep_t[1] + got_t[1]
    got, half_t = lax.optimization_barrier((got, half_t))
    across_t = perm(half_t, "col", 2)
    keep_g, send_g, dkv, dqx, dv1 = call(
        functools.partial(low_layer_kernel, rows, cols),
        [idx, ln] + segs + moments
        + [keep, got, across, h_full, mid, act, wqo, kv, qx, att, lse, n1, i1, up, dn, before, n2, i2],
        [pair, pair, keys, queries, own], [wide, own, norms], flops=12 * 10**9, vmem=12,
    )
    got, across = fold_core(keep_g, send_g)
    mine = keep_g[0] + got[0] + across
    top = keep_t[0] + got_t[0] + across_t
    top, mine = [
        lax.optimization_barrier(x + perm(x, "dp", 1) if dps == 2 else lax.psum(x, "dp")) for x in (top, mine)
    ]
    keep, send = call(
        low_input_kernel, [wkv, wqo, dkv, dqx, dv1], [pair, pair], flops=2 * 10**9, vmem=6,
    )
    got, across = fold_core(keep, send)
    input_grad = (keep[0] + got[0] + across)[:, :HD][None]

    tops, parts = spread_cols(top), spread_cols(mine)
    large, small = jnp.where(row < 2, top, mine), jnp.where(row < 2, mine, top)
    moms = jnp.concatenate([large.reshape(rows, HD, D), small.reshape(rows, HD, D)], axis=1)
    moms = spread_rows([moms[k] for k in range(rows)])
    large, small = call(
        functools.partial(orthogonal_kernel, cols), [idx] + tops + parts, [own, (D, TILE)],
        [(D, FF), (D, cols * TILE)], flops=8 * 10**9, vmem=16,
    )
    steps = jnp.concatenate([large.reshape(rows, HD, D), small.reshape(rows, HD, TILE)], axis=2)
    steps = spread_rows([steps[k] for k in range(rows)])
    three = (LAYERS, 4, HD)
    updates = list(call(
        functools.partial(update_kernel, rows),
        [idx, heads, outs, ups, downs, norm_params, norm_first, norm_second] + moms + steps,
        [heads.shape, outs.shape, ups.shape, downs.shape] * 2 + [three] * 3,
        [(rows, 2 * HD, D), (rows, HD, D + TILE)], vmem=8,
    ))
    for at in (3, 7):
        updates[at] = swap2(updates[at])
    return (layer_output, input_grad, *updates)


def solution(mesh):
    placed = (
        P("dp", "col", "row"),
        P("dp", None),
        P(None, None, "row", "col"),
        P(None, "col", "row"),
        P(None, "row", "col"),
        P(None, "col", "row"),
        P(None, None, "row", "col"),
        P(None, "col", "row"),
        P(None, "row", "col"),
        P(None, "col", "row"),
        P(None, None, "row"),
        P(None, None, "row"),
        P(None, None, "row"),
        P("dp", "col", "row"),
    )
    return jax.shard_map(
        on_device,
        mesh=mesh,
        in_specs=placed,
        out_specs=(
            P("dp", "col", "row"),
            P("dp", "col", "row"),
            P(None, None, "row", "col"),
            P(None, "col", "row"),
            P(None, "row", "col"),
            P(None, "col", "row"),
            P(None, None, "row", "col"),
            P(None, "col", "row"),
            P(None, "row", "col"),
            P(None, "col", "row"),
            P(None, None, "row"),
            P(None, None, "row"),
            P(None, None, "row"),
        ),
        check_vma=False,
    )
```

```python
import functools
import math

import jax
import jax.numpy as jnp
from jax import lax
from jax.experimental import pallas as pl
from jax.experimental.pallas import tpu as pltpu
from jax.sharding import PartitionSpec as P

D = 256
FF = 1024
LAYERS = 2
NS_STEPS = 5
STEP = 10
HD = 64
TILE = 128

norm_eps = 1e-05
newton_coefs = (3.4445, -4.775, 2.0315)
frob_eps = 1e-07
muon_decay = 0.95
muon_rate = 0.5
adam_first = 0.9
adam_second = 0.999
adam_eps = 1e-08
adam_rate = 0.2
masked_score = -1e30

f32 = jnp.float32
bf16 = jnp.bfloat16

NN = (((1,), (0,)), ((), ()))
NT = (((1,), (1,)), ((), ()))
TN = (((0,), (0,)), ((), ()))


def dot(a, b, dims=NN):
    return lax.dot_general(a, b, dims, precision=lax.Precision.HIGH, preferred_element_type=f32)


def dot1(a, b, dims=NN):
    return lax.dot_general(a, b, dims, preferred_element_type=f32)


def low_lanes(rows):
    return lax.broadcasted_iota(jnp.int32, (rows, TILE), 1) < HD


def swap(t):
    return pltpu.roll(t, HD, 1)


def dup_low(t):
    return jnp.where(low_lanes(t.shape[0]), t, swap(t))


def dup_high(t):
    return jnp.where(low_lanes(t.shape[0]), swap(t), t)


def halves(t):
    high = t.astype(bf16)
    return high, (t - high.astype(f32)).astype(bf16)


def mixed(t):
    high = t.astype(bf16).astype(f32)
    return jnp.where(low_lanes(t.shape[0]), high, t - high).astype(bf16)


def high_only(t):
    return jnp.where(low_lanes(t.shape[0]), t, 0.0).astype(bf16)


def left_stack(t):
    m = mixed(t)
    return jnp.concatenate([m, m], axis=1)


def right_stack(t):
    high, low = halves(t)
    return jnp.concatenate([high, low], axis=1)


def normalize(values):
    mean = jnp.sum(values, axis=-1, keepdims=True) * (1.0 / D)
    center = values - mean
    variance = jnp.sum(center * center, axis=-1, keepdims=True) * (1.0 / D)
    inverse = lax.rsqrt(variance + norm_eps)
    return center * inverse, inverse


def normalize_back(grad_out, normed, inverse, gain):
    scaled = grad_out * gain
    first = jnp.sum(scaled, axis=-1, keepdims=True) * (1.0 / D)
    second = jnp.sum(scaled * normed, axis=-1, keepdims=True) * (1.0 / D)
    grad_in = inverse * (scaled - first - normed * second)
    gain_grad = jnp.sum(grad_out * normed, axis=0, keepdims=True)
    shift_grad = jnp.sum(grad_out, axis=0, keepdims=True)
    return grad_in, gain_grad, shift_grad


def pack_reader(refs):
    return lambda r, k, lo, hi: refs[k][r, lo:hi, :]


def segment_row(seg_ref, chunk, span):
    return seg_ref[:, pl.ds(pl.multiple_of(chunk * span, span), span)].astype(f32)


def segment_column(seg_ref, chunk, span):
    return jnp.transpose(jnp.broadcast_to(segment_row(seg_ref, chunk, span), (TILE, span)))[:, 0:1]


def project_and_attend(c, h, wkv_ref, wqo_ref, seg_ref, kv_ref, qx_ref, att_ref, lse_ref):
    cols = h.shape[0]
    span = h.shape[1]
    wkv = wkv_ref[...]
    for j in range(cols):
        kv_ref[j * span:(j + 1) * span, :] = dot(h[j], wkv)
    h_own = h[0]
    qx_ref[...] = dot(h_own, wqo_ref[...])
    lane = lax.broadcasted_iota(jnp.int32, (span, TILE), 1)
    seg_row = jnp.concatenate([segment_row(seg_ref, c ^ k, span) for k in range(cols)], axis=1)
    allowed = segment_column(seg_ref, c, span) == seg_row
    lse_all = jnp.zeros((span, TILE), f32)
    for j in range(cols):
        tile = slice(j * TILE, (j + 1) * TILE)
        kv = kv_ref[:, tile]
        k_right = right_stack(dup_low(kv))
        v_dup = dup_high(kv)
        v_mix = mixed(v_dup)
        v_high = high_only(v_dup)
        q_left = left_stack(dup_low(qx_ref[:, tile]) * (HD ** -0.5))
        scores = jnp.where(allowed, dot1(q_left, k_right, NT), masked_score)
        top = jnp.max(scores, axis=-1, keepdims=True)
        raised = jnp.exp(scores - top)
        total = jnp.sum(raised, axis=-1, keepdims=True)
        p_high, p_low = halves(raised)
        out = dot1(p_high, v_mix) + dot1(p_low, v_high)
        out = (out + swap(out)) / total
        att_ref[:, tile] = jnp.where(low_lanes(span), 0.0, out)
        lse_all = jnp.where(lane == j, top + jnp.log(total), lse_all)
    lse_ref[...] = jnp.transpose(lse_all)[0:8, :]
    return dot(att_ref[...], wqo_ref[...], NT), h_own


def place_attention(rows, cols, block, at, wkv_ref, wqo_ref):
    for j in range(cols):
        for r in range(rows):
            piece = block(r, j, at, at + HD)
            wkv_ref[r * HD:(r + 1) * HD, j * TILE:(j + 1) * TILE] = piece[:, :TILE]
            wqo_ref[r * HD:(r + 1) * HD, j * TILE:(j + 1) * TILE] = piece[:, TILE:]


def place_feed(rows, cols, block, at, up_ref, dn_ref):
    for j in range(cols):
        for r in range(rows):
            to = (slice(r * HD, (r + 1) * HD), slice(j * 2 * TILE, (j + 1) * 2 * TILE))
            up_ref[to] = block(r, j, at, at + HD)
            dn_ref[to] = block(r, j, at + HD, at + 2 * HD)


def feed_forward(mid, up_ref, dn_ref, before_ref, act_ref):
    before = dot(mid, up_ref[...])
    before_ref[...] = before
    activated = 0.5 * before * (1.0 + lax.erf(before * 0.7071067811865476))
    act_ref[...] = activated
    return normalize(mid + dot(activated, dn_ref[...], NT))


def attention_kernel(rows, cols, idx_ref, seg_ref, *refs):
    c = idx_ref[0]
    packs, refs = refs[:cols], refs[cols:]
    h_out, wkv_out, wqo_out, kv_out, qx_out, att_out, lse_out, mid_out, n1_out, i1_out, params_out = refs
    block = pack_reader(packs)
    span = mid_out.shape[0]
    place_attention(rows, cols, block, 0, wkv_out, wqo_out)
    for j in range(cols):
        h_out[j] = jnp.transpose(
            jnp.concatenate([block(r, j, HD, 2 * HD) for r in range(rows)], axis=0)
        )
    tiles = []
    for t in range(rows // 2):
        a = block(2 * t, 0, 2 * HD, 2 * HD + 8)[:, 0:TILE]
        b = block(2 * t + 1, 0, 2 * HD, 2 * HD + 8)[:, 0:TILE]
        tiles.append(jnp.where(low_lanes(8), a, swap(b)))
    params_out[...] = jnp.concatenate(tiles, axis=1)
    branch, h_own = project_and_attend(
        c, h_out, wkv_out, wqo_out, seg_ref, kv_out, qx_out, att_out, lse_out
    )
    normed, inverse = normalize(h_own + branch)
    n1_out[...] = normed
    i1_out[...] = jnp.broadcast_to(inverse, (span, TILE))
    mid_out[...] = normed * params_out[0:1, :] + params_out[1:2, :]


def feed_kernel(rows, cols, mid_ref, ln_ref, *refs):
    packs, refs = refs[:cols], refs[cols:]
    h_out, up_out, dn_out, before_out, act_out, n2_out, i2_out = refs
    block = pack_reader(packs)
    place_feed(rows, cols, block, 0, up_out, dn_out)
    normed, inverse = feed_forward(mid_ref[...], up_out, dn_out, before_out, act_out)
    n2_out[...] = normed
    i2_out[...] = jnp.broadcast_to(inverse, i2_out.shape)
    h_out[...] = normed * ln_ref[2:3, :] + ln_ref[3:4, :]


def backward(
    c, dh, gains, seg_ref, wqo_ref, kv_ref, qx_ref, att_ref, lse_ref, n1, i1, up_ref, dn_ref,
    before_ref, n2, i2, dkv_ref, dqx_ref, dbef_ref, dv1_ref, dv2_ref, norm_ref
):
    span = n1.shape[0]
    cols = seg_ref.shape[1] // span
    dv2, gain2, shift2 = normalize_back(dh, n2, i2, gains[2])
    dv2_ref[...] = dv2
    d_act = dot(dv2, dn_ref[...])
    before = before_ref[...]
    slope = (
        0.5 * (1.0 + lax.erf(before * 0.7071067811865476))
        + before * jnp.exp(-0.5 * before * before) * 0.3989422804014327
    )
    dbef_ref[...] = d_act * slope
    d_mid = dv2 + dot(dbef_ref[...], up_ref[...], NT)
    dv1, gain1, shift1 = normalize_back(d_mid, n1, i1, gains[0])
    dv1_ref[...] = dv1
    norm_ref[...] = jnp.zeros_like(norm_ref)
    for k, row in enumerate((gain1, shift1, gain2, shift2)):
        norm_ref[k:k + 1, :] = row
    d_att = dot(dv1, wqo_ref[...])
    lane = lax.broadcasted_iota(jnp.int32, (span, TILE), 1)
    inner_all = jnp.zeros((span, TILE), f32)
    for j in range(cols):
        tile = slice(j * TILE, (j + 1) * TILE)
        inner = jnp.sum(d_att[:, tile] * att_ref[:, tile], axis=-1, keepdims=True)
        inner_all = jnp.where(lane == j, inner, inner_all)
    inner_rows = jnp.transpose(inner_all)
    seg_row = segment_row(seg_ref, c, span)
    seg_cols = [segment_column(seg_ref, c ^ b, span) for b in range(cols)]
    low = low_lanes(span)
    for j in range(cols):
        tile = slice(j * TILE, (j + 1) * TILE)
        q_dup = dup_low(qx_ref[:, tile]) * (HD ** -0.5)
        q_mix = mixed(q_dup)
        q_left = jnp.concatenate([q_mix, q_mix], axis=1)
        q_high = high_only(q_dup)
        do_dup = dup_high(d_att[:, tile])
        do_mix = mixed(do_dup)
        do_left = jnp.concatenate([do_mix, do_mix], axis=1)
        do_high = high_only(do_dup)
        lse_row = lse_ref[j:j + 1, :]
        inner_row = inner_rows[j:j + 1, :]
        dq_t = jnp.zeros((TILE, span), f32)
        for b in range(cols):
            keys = slice(b * span, (b + 1) * span)
            kv = kv_ref[keys, tile]
            k_dup = dup_low(kv)
            v_dup = dup_high(kv)
            scores = dot1(right_stack(k_dup), q_left, NT)
            shares = jnp.where(seg_cols[b] == seg_row, jnp.exp(scores - lse_row), 0.0)
            d_shares = dot1(right_stack(v_dup), do_left, NT)
            d_scores = shares * (d_shares - inner_row)
            p_high, p_low = halves(shares)
            s_high, s_low = halves(d_scores)
            dv = dot1(p_high, do_mix) + dot1(p_low, do_high)
            dk = dot1(s_high, q_mix) + dot1(s_low, q_high)
            dkv_ref[keys, tile] = jnp.where(low, dk + swap(dk), dv + swap(dv))
            k_t = jnp.transpose(k_dup)
            k_t_high = k_t.astype(bf16)
            upper = lax.broadcasted_iota(jnp.int32, (TILE, span), 0) < HD
            k_t_mix = jnp.where(upper, k_t_high.astype(f32), k_t - k_t_high.astype(f32)).astype(bf16)
            k_t_only = jnp.where(upper, k_t, 0.0).astype(bf16)
            dq_t = dq_t + dot1(k_t_mix, s_high) + dot1(k_t_only, s_low)
        dq = jnp.transpose(dq_t)
        dqx_ref[:, tile] = jnp.where(low, (dq + swap(dq)) * (HD ** -0.5), 0.0)


def input_gradient(wkv_ref, wqo_ref, dkv_ref, dqx_ref, dv1_ref, keep_out, send_out):
    span = dv1_ref.shape[0]
    wkv = wkv_ref[...]
    for k in (1, 3, 0, 2):
        part = dot(dkv_ref[k * span:(k + 1) * span, :], wkv, NT)
        if k == 0:
            part = part + dot(dqx_ref[...], wqo_ref[...], NT) + dv1_ref[...]
        (send_out if k % 2 else keep_out)[k // 2] = part


def weight_gradients(
    role, cols, h_ref, mid_ref, act_ref, att_ref, dkv_ref, dqx_ref, dbef_ref, dv1_ref, dv2_ref, norm_ref, grad_at
):
    span = dv1_ref.shape[0]

    @pl.when(role == 0)
    def _():
        mid = mid_ref[...]
        for k in range(cols):
            grad_at(k)[...] = dot(mid, dbef_ref[:, k * 2 * TILE:(k + 1) * 2 * TILE], TN)

    @pl.when(role == 1)
    def _():
        for k in range(cols):
            grad_at(k)[...] = dot(dv2_ref[...], act_ref[:, k * 2 * TILE:(k + 1) * 2 * TILE], TN)

    @pl.when(role == 2)
    def _():
        total = dot(h_ref[0], dkv_ref[0:span, :], TN)
        for b in range(1, cols):
            total += dot(h_ref[b], dkv_ref[b * span:(b + 1) * span, :], TN)
        for k in range(cols):
            grad_at(k)[:, 0:TILE] = total[:, k * TILE:(k + 1) * TILE]
            grad_at(k)[:, TILE:] = jnp.zeros((D, TILE), f32)

    @pl.when(role == 3)
    def _():
        total = dot(h_ref[0], dqx_ref[...], TN) + dot(dv1_ref[...], att_ref[...], TN)
        norms = jnp.transpose(norm_ref[...])
        for k in range(cols):
            grad_at(k)[:, 0:TILE] = total[:, k * TILE:(k + 1) * TILE]
            grad_at(k)[:, TILE:] = norms


def top_layer_kernel(rows, cols, idx_ref, ln_ref, seg_ref, *refs):
    c = idx_ref[0]
    packs, wide_packs, refs = refs[:cols], refs[cols:2 * cols], refs[2 * cols:]
    late_refs, h_refs, refs = refs[:rows], refs[rows:rows + cols], refs[rows + cols:]
    (out_ref, h_full, mid_ref, act_ref, att_ref, dkv_ref, dqx_ref, dbef_ref, dv1_ref, dv2_ref, norm_ref,
     keep_out, send_out, wkv_ref, wqo_ref, kv_ref, qx_ref, lse_ref, up_ref, dn_ref, before_ref) = refs
    place_attention(rows, cols, pack_reader(packs), 2 * HD, wkv_ref, wqo_ref)
    place_feed(rows, cols, pack_reader(wide_packs), 0, up_ref, dn_ref)
    for j in range(cols):
        h_full[j] = h_refs[j][...]
    gains = [ln_ref[k:k + 1, :] for k in range(4, 8)]
    branch, h_own = project_and_attend(
        c, h_full, wkv_ref, wqo_ref, seg_ref, kv_ref, qx_ref, att_ref, lse_ref
    )
    n1, i1 = normalize(h_own + branch)
    mid_ref[...] = n1 * gains[0] + gains[1]
    n2, i2 = feed_forward(mid_ref[...], up_ref, dn_ref, before_ref, act_ref)
    out_ref[...] = n2 * gains[2] + gains[3]
    dh = jnp.transpose(jnp.concatenate([ref[...] for ref in late_refs], axis=0))
    backward(
        c, dh, gains, seg_ref, wqo_ref, kv_ref, qx_ref, att_ref, lse_ref, n1, i1, up_ref, dn_ref,
        before_ref, n2, i2, dkv_ref, dqx_ref, dbef_ref, dv1_ref, dv2_ref, norm_ref
    )
    input_gradient(wkv_ref, wqo_ref, dkv_ref, dqx_ref, dv1_ref, keep_out, send_out)


def add_moment(idx_ref, late_refs, big, at):
    first = 0 if big else HD

    @pl.when(idx_ref[2] == 0)
    def _():
        for r, ref in enumerate(late_refs):
            at[r * HD:(r + 1) * HD, :] += ref[first:first + HD, :]


def top_gradients_kernel(rows, cols, idx_ref, *refs):
    z = idx_ref[1]
    late_refs, refs = refs[:rows], refs[rows:]
    keep_out, send_out = refs[-2:]
    weight_gradients(z, cols, *refs[:-2], lambda k: (send_out if k % 2 else keep_out).at[k // 2])
    for big in (True, False):

        @pl.when((z < 2) == big)
        def _():
            add_moment(idx_ref, late_refs, big, keep_out.at[0])


def low_layer_kernel(rows, cols, idx_ref, ln_ref, seg_ref, *refs):
    late_refs, refs = refs[:rows], refs[rows:]
    z = idx_ref[1]
    (dh_keep, dh_got, dh_across, h_ref, mid_ref, act_ref, wqo_ref, kv_ref, qx_ref, att_ref, lse_ref, n1_ref,
     i1_ref, up_ref, dn_ref, before_ref, n2_ref, i2_ref, keep_out, send_out, dkv_ref, dqx_ref, dv1_ref,
     dbef_ref, dv2_ref, norm_ref) = refs
    dh = dh_keep[0] + dh_got[0] + dh_across[...]
    gains = [ln_ref[k:k + 1, :] for k in range(4)]
    backward(
        idx_ref[0], dh, gains, seg_ref, wqo_ref, kv_ref, qx_ref, att_ref, lse_ref, n1_ref[...],
        i1_ref[:, 0:1], up_ref, dn_ref, before_ref, n2_ref[...], i2_ref[:, 0:1], dkv_ref, dqx_ref, dbef_ref,
        dv1_ref, dv2_ref, norm_ref
    )
    weight_gradients(
        z ^ 2, cols, h_ref, mid_ref, act_ref, att_ref, dkv_ref, dqx_ref, dbef_ref, dv1_ref, dv2_ref, norm_ref,
        lambda k: (send_out if k % 2 else keep_out).at[k // 2]
    )
    for big in (True, False):

        @pl.when((z >= 2) == big)
        def _():
            add_moment(idx_ref, late_refs, big, keep_out.at[0])


def low_input_kernel(*refs):
    input_gradient(*refs)


def symmetric(high, low, dims):
    return dot1(high, high, dims) + (dot1(high, low, dims) + dot1(low, high, dims))


def newton_schulz(blocks, wanted):
    sizes = [jnp.sum(x * x, keepdims=True) for x in blocks]
    blocks = [x / (jnp.sqrt(s) + frob_eps) for x, s in zip(blocks, sizes)]
    for step in range(NS_STEPS):
        parts = [halves(x) for x in blocks]
        grams = [symmetric(h, l, NT) for h, l in parts]
        squares = [symmetric(*halves(a), NN) for a in grams]
        polys = [halves(newton_coefs[1] * a + newton_coefs[2] * s) for a, s in zip(grams, squares)]
        if step == NS_STEPS - 1:
            blocks = [x[:, :n] for x, n in zip(blocks, wanted)]
            parts = [(h[:, :n], l[:, :n]) for (h, l), n in zip(parts, wanted)]
        blocks = [
            newton_coefs[0] * x + (dot1(ph, h) + dot1(ph, l) + dot1(pl_, h))
            for x, (h, l), (ph, pl_) in zip(blocks, parts, polys)
        ]
    return blocks


def orthogonal_kernel(cols, idx_ref, *refs):
    z = idx_ref[1]
    top_refs, low_refs = refs[:cols], refs[cols:2 * cols]
    big_out, small_out, big, small = refs[2 * cols:]

    @pl.when(z < 2)
    def _():
        for k in range(cols):
            big[:, k * 2 * TILE:(k + 1) * 2 * TILE] = top_refs[k][...]
            small[:, k * TILE:(k + 1) * TILE] = low_refs[k][:, 0:TILE]

    @pl.when(z >= 2)
    def _():
        for k in range(cols):
            big[:, k * 2 * TILE:(k + 1) * 2 * TILE] = low_refs[k][...]
            small[:, k * TILE:(k + 1) * TILE] = top_refs[k][:, 0:TILE]

    low = low_lanes(D)
    lefts, rights = [], []
    for t in range(cols // 2):
        a = small[:, 2 * t * TILE:(2 * t + 1) * TILE]
        b = small[:, (2 * t + 1) * TILE:(2 * t + 2) * TILE]
        lefts.append(jnp.where(low, a, swap(b)))
        rights.append(jnp.where(low, swap(a), b))
    wide, left, right = newton_schulz(
        [big[...], jnp.concatenate(lefts, axis=1), jnp.concatenate(rights, axis=1)], (2 * TILE, TILE, TILE)
    )
    big_out[...] = wide * math.sqrt(FF)
    small_out[...] = jnp.where(low, left, swap(right)) * math.sqrt(D)


def first_pack_kernel(heads_hbm, outs_hbm, x_hbm, params_hbm, shard_out, heads_ref, outs_ref, params_ref, sems):
    shard_out[2 * HD:, :] = jnp.zeros((8, 2 * TILE), f32)
    copies = [
        pltpu.make_async_copy(source, target, sems.at[i])
        for i, (source, target) in enumerate(
            (
                (heads_hbm.at[0], heads_ref),
                (outs_hbm.at[0], outs_ref),
                (params_hbm, params_ref),
                (x_hbm, shard_out.at[pl.ds(HD, HD)]),
            )
        )
    ]
    for copy in copies:
        copy.start()
    for copy in copies:
        copy.wait()
    shard_out[0:HD, 0:HD] = heads_ref[1]
    shard_out[0:HD, HD:TILE] = heads_ref[2]
    shard_out[0:HD, TILE:TILE + HD] = heads_ref[0]
    shard_out[0:HD, TILE + HD:] = jnp.transpose(outs_ref[...])
    shard_out[2 * HD:, 0:HD] = params_ref[...]


def pack_kernel(
    rows, idx_ref, heads_ref, outs_ref, up_ref, dn_ref, mh_ref, mo_ref, mu_ref, md_ref, f_out, b_out, *refs
):
    z = idx_ref[1]
    late_outs, moments = refs[:rows], refs[rows]
    f_out[0:HD, :] = up_ref[0]
    f_out[HD:2 * HD, :] = dn_ref[0]
    f_out[2 * HD:, 0:HD] = heads_ref[1, 1]
    f_out[2 * HD:, HD:TILE] = heads_ref[1, 2]
    f_out[2 * HD:, TILE:TILE + HD] = heads_ref[1, 0]
    f_out[2 * HD:, TILE + HD:] = jnp.transpose(outs_ref[1])
    b_out[0:HD, :] = up_ref[1]
    b_out[HD:, :] = dn_ref[1]
    for l in range(LAYERS):
        large, small = (0, 2) if l else (2, 0)
        moments[large, 0:HD, :] = mu_ref[l] * muon_decay
        moments[large + 1, 0:HD, :] = md_ref[l] * muon_decay
        moments[small, HD:, 0:HD] = mh_ref[l, 1] * muon_decay
        moments[small, HD:, HD:TILE] = mh_ref[l, 2] * muon_decay
        moments[small + 1, HD:, 0:HD] = mh_ref[l, 0] * muon_decay
        moments[small + 1, HD:, HD:TILE] = jnp.transpose(mo_ref[l]) * muon_decay
    for r in range(rows):
        moments[r, HD:, TILE:] = jnp.zeros((HD, TILE), f32)
    for k in range(rows):
        late_outs[k][...] = moments[z ^ k]


def update_kernel(
    rows, idx_ref, heads_ref, outs_ref, up_ref, dn_ref, params_ref, first_ref, second_ref, *refs
):
    z = idx_ref[1]
    mom_refs, step_refs, refs = refs[:rows], refs[rows:2 * rows], refs[2 * rows:]
    (heads_out, outs_out, up_out, dn_out, mh_out, mo_out, mu_out, md_out, first_out, second_out, params_out,
     mom, step) = refs
    for k in range(rows):
        mom[z ^ k] = mom_refs[k][...]
        step[z ^ k] = step_refs[k][...] * muon_rate
    for l in range(LAYERS):
        large, small = (0, 2) if l else (2, 0)
        mu_out[l] = mom[large, 0:HD, :]
        md_out[l] = mom[large + 1, 0:HD, :]
        up_out[l] = up_ref[l] - D ** -0.5 * step[large, :, 0:2 * TILE]
        dn_out[l] = dn_ref[l] - FF ** -0.5 * step[large + 1, :, 0:2 * TILE]
        kv, qo = mom[small, HD:, 0:TILE], mom[small + 1, HD:, 0:TILE]
        mh_out[l, 0] = qo[:, 0:HD]
        mh_out[l, 1] = kv[:, 0:HD]
        mh_out[l, 2] = swap(kv)[:, 0:HD]
        mo_out[l] = jnp.transpose(swap(qo))[0:HD, :]
        kv, qo = step[small, :, 2 * TILE:], step[small + 1, :, 2 * TILE:]
        heads_out[l, 0] = heads_ref[l, 0] - D ** -0.5 * qo[:, 0:HD]
        heads_out[l, 1] = heads_ref[l, 1] - D ** -0.5 * kv[:, 0:HD]
        heads_out[l, 2] = heads_ref[l, 2] - D ** -0.5 * swap(kv)[:, 0:HD]
        outs_out[l] = outs_ref[l] - (D // 16) ** -0.5 * jnp.transpose(swap(qo))[0:HD, :]
        grad = jnp.transpose(mom[small + 1, HD:, TILE:])[0:4, :]
        first = adam_first * first_ref[l] + (1.0 - adam_first) * grad
        second = adam_second * second_ref[l] + (1.0 - adam_second) * grad * grad
        first_out[l] = first
        second_out[l] = second
        params_out[l] = params_ref[l] - adam_rate * (first / (1.0 - adam_first**STEP)) / (
            jnp.sqrt(second / (1.0 - adam_second**STEP)) + adam_eps
        )


def call(body, operands, outs, scratch=(), flops=0, vmem=50):
    specs = [pl.BlockSpec(memory_space=pltpu.SMEM if x.ndim == 1 else pltpu.VMEM) for x in operands]
    moved = sum(4 * math.prod(x.shape) for x in operands) + sum(4 * math.prod(s) for s in outs)
    return pl.pallas_call(
        body,
        out_shape=[jax.ShapeDtypeStruct(s, f32) for s in outs],
        in_specs=specs,
        out_specs=[pl.BlockSpec(memory_space=pltpu.VMEM) for _ in outs],
        scratch_shapes=[pltpu.VMEM(s, f32) for s in scratch],
        compiler_params=pltpu.CompilerParams(vmem_limit_bytes=vmem * 2**20),
        cost_estimate=pl.CostEstimate(flops=flops, bytes_accessed=moved if flops else 0, transcendentals=0),
    )(*operands)


def fetched_call(body, idx, operands, outs, scratch):
    count, given = len(operands), len(outs) + len(scratch)

    def kernel(idx_ref, *refs):
        sources, rest, held, sems = refs[:count], refs[count:count + given], refs[count + given:-1], refs[-1]
        copies = [pltpu.make_async_copy(a, b, sems.at[i]) for i, (a, b) in enumerate(zip(sources, held))]
        for copy in copies:
            copy.start()
        for copy in copies:
            copy.wait()
        body(idx_ref, *held, *rest)

    return pl.pallas_call(
        kernel,
        out_shape=[jax.ShapeDtypeStruct(s, f32) for s in outs],
        in_specs=[pl.BlockSpec(memory_space=pltpu.SMEM)] + [pl.BlockSpec(memory_space=pltpu.HBM)] * count,
        out_specs=[pl.BlockSpec(memory_space=pltpu.VMEM) for _ in outs],
        scratch_shapes=[pltpu.VMEM(s, f32) for s in scratch]
        + [pltpu.VMEM(x.shape, f32) for x in operands] + [pltpu.SemaphoreType.DMA((count,))],
        compiler_params=pltpu.CompilerParams(vmem_limit_bytes=56 * 2**20),
    )(idx, *operands)


def on_device(
    layer_input,
    segment_ids,
    head_projection_weights,
    output_projection_weights,
    up_projection_weights,
    down_projection_weights,
    head_moment,
    out_moment,
    up_moment,
    down_moment,
    norm_params,
    norm_first,
    norm_second,
    output_grad,
):
    row = lax.axis_index("row").astype(jnp.int32)
    col = lax.axis_index("col").astype(jnp.int32)
    rows = lax.axis_size("row")
    cols = lax.axis_size("col")
    dps = lax.axis_size("dp")
    span = layer_input.shape[1]
    length = span * cols
    idx = jnp.stack([col, row, lax.axis_index("dp").astype(jnp.int32)])
    swap2 = lambda x: jnp.swapaxes(x, -1, -2)

    def perm(x, axis, bit):
        return lax.ppermute(x, axis, [(i, i ^ bit) for i in range(lax.axis_size(axis))])

    def spread_cols(x):
        across = perm(x, "col", 2)
        return [x, perm(x, "col", 1), across, perm(across, "col", 1)]

    def spread_rows(parts):
        return [parts[0]] + [perm(parts[k], "row", k) for k in range(1, rows)]

    heads, outs, ups = head_projection_weights, output_projection_weights, up_projection_weights
    downs = swap2(down_projection_weights)
    shard_a = pl.pallas_call(
        first_pack_kernel,
        out_shape=jax.ShapeDtypeStruct((2 * HD + 8, D), f32),
        in_specs=[pl.BlockSpec(memory_space=pltpu.HBM)] * 4,
        out_specs=pl.BlockSpec(memory_space=pltpu.VMEM),
        scratch_shapes=[
            pltpu.VMEM((3, HD, HD), f32), pltpu.VMEM((HD, HD), f32), pltpu.VMEM((8, HD), f32), pltpu.SemaphoreType.DMA((4,)),
        ],
        compiler_params=pltpu.CompilerParams(vmem_limit_bytes=60 * 2**20),
    )(heads, outs, swap2(layer_input[0]), norm_params.reshape(8, HD))
    og = swap2(output_grad[0])
    shard_f, shard_b, *moments = fetched_call(
        functools.partial(pack_kernel, rows),
        idx, [heads, outs, ups, downs, head_moment, out_moment, up_moment, swap2(down_moment)],
        [(3 * HD, D), (2 * HD, D)] + [(2 * HD, D)] * rows, [(rows, 2 * HD, D)],
    )
    pieces = spread_rows([shard_a] * rows)
    *pieces, shard_f = lax.optimization_barrier((*pieces, shard_f))
    mine_a = jnp.stack(pieces)
    across_a, core_a = perm(mine_a, "col", 2), perm(mine_a, "col", 1)
    shard_f, _ = lax.optimization_barrier((shard_f, core_a))
    pieces_f = spread_rows([shard_f] * rows)
    mine_f = jnp.stack(pieces_f)
    across_a, mine_f = lax.optimization_barrier((across_a, mine_f))
    packs_a = [mine_a, core_a, across_a, perm(across_a, "col", 1)]
    across_f = perm(mine_f, "col", 2)
    shard_b, _ = lax.optimization_barrier((shard_b, pieces_f[1]))
    pieces_b = spread_rows([shard_b] * rows)

    full = (cols, span, D)
    pair = (2, span, D)
    own = (span, D)
    wide = (span, FF)
    half = (D, cols * TILE)
    keys = (length, cols * TILE)
    queries = (span, cols * TILE)
    one = (span, TILE)
    stats = (8, span)
    norms = (TILE, D)
    segs = [segment_ids]

    h_full, wkv, wqo, kv, qx, att, lse, mid, n1, i1, ln = call(
        functools.partial(attention_kernel, rows, cols),
        [idx] + segs + packs_a,
        [full, half, half, keys, queries, queries, stats, own, own, one, (8, D)], flops=5 * 10**9, vmem=12,
    )
    mid, across_f, og, *rest = lax.optimization_barrier((mid, across_f, og, *moments, *pieces_b))
    moments, pieces_b = rest[:rows], rest[rows:]
    packs_f = [mine_f, perm(mine_f, "col", 1), across_f, perm(across_f, "col", 1)]
    og = spread_rows([og] * rows)
    moments = spread_rows(moments)
    h_own, up, dn, before, act, n2, i2 = call(
        functools.partial(feed_kernel, rows, cols),
        [mid, ln] + packs_f,
        [own, (D, FF), (D, FF), wide, wide, own, one], flops=2 * 10**9, vmem=8,
    )
    h_own, *og = lax.optimization_barrier((h_own, *og))
    hidden = spread_cols(h_own)
    mine_b = jnp.stack(pieces_b)
    across_b = perm(mine_b, "col", 2)
    across_b, hidden[2] = lax.optimization_barrier((across_b, hidden[2]))
    packs_b = [mine_b, perm(mine_b, "col", 1), across_b, perm(across_b, "col", 1)]
    top, *saved, keep, send = call(
        functools.partial(top_layer_kernel, rows, cols),
        [idx, ln] + segs + packs_f + packs_b + og + hidden,
        [own, full, own, wide, queries, keys, queries, wide, own, own, norms, pair, pair],
        [half, half, keys, queries, stats, (D, FF), (D, FF), wide], flops=20 * 10**9, vmem=18,
    )
    layer_output = top[:, :HD][None]

    def fold_core(keep, send):
        got = perm(send, "col", 1)
        return got, perm(keep[1] + got[1], "col", 2)

    got, across = fold_core(keep, send)
    keep_t, send_t = call(
        functools.partial(top_gradients_kernel, rows, cols), [idx] + moments + saved, [pair, pair],
        flops=2 * 10**9, vmem=6,
    )
    got_t = perm(send_t, "col", 1)
    half_t = keep_t[1] + got_t[1]
    got, half_t = lax.optimization_barrier((got, half_t))
    across_t = perm(half_t, "col", 2)
    keep_g, send_g, dkv, dqx, dv1 = call(
        functools.partial(low_layer_kernel, rows, cols),
        [idx, ln] + segs + moments
        + [keep, got, across, h_full, mid, act, wqo, kv, qx, att, lse, n1, i1, up, dn, before, n2, i2],
        [pair, pair, keys, queries, own], [wide, own, norms], flops=12 * 10**9, vmem=12,
    )
    got, across = fold_core(keep_g, send_g)
    mine = keep_g[0] + got[0] + across
    top = keep_t[0] + got_t[0] + across_t
    top, mine = [
        lax.optimization_barrier(x + perm(x, "dp", 1) if dps == 2 else lax.psum(x, "dp")) for x in (top, mine)
    ]
    keep, send = call(
        low_input_kernel, [wkv, wqo, dkv, dqx, dv1], [pair, pair], flops=2 * 10**9, vmem=6,
    )
    got, across = fold_core(keep, send)
    input_grad = (keep[0] + got[0] + across)[:, :HD][None]

    tops, parts = spread_cols(top), spread_cols(mine)
    large, small = jnp.where(row < 2, top, mine), jnp.where(row < 2, mine, top)
    moms = jnp.concatenate([large.reshape(rows, HD, D), small.reshape(rows, HD, D)], axis=1)
    moms = spread_rows([moms[k] for k in range(rows)])
    large, small = call(
        functools.partial(orthogonal_kernel, cols), [idx] + tops + parts, [own, (D, TILE)],
        [(D, FF), (D, cols * TILE)], flops=8 * 10**9, vmem=16,
    )
    steps = jnp.concatenate([large.reshape(rows, HD, D), small.reshape(rows, HD, TILE)], axis=2)
    steps = spread_rows([steps[k] for k in range(rows)])
    three = (LAYERS, 4, HD)
    updates = list(call(
        functools.partial(update_kernel, rows),
        [idx, heads, outs, ups, downs, norm_params, norm_first, norm_second] + moms + steps,
        [heads.shape, outs.shape, ups.shape, downs.shape] * 2 + [three] * 3,
        [(rows, 2 * HD, D), (rows, HD, D + TILE)], vmem=8,
    ))
    for at in (3, 7):
        updates[at] = swap2(updates[at])
    return (layer_output, input_grad, *updates)


def solution(mesh):
    placed = (
        P("dp", "col", "row"),
        P("dp", None),
        P(None, None, "row", "col"),
        P(None, "col", "row"),
        P(None, "row", "col"),
        P(None, "col", "row"),
        P(None, None, "row", "col"),
        P(None, "col", "row"),
        P(None, "row", "col"),
        P(None, "col", "row"),
        P(None, None, "row"),
        P(None, None, "row"),
        P(None, None, "row"),
        P("dp", "col", "row"),
    )
    return jax.shard_map(
        on_device,
        mesh=mesh,
        in_specs=placed,
        out_specs=(
            P("dp", "col", "row"),
            P("dp", "col", "row"),
            P(None, None, "row", "col"),
            P(None, "col", "row"),
            P(None, "row", "col"),
            P(None, "col", "row"),
            P(None, None, "row", "col"),
            P(None, "col", "row"),
            P(None, "row", "col"),
            P(None, "col", "row"),
            P(None, None, "row"),
            P(None, None, "row"),
            P(None, None, "row"),
        ),
        check_vma=False,
    )
```

```python
import functools
import math

import jax
import jax.numpy as jnp
from jax import lax
from jax.experimental import pallas as pl
from jax.experimental.pallas import tpu as pltpu
from jax.sharding import PartitionSpec as P

D = 256
FF = 1024
LAYERS = 2
NS_STEPS = 5
STEP = 10
HD = 64
TILE = 128

norm_eps = 1e-05
newton_coefs = (3.4445, -4.775, 2.0315)
frob_eps = 1e-07
muon_decay = 0.95
muon_rate = 0.5
adam_first = 0.9
adam_second = 0.999
adam_eps = 1e-08
adam_rate = 0.2
masked_score = -1e30

f32 = jnp.float32
bf16 = jnp.bfloat16

NN = (((1,), (0,)), ((), ()))
NT = (((1,), (1,)), ((), ()))
TN = (((0,), (0,)), ((), ()))


def dot(a, b, dims=NN):
    return lax.dot_general(a, b, dims, precision=lax.Precision.HIGH, preferred_element_type=f32)


def dot1(a, b, dims=NN):
    return lax.dot_general(a, b, dims, preferred_element_type=f32)


def low_lanes(rows):
    return lax.broadcasted_iota(jnp.int32, (rows, TILE), 1) < HD


def swap(t):
    return pltpu.roll(t, HD, 1)


def dup_low(t):
    return jnp.where(low_lanes(t.shape[0]), t, swap(t))


def dup_high(t):
    return jnp.where(low_lanes(t.shape[0]), swap(t), t)


def halves(t):
    high = t.astype(bf16)
    return high, (t - high.astype(f32)).astype(bf16)


def mixed(t):
    high = t.astype(bf16).astype(f32)
    return jnp.where(low_lanes(t.shape[0]), high, t - high).astype(bf16)


def high_only(t):
    return jnp.where(low_lanes(t.shape[0]), t, 0.0).astype(bf16)


def left_stack(t):
    m = mixed(t)
    return jnp.concatenate([m, m], axis=1)


def right_stack(t):
    high, low = halves(t)
    return jnp.concatenate([high, low], axis=1)


def normalize(values):
    mean = jnp.sum(values, axis=-1, keepdims=True) * (1.0 / D)
    center = values - mean
    variance = jnp.sum(center * center, axis=-1, keepdims=True) * (1.0 / D)
    inverse = lax.rsqrt(variance + norm_eps)
    return center * inverse, inverse


def normalize_back(grad_out, normed, inverse, gain):
    scaled = grad_out * gain
    first = jnp.sum(scaled, axis=-1, keepdims=True) * (1.0 / D)
    second = jnp.sum(scaled * normed, axis=-1, keepdims=True) * (1.0 / D)
    grad_in = inverse * (scaled - first - normed * second)
    gain_grad = jnp.sum(grad_out * normed, axis=0, keepdims=True)
    shift_grad = jnp.sum(grad_out, axis=0, keepdims=True)
    return grad_in, gain_grad, shift_grad


def pack_reader(refs):
    return lambda r, k, lo, hi: refs[k][r, lo:hi, :]


def segment_row(seg_ref, chunk, span):
    return seg_ref[:, pl.ds(pl.multiple_of(chunk * span, span), span)].astype(f32)


def segment_column(seg_ref, chunk, span):
    return jnp.transpose(jnp.broadcast_to(segment_row(seg_ref, chunk, span), (TILE, span)))[:, 0:1]


def project_and_attend(c, h, wkv_ref, wqo_ref, seg_ref, kv_ref, qx_ref, att_ref, lse_ref):
    cols = h.shape[0]
    span = h.shape[1]
    wkv = wkv_ref[...]
    for j in range(cols):
        kv_ref[j * span:(j + 1) * span, :] = dot(h[j], wkv)
    h_own = h[0]
    qx_ref[...] = dot(h_own, wqo_ref[...])
    lane = lax.broadcasted_iota(jnp.int32, (span, TILE), 1)
    seg_row = jnp.concatenate([segment_row(seg_ref, c ^ k, span) for k in range(cols)], axis=1)
    allowed = segment_column(seg_ref, c, span) == seg_row
    lse_all = jnp.zeros((span, TILE), f32)
    for j in range(cols):
        tile = slice(j * TILE, (j + 1) * TILE)
        kv = kv_ref[:, tile]
        k_right = right_stack(dup_low(kv))
        v_dup = dup_high(kv)
        v_mix = mixed(v_dup)
        v_high = high_only(v_dup)
        q_left = left_stack(dup_low(qx_ref[:, tile]) * (HD ** -0.5))
        scores = jnp.where(allowed, dot1(q_left, k_right, NT), masked_score)
        top = jnp.max(scores, axis=-1, keepdims=True)
        raised = jnp.exp(scores - top)
        total = jnp.sum(raised, axis=-1, keepdims=True)
        p_high, p_low = halves(raised)
        out = dot1(p_high, v_mix) + dot1(p_low, v_high)
        out = (out + swap(out)) / total
        att_ref[:, tile] = jnp.where(low_lanes(span), 0.0, out)
        lse_all = jnp.where(lane == j, top + jnp.log(total), lse_all)
    lse_ref[...] = jnp.transpose(lse_all)[0:8, :]
    return dot(att_ref[...], wqo_ref[...], NT), h_own


def place_attention(rows, cols, block, at, wkv_ref, wqo_ref):
    for j in range(cols):
        for r in range(rows):
            piece = block(r, j, at, at + HD)
            wkv_ref[r * HD:(r + 1) * HD, j * TILE:(j + 1) * TILE] = piece[:, :TILE]
            wqo_ref[r * HD:(r + 1) * HD, j * TILE:(j + 1) * TILE] = piece[:, TILE:]


def place_feed(rows, cols, block, at, up_ref, dn_ref):
    for j in range(cols):
        for r in range(rows):
            to = (slice(r * HD, (r + 1) * HD), slice(j * 2 * TILE, (j + 1) * 2 * TILE))
            up_ref[to] = block(r, j, at, at + HD)
            dn_ref[to] = block(r, j, at + HD, at + 2 * HD)


def feed_forward(mid, up_ref, dn_ref, before_ref, act_ref):
    before = dot(mid, up_ref[...])
    before_ref[...] = before
    activated = 0.5 * before * (1.0 + lax.erf(before * 0.7071067811865476))
    act_ref[...] = activated
    return normalize(mid + dot(activated, dn_ref[...], NT))


def attention_kernel(rows, cols, idx_ref, seg_ref, *refs):
    c = idx_ref[0]
    packs, refs = refs[:cols], refs[cols:]
    h_out, wkv_out, wqo_out, kv_out, qx_out, att_out, lse_out, mid_out, n1_out, i1_out, params_out = refs
    block = pack_reader(packs)
    span = mid_out.shape[0]
    place_attention(rows, cols, block, 0, wkv_out, wqo_out)
    for j in range(cols):
        h_out[j] = jnp.transpose(
            jnp.concatenate([block(r, j, HD, 2 * HD) for r in range(rows)], axis=0)
        )
    tiles = []
    for t in range(rows // 2):
        a = block(2 * t, 0, 2 * HD, 2 * HD + 8)[:, 0:TILE]
        b = block(2 * t + 1, 0, 2 * HD, 2 * HD + 8)[:, 0:TILE]
        tiles.append(jnp.where(low_lanes(8), a, swap(b)))
    params_out[...] = jnp.concatenate(tiles, axis=1)
    branch, h_own = project_and_attend(
        c, h_out, wkv_out, wqo_out, seg_ref, kv_out, qx_out, att_out, lse_out
    )
    normed, inverse = normalize(h_own + branch)
    n1_out[...] = normed
    i1_out[...] = jnp.broadcast_to(inverse, (span, TILE))
    mid_out[...] = normed * params_out[0:1, :] + params_out[1:2, :]


def feed_kernel(rows, cols, mid_ref, ln_ref, *refs):
    packs, refs = refs[:cols], refs[cols:]
    h_out, up_out, dn_out, before_out, act_out, n2_out, i2_out = refs
    block = pack_reader(packs)
    place_feed(rows, cols, block, 0, up_out, dn_out)
    normed, inverse = feed_forward(mid_ref[...], up_out, dn_out, before_out, act_out)
    n2_out[...] = normed
    i2_out[...] = jnp.broadcast_to(inverse, i2_out.shape)
    h_out[...] = normed * ln_ref[2:3, :] + ln_ref[3:4, :]


def backward(
    c, dh, gains, seg_ref, wqo_ref, kv_ref, qx_ref, att_ref, lse_ref, n1, i1, up_ref, dn_ref,
    before_ref, n2, i2, dkv_ref, dqx_ref, dbef_ref, dv1_ref, dv2_ref, norm_ref
):
    span = n1.shape[0]
    cols = seg_ref.shape[1] // span
    dv2, gain2, shift2 = normalize_back(dh, n2, i2, gains[2])
    dv2_ref[...] = dv2
    d_act = dot(dv2, dn_ref[...])
    before = before_ref[...]
    slope = (
        0.5 * (1.0 + lax.erf(before * 0.7071067811865476))
        + before * jnp.exp(-0.5 * before * before) * 0.3989422804014327
    )
    dbef_ref[...] = d_act * slope
    d_mid = dv2 + dot(dbef_ref[...], up_ref[...], NT)
    dv1, gain1, shift1 = normalize_back(d_mid, n1, i1, gains[0])
    dv1_ref[...] = dv1
    norm_ref[...] = jnp.zeros_like(norm_ref)
    for k, row in enumerate((gain1, shift1, gain2, shift2)):
        norm_ref[k:k + 1, :] = row
    d_att = dot(dv1, wqo_ref[...])
    lane = lax.broadcasted_iota(jnp.int32, (span, TILE), 1)
    inner_all = jnp.zeros((span, TILE), f32)
    for j in range(cols):
        tile = slice(j * TILE, (j + 1) * TILE)
        inner = jnp.sum(d_att[:, tile] * att_ref[:, tile], axis=-1, keepdims=True)
        inner_all = jnp.where(lane == j, inner, inner_all)
    inner_rows = jnp.transpose(inner_all)
    seg_row = segment_row(seg_ref, c, span)
    seg_cols = [segment_column(seg_ref, c ^ b, span) for b in range(cols)]
    low = low_lanes(span)
    for j in range(cols):
        tile = slice(j * TILE, (j + 1) * TILE)
        q_dup = dup_low(qx_ref[:, tile]) * (HD ** -0.5)
        q_mix = mixed(q_dup)
        q_left = jnp.concatenate([q_mix, q_mix], axis=1)
        q_high = high_only(q_dup)
        do_dup = dup_high(d_att[:, tile])
        do_mix = mixed(do_dup)
        do_left = jnp.concatenate([do_mix, do_mix], axis=1)
        do_high = high_only(do_dup)
        lse_row = lse_ref[j:j + 1, :]
        inner_row = inner_rows[j:j + 1, :]
        dq_t = jnp.zeros((TILE, span), f32)
        for b in range(cols):
            keys = slice(b * span, (b + 1) * span)
            kv = kv_ref[keys, tile]
            k_dup = dup_low(kv)
            v_dup = dup_high(kv)
            scores = dot1(right_stack(k_dup), q_left, NT)
            shares = jnp.where(seg_cols[b] == seg_row, jnp.exp(scores - lse_row), 0.0)
            d_shares = dot1(right_stack(v_dup), do_left, NT)
            d_scores = shares * (d_shares - inner_row)
            p_high, p_low = halves(shares)
            s_high, s_low = halves(d_scores)
            dv = dot1(p_high, do_mix) + dot1(p_low, do_high)
            dk = dot1(s_high, q_mix) + dot1(s_low, q_high)
            dkv_ref[keys, tile] = jnp.where(low, dk + swap(dk), dv + swap(dv))
            k_t = jnp.transpose(k_dup)
            k_t_high = k_t.astype(bf16)
            upper = lax.broadcasted_iota(jnp.int32, (TILE, span), 0) < HD
            k_t_mix = jnp.where(upper, k_t_high.astype(f32), k_t - k_t_high.astype(f32)).astype(bf16)
            k_t_only = jnp.where(upper, k_t, 0.0).astype(bf16)
            dq_t = dq_t + dot1(k_t_mix, s_high) + dot1(k_t_only, s_low)
        dq = jnp.transpose(dq_t)
        dqx_ref[:, tile] = jnp.where(low, (dq + swap(dq)) * (HD ** -0.5), 0.0)


def input_gradient(wkv_ref, wqo_ref, dkv_ref, dqx_ref, dv1_ref, keep_out, send_out):
    span = dv1_ref.shape[0]
    wkv = wkv_ref[...]
    for k in (1, 3, 0, 2):
        part = dot(dkv_ref[k * span:(k + 1) * span, :], wkv, NT)
        if k == 0:
            part = part + dot(dqx_ref[...], wqo_ref[...], NT) + dv1_ref[...]
        (send_out if k % 2 else keep_out)[k // 2] = part


def weight_gradients(
    role, cols, h_ref, mid_ref, act_ref, att_ref, dkv_ref, dqx_ref, dbef_ref, dv1_ref, dv2_ref, norm_ref, grad_at
):
    span = dv1_ref.shape[0]

    @pl.when(role == 0)
    def _():
        mid = mid_ref[...]
        for k in range(cols):
            grad_at(k)[...] = dot(mid, dbef_ref[:, k * 2 * TILE:(k + 1) * 2 * TILE], TN)

    @pl.when(role == 1)
    def _():
        for k in range(cols):
            grad_at(k)[...] = dot(dv2_ref[...], act_ref[:, k * 2 * TILE:(k + 1) * 2 * TILE], TN)

    @pl.when(role == 2)
    def _():
        total = dot(h_ref[0], dkv_ref[0:span, :], TN)
        for b in range(1, cols):
            total += dot(h_ref[b], dkv_ref[b * span:(b + 1) * span, :], TN)
        for k in range(cols):
            grad_at(k)[:, 0:TILE] = total[:, k * TILE:(k + 1) * TILE]
            grad_at(k)[:, TILE:] = jnp.zeros((D, TILE), f32)

    @pl.when(role == 3)
    def _():
        total = dot(h_ref[0], dqx_ref[...], TN) + dot(dv1_ref[...], att_ref[...], TN)
        norms = jnp.transpose(norm_ref[...])
        for k in range(cols):
            grad_at(k)[:, 0:TILE] = total[:, k * TILE:(k + 1) * TILE]
            grad_at(k)[:, TILE:] = norms


def top_layer_kernel(rows, cols, idx_ref, ln_ref, seg_ref, *refs):
    c = idx_ref[0]
    packs, wide_packs, refs = refs[:cols], refs[cols:2 * cols], refs[2 * cols:]
    late_refs, h_refs, refs = refs[:rows], refs[rows:rows + cols], refs[rows + cols:]
    (out_ref, h_full, mid_ref, act_ref, att_ref, dkv_ref, dqx_ref, dbef_ref, dv1_ref, dv2_ref, norm_ref,
     keep_out, send_out, wkv_ref, wqo_ref, kv_ref, qx_ref, lse_ref, up_ref, dn_ref, before_ref) = refs
    place_attention(rows, cols, pack_reader(packs), 2 * HD, wkv_ref, wqo_ref)
    place_feed(rows, cols, pack_reader(wide_packs), 0, up_ref, dn_ref)
    for j in range(cols):
        h_full[j] = h_refs[j][...]
    gains = [ln_ref[k:k + 1, :] for k in range(4, 8)]
    branch, h_own = project_and_attend(
        c, h_full, wkv_ref, wqo_ref, seg_ref, kv_ref, qx_ref, att_ref, lse_ref
    )
    n1, i1 = normalize(h_own + branch)
    mid_ref[...] = n1 * gains[0] + gains[1]
    n2, i2 = feed_forward(mid_ref[...], up_ref, dn_ref, before_ref, act_ref)
    out_ref[...] = n2 * gains[2] + gains[3]
    dh = jnp.transpose(jnp.concatenate([ref[2 * HD:, :] for ref in late_refs], axis=0))
    backward(
        c, dh, gains, seg_ref, wqo_ref, kv_ref, qx_ref, att_ref, lse_ref, n1, i1, up_ref, dn_ref,
        before_ref, n2, i2, dkv_ref, dqx_ref, dbef_ref, dv1_ref, dv2_ref, norm_ref
    )
    input_gradient(wkv_ref, wqo_ref, dkv_ref, dqx_ref, dv1_ref, keep_out, send_out)


def add_moment(idx_ref, late_refs, big, at):
    first = 0 if big else HD

    @pl.when(idx_ref[2] == 0)
    def _():
        for r, ref in enumerate(late_refs):
            at[r * HD:(r + 1) * HD, :] += ref[first:first + HD, :]


def top_gradients_kernel(rows, cols, idx_ref, *refs):
    z = idx_ref[1]
    late_refs, refs = refs[:rows], refs[rows:]
    keep_out, send_out = refs[-2:]
    weight_gradients(z, cols, *refs[:-2], lambda k: (send_out if k % 2 else keep_out).at[k // 2])
    for big in (True, False):

        @pl.when((z < 2) == big)
        def _():
            add_moment(idx_ref, late_refs, big, keep_out.at[0])


def low_layer_kernel(rows, cols, idx_ref, ln_ref, seg_ref, *refs):
    late_refs, refs = refs[:rows], refs[rows:]
    z = idx_ref[1]
    (dh_keep, dh_got, dh_across, h_ref, mid_ref, act_ref, wqo_ref, kv_ref, qx_ref, att_ref, lse_ref, n1_ref,
     i1_ref, up_ref, dn_ref, before_ref, n2_ref, i2_ref, keep_out, send_out, dkv_ref, dqx_ref, dv1_ref,
     dbef_ref, dv2_ref, norm_ref) = refs
    dh = dh_keep[0] + dh_got[0] + dh_across[...]
    gains = [ln_ref[k:k + 1, :] for k in range(4)]
    backward(
        idx_ref[0], dh, gains, seg_ref, wqo_ref, kv_ref, qx_ref, att_ref, lse_ref, n1_ref[...],
        i1_ref[:, 0:1], up_ref, dn_ref, before_ref, n2_ref[...], i2_ref[:, 0:1], dkv_ref, dqx_ref, dbef_ref,
        dv1_ref, dv2_ref, norm_ref
    )
    weight_gradients(
        z ^ 2, cols, h_ref, mid_ref, act_ref, att_ref, dkv_ref, dqx_ref, dbef_ref, dv1_ref, dv2_ref, norm_ref,
        lambda k: (send_out if k % 2 else keep_out).at[k // 2]
    )
    for big in (True, False):

        @pl.when((z >= 2) == big)
        def _():
            add_moment(idx_ref, late_refs, big, keep_out.at[0])


def low_input_kernel(*refs):
    input_gradient(*refs)


def symmetric(high, low, dims):
    return dot1(high, high, dims) + (dot1(high, low, dims) + dot1(low, high, dims))


def newton_schulz(blocks, wanted):
    sizes = [jnp.sum(x * x, keepdims=True) for x in blocks]
    blocks = [x / (jnp.sqrt(s) + frob_eps) for x, s in zip(blocks, sizes)]
    for step in range(NS_STEPS):
        parts = [halves(x) for x in blocks]
        grams = [symmetric(h, l, NT) for h, l in parts]
        squares = [symmetric(*halves(a), NN) for a in grams]
        polys = [halves(newton_coefs[1] * a + newton_coefs[2] * s) for a, s in zip(grams, squares)]
        if step == NS_STEPS - 1:
            blocks = [x[:, :n] for x, n in zip(blocks, wanted)]
            parts = [(h[:, :n], l[:, :n]) for (h, l), n in zip(parts, wanted)]
        blocks = [
            newton_coefs[0] * x + (dot1(ph, h) + dot1(ph, l) + dot1(pl_, h))
            for x, (h, l), (ph, pl_) in zip(blocks, parts, polys)
        ]
    return blocks


def orthogonal_kernel(cols, idx_ref, *refs):
    z = idx_ref[1]
    top_refs, low_refs = refs[:cols], refs[cols:2 * cols]
    big_out, small_out, big, small = refs[2 * cols:]

    @pl.when(z < 2)
    def _():
        for k in range(cols):
            big[:, k * 2 * TILE:(k + 1) * 2 * TILE] = top_refs[k][...]
            small[:, k * TILE:(k + 1) * TILE] = low_refs[k][:, 0:TILE]

    @pl.when(z >= 2)
    def _():
        for k in range(cols):
            big[:, k * 2 * TILE:(k + 1) * 2 * TILE] = low_refs[k][...]
            small[:, k * TILE:(k + 1) * TILE] = top_refs[k][:, 0:TILE]

    low = low_lanes(D)
    lefts, rights = [], []
    for t in range(cols // 2):
        a = small[:, 2 * t * TILE:(2 * t + 1) * TILE]
        b = small[:, (2 * t + 1) * TILE:(2 * t + 2) * TILE]
        lefts.append(jnp.where(low, a, swap(b)))
        rights.append(jnp.where(low, swap(a), b))
    wide, left, right = newton_schulz(
        [big[...], jnp.concatenate(lefts, axis=1), jnp.concatenate(rights, axis=1)], (2 * TILE, TILE, TILE)
    )
    big_out[...] = wide * math.sqrt(FF)
    small_out[...] = jnp.where(low, left, swap(right)) * math.sqrt(D)


def first_pack_kernel(heads_hbm, outs_hbm, x_hbm, params_hbm, shard_out, heads_ref, outs_ref, params_ref, sems):
    shard_out[2 * HD:, :] = jnp.zeros((8, 2 * TILE), f32)
    copies = [
        pltpu.make_async_copy(source, target, sems.at[i])
        for i, (source, target) in enumerate(
            (
                (heads_hbm.at[0], heads_ref),
                (outs_hbm.at[0], outs_ref),
                (params_hbm, params_ref),
                (x_hbm, shard_out.at[pl.ds(HD, HD)]),
            )
        )
    ]
    for copy in copies:
        copy.start()
    for copy in copies:
        copy.wait()
    shard_out[0:HD, 0:HD] = heads_ref[1]
    shard_out[0:HD, HD:TILE] = heads_ref[2]
    shard_out[0:HD, TILE:TILE + HD] = heads_ref[0]
    shard_out[0:HD, TILE + HD:] = jnp.transpose(outs_ref[...])
    shard_out[2 * HD:, 0:HD] = params_ref[...]


def pack_kernel(
    rows, idx_ref, heads_ref, outs_ref, up_ref, dn_ref, og_ref, mh_ref, mo_ref, mu_ref, md_ref, f_out, b_out, *refs
):
    z = idx_ref[1]
    late_outs, moments = refs[:rows], refs[rows]
    f_out[0:HD, :] = up_ref[0]
    f_out[HD:2 * HD, :] = dn_ref[0]
    f_out[2 * HD:, 0:HD] = heads_ref[1, 1]
    f_out[2 * HD:, HD:TILE] = heads_ref[1, 2]
    f_out[2 * HD:, TILE:TILE + HD] = heads_ref[1, 0]
    f_out[2 * HD:, TILE + HD:] = jnp.transpose(outs_ref[1])
    b_out[0:HD, :] = up_ref[1]
    b_out[HD:2 * HD, :] = dn_ref[1]
    b_out[2 * HD:, :] = og_ref[...]
    for l in range(LAYERS):
        large, small = (0, 2) if l else (2, 0)
        moments[large, 0:HD, :] = mu_ref[l] * muon_decay
        moments[large + 1, 0:HD, :] = md_ref[l] * muon_decay
        moments[small, HD:, 0:HD] = mh_ref[l, 1] * muon_decay
        moments[small, HD:, HD:TILE] = mh_ref[l, 2] * muon_decay
        moments[small + 1, HD:, 0:HD] = mh_ref[l, 0] * muon_decay
        moments[small + 1, HD:, HD:TILE] = jnp.transpose(mo_ref[l]) * muon_decay
    for r in range(rows):
        moments[r, HD:, TILE:] = jnp.zeros((HD, TILE), f32)
    for k in range(rows):
        late_outs[k][...] = moments[z ^ k]


def update_kernel(
    rows, idx_ref, heads_ref, outs_ref, up_ref, dn_ref, params_ref, first_ref, second_ref, *refs
):
    z = idx_ref[1]
    mom_refs, step_refs, refs = refs[:rows], refs[rows:2 * rows], refs[2 * rows:]
    (heads_out, outs_out, up_out, dn_out, mh_out, mo_out, mu_out, md_out, first_out, second_out, params_out,
     mom, step) = refs
    for k in range(rows):
        mom[z ^ k] = mom_refs[k][...]
        step[z ^ k] = step_refs[k][...] * muon_rate
    for l in range(LAYERS):
        large, small = (0, 2) if l else (2, 0)
        mu_out[l] = mom[large, 0:HD, :]
        md_out[l] = mom[large + 1, 0:HD, :]
        up_out[l] = up_ref[l] - D ** -0.5 * step[large, :, 0:2 * TILE]
        dn_out[l] = dn_ref[l] - FF ** -0.5 * step[large + 1, :, 0:2 * TILE]
        kv, qo = mom[small, HD:, 0:TILE], mom[small + 1, HD:, 0:TILE]
        mh_out[l, 0] = qo[:, 0:HD]
        mh_out[l, 1] = kv[:, 0:HD]
        mh_out[l, 2] = swap(kv)[:, 0:HD]
        mo_out[l] = jnp.transpose(swap(qo))[0:HD, :]
        kv, qo = step[small, :, 2 * TILE:], step[small + 1, :, 2 * TILE:]
        heads_out[l, 0] = heads_ref[l, 0] - D ** -0.5 * qo[:, 0:HD]
        heads_out[l, 1] = heads_ref[l, 1] - D ** -0.5 * kv[:, 0:HD]
        heads_out[l, 2] = heads_ref[l, 2] - D ** -0.5 * swap(kv)[:, 0:HD]
        outs_out[l] = outs_ref[l] - (D // 16) ** -0.5 * jnp.transpose(swap(qo))[0:HD, :]
        grad = jnp.transpose(mom[small + 1, HD:, TILE:])[0:4, :]
        first = adam_first * first_ref[l] + (1.0 - adam_first) * grad
        second = adam_second * second_ref[l] + (1.0 - adam_second) * grad * grad
        first_out[l] = first
        second_out[l] = second
        params_out[l] = params_ref[l] - adam_rate * (first / (1.0 - adam_first**STEP)) / (
            jnp.sqrt(second / (1.0 - adam_second**STEP)) + adam_eps
        )


def call(body, operands, outs, scratch=(), flops=0, vmem=50):
    specs = [pl.BlockSpec(memory_space=pltpu.SMEM if x.ndim == 1 else pltpu.VMEM) for x in operands]
    moved = sum(4 * math.prod(x.shape) for x in operands) + sum(4 * math.prod(s) for s in outs)
    return pl.pallas_call(
        body,
        out_shape=[jax.ShapeDtypeStruct(s, f32) for s in outs],
        in_specs=specs,
        out_specs=[pl.BlockSpec(memory_space=pltpu.VMEM) for _ in outs],
        scratch_shapes=[pltpu.VMEM(s, f32) for s in scratch],
        compiler_params=pltpu.CompilerParams(vmem_limit_bytes=vmem * 2**20),
        cost_estimate=pl.CostEstimate(flops=flops, bytes_accessed=moved if flops else 0, transcendentals=0),
    )(*operands)


def fetched_call(body, idx, operands, outs, scratch):
    count, given = len(operands), len(outs) + len(scratch)

    def kernel(idx_ref, *refs):
        sources, rest, held, sems = refs[:count], refs[count:count + given], refs[count + given:-1], refs[-1]
        copies = [pltpu.make_async_copy(a, b, sems.at[i]) for i, (a, b) in enumerate(zip(sources, held))]
        for copy in copies:
            copy.start()
        for copy in copies:
            copy.wait()
        body(idx_ref, *held, *rest)

    return pl.pallas_call(
        kernel,
        out_shape=[jax.ShapeDtypeStruct(s, f32) for s in outs],
        in_specs=[pl.BlockSpec(memory_space=pltpu.SMEM)] + [pl.BlockSpec(memory_space=pltpu.HBM)] * count,
        out_specs=[pl.BlockSpec(memory_space=pltpu.VMEM) for _ in outs],
        scratch_shapes=[pltpu.VMEM(s, f32) for s in scratch]
        + [pltpu.VMEM(x.shape, f32) for x in operands] + [pltpu.SemaphoreType.DMA((count,))],
        compiler_params=pltpu.CompilerParams(vmem_limit_bytes=56 * 2**20),
    )(idx, *operands)


def on_device(
    layer_input,
    segment_ids,
    head_projection_weights,
    output_projection_weights,
    up_projection_weights,
    down_projection_weights,
    head_moment,
    out_moment,
    up_moment,
    down_moment,
    norm_params,
    norm_first,
    norm_second,
    output_grad,
):
    row = lax.axis_index("row").astype(jnp.int32)
    col = lax.axis_index("col").astype(jnp.int32)
    rows = lax.axis_size("row")
    cols = lax.axis_size("col")
    dps = lax.axis_size("dp")
    span = layer_input.shape[1]
    length = span * cols
    idx = jnp.stack([col, row, lax.axis_index("dp").astype(jnp.int32)])
    swap2 = lambda x: jnp.swapaxes(x, -1, -2)

    def perm(x, axis, bit):
        return lax.ppermute(x, axis, [(i, i ^ bit) for i in range(lax.axis_size(axis))])

    def spread_cols(x):
        across = perm(x, "col", 2)
        return [x, perm(x, "col", 1), across, perm(across, "col", 1)]

    def spread_rows(parts):
        return [parts[0]] + [perm(parts[k], "row", k) for k in range(1, rows)]

    heads, outs, ups = head_projection_weights, output_projection_weights, up_projection_weights
    downs = swap2(down_projection_weights)
    shard_a = pl.pallas_call(
        first_pack_kernel,
        out_shape=jax.ShapeDtypeStruct((2 * HD + 8, D), f32),
        in_specs=[pl.BlockSpec(memory_space=pltpu.HBM)] * 4,
        out_specs=pl.BlockSpec(memory_space=pltpu.VMEM),
        scratch_shapes=[
            pltpu.VMEM((3, HD, HD), f32), pltpu.VMEM((HD, HD), f32), pltpu.VMEM((8, HD), f32), pltpu.SemaphoreType.DMA((4,)),
        ],
        compiler_params=pltpu.CompilerParams(vmem_limit_bytes=60 * 2**20),
    )(heads, outs, swap2(layer_input[0]), norm_params.reshape(8, HD))
    shard_f, shard_b, *moments = fetched_call(
        functools.partial(pack_kernel, rows),
        idx, [heads, outs, ups, downs, swap2(output_grad[0]), head_moment, out_moment, up_moment, swap2(down_moment)],
        [(3 * HD, D), (3 * HD, D)] + [(2 * HD, D)] * rows, [(rows, 2 * HD, D)],
    )
    pieces = spread_rows([shard_a] * rows)
    *pieces, shard_f = lax.optimization_barrier((*pieces, shard_f))
    mine_a = jnp.stack(pieces)
    across_a, core_a = perm(mine_a, "col", 2), perm(mine_a, "col", 1)
    shard_f, _ = lax.optimization_barrier((shard_f, core_a))
    pieces_f = spread_rows([shard_f] * rows)
    mine_f = jnp.stack(pieces_f)
    across_a, mine_f = lax.optimization_barrier((across_a, mine_f))
    packs_a = [mine_a, core_a, across_a, perm(across_a, "col", 1)]
    across_f = perm(mine_f, "col", 2)
    shard_b, _ = lax.optimization_barrier((shard_b, pieces_f[1]))
    pieces_b = spread_rows([shard_b] * rows)

    full = (cols, span, D)
    pair = (2, span, D)
    own = (span, D)
    wide = (span, FF)
    half = (D, cols * TILE)
    keys = (length, cols * TILE)
    queries = (span, cols * TILE)
    one = (span, TILE)
    stats = (8, span)
    norms = (TILE, D)
    segs = [segment_ids]

    h_full, wkv, wqo, kv, qx, att, lse, mid, n1, i1, ln = call(
        functools.partial(attention_kernel, rows, cols),
        [idx] + segs + packs_a,
        [full, half, half, keys, queries, queries, stats, own, own, one, (8, D)], flops=5 * 10**9, vmem=12,
    )
    mid, across_f, *rest = lax.optimization_barrier((mid, across_f, *moments, *pieces_b))
    moments, pieces_b = rest[:rows], rest[rows:]
    packs_f = [mine_f, perm(mine_f, "col", 1), across_f, perm(across_f, "col", 1)]
    moments = spread_rows(moments)
    h_own, up, dn, before, act, n2, i2 = call(
        functools.partial(feed_kernel, rows, cols),
        [mid, ln] + packs_f,
        [own, (D, FF), (D, FF), wide, wide, own, one], flops=2 * 10**9, vmem=8,
    )
    hidden = spread_cols(h_own)
    mine_b = jnp.stack([x[:2 * HD] for x in pieces_b])
    across_b = perm(mine_b, "col", 2)
    across_b, hidden[2], *moments = lax.optimization_barrier((across_b, hidden[2], *moments))
    packs_b = [mine_b, perm(mine_b, "col", 1), across_b, perm(across_b, "col", 1)]
    top, *saved, keep, send = call(
        functools.partial(top_layer_kernel, rows, cols),
        [idx, ln] + segs + packs_f + packs_b + pieces_b + hidden,
        [own, full, own, wide, queries, keys, queries, wide, own, own, norms, pair, pair],
        [half, half, keys, queries, stats, (D, FF), (D, FF), wide], flops=20 * 10**9, vmem=18,
    )
    layer_output = top[:, :HD][None]

    def fold_core(keep, send):
        got = perm(send, "col", 1)
        return got, perm(keep[1] + got[1], "col", 2)

    got, across = fold_core(keep, send)
    keep_t, send_t = call(
        functools.partial(top_gradients_kernel, rows, cols), [idx] + moments + saved, [pair, pair],
        flops=2 * 10**9, vmem=6,
    )
    got_t = perm(send_t, "col", 1)
    half_t = keep_t[1] + got_t[1]
    got, half_t = lax.optimization_barrier((got, half_t))
    across_t = perm(half_t, "col", 2)
    keep_g, send_g, dkv, dqx, dv1 = call(
        functools.partial(low_layer_kernel, rows, cols),
        [idx, ln] + segs + moments
        + [keep, got, across, h_full, mid, act, wqo, kv, qx, att, lse, n1, i1, up, dn, before, n2, i2],
        [pair, pair, keys, queries, own], [wide, own, norms], flops=12 * 10**9, vmem=12,
    )
    got, across = fold_core(keep_g, send_g)
    mine = keep_g[0] + got[0] + across
    top = keep_t[0] + got_t[0] + across_t
    top, mine = [
        lax.optimization_barrier(x + perm(x, "dp", 1) if dps == 2 else lax.psum(x, "dp")) for x in (top, mine)
    ]
    keep, send = call(
        low_input_kernel, [wkv, wqo, dkv, dqx, dv1], [pair, pair], flops=2 * 10**9, vmem=6,
    )
    got, across = fold_core(keep, send)
    input_grad = (keep[0] + got[0] + across)[:, :HD][None]

    tops, parts = spread_cols(top), spread_cols(mine)
    large, small = jnp.where(row < 2, top, mine), jnp.where(row < 2, mine, top)
    moms = jnp.concatenate([large.reshape(rows, HD, D), small.reshape(rows, HD, D)], axis=1)
    moms = spread_rows([moms[k] for k in range(rows)])
    large, small = call(
        functools.partial(orthogonal_kernel, cols), [idx] + tops + parts, [own, (D, TILE)],
        [(D, FF), (D, cols * TILE)], flops=8 * 10**9, vmem=16,
    )
    steps = jnp.concatenate([large.reshape(rows, HD, D), small.reshape(rows, HD, TILE)], axis=2)
    steps = spread_rows([steps[k] for k in range(rows)])
    three = (LAYERS, 4, HD)
    updates = list(call(
        functools.partial(update_kernel, rows),
        [idx, heads, outs, ups, downs, norm_params, norm_first, norm_second] + moms + steps,
        [heads.shape, outs.shape, ups.shape, downs.shape] * 2 + [three] * 3,
        [(rows, 2 * HD, D), (rows, HD, D + TILE)], vmem=8,
    ))
    for at in (3, 7):
        updates[at] = swap2(updates[at])
    return (layer_output, input_grad, *updates)


def solution(mesh):
    placed = (
        P("dp", "col", "row"),
        P("dp", None),
        P(None, None, "row", "col"),
        P(None, "col", "row"),
        P(None, "row", "col"),
        P(None, "col", "row"),
        P(None, None, "row", "col"),
        P(None, "col", "row"),
        P(None, "row", "col"),
        P(None, "col", "row"),
        P(None, None, "row"),
        P(None, None, "row"),
        P(None, None, "row"),
        P("dp", "col", "row"),
    )
    return jax.shard_map(
        on_device,
        mesh=mesh,
        in_specs=placed,
        out_specs=(
            P("dp", "col", "row"),
            P("dp", "col", "row"),
            P(None, None, "row", "col"),
            P(None, "col", "row"),
            P(None, "row", "col"),
            P(None, "col", "row"),
            P(None, None, "row", "col"),
            P(None, "col", "row"),
            P(None, "row", "col"),
            P(None, "col", "row"),
            P(None, None, "row"),
            P(None, None, "row"),
            P(None, None, "row"),
        ),
        check_vma=False,
    )
```

```python
import functools
import math

import jax
import jax.numpy as jnp
from jax import lax
from jax.experimental import pallas as pl
from jax.experimental.pallas import tpu as pltpu
from jax.sharding import PartitionSpec as P

D = 256
FF = 1024
LAYERS = 2
NS_STEPS = 5
STEP = 10
HD = 64
TILE = 128

norm_eps = 1e-05
newton_coefs = (3.4445, -4.775, 2.0315)
frob_eps = 1e-07
muon_decay = 0.95
muon_rate = 0.5
adam_first = 0.9
adam_second = 0.999
adam_eps = 1e-08
adam_rate = 0.2
masked_score = -1e30

f32 = jnp.float32
bf16 = jnp.bfloat16

NN = (((1,), (0,)), ((), ()))
NT = (((1,), (1,)), ((), ()))
TN = (((0,), (0,)), ((), ()))


def dot(a, b, dims=NN):
    return lax.dot_general(a, b, dims, precision=lax.Precision.HIGH, preferred_element_type=f32)


def dot1(a, b, dims=NN):
    return lax.dot_general(a, b, dims, preferred_element_type=f32)


def low_lanes(rows):
    return lax.broadcasted_iota(jnp.int32, (rows, TILE), 1) < HD


def swap(t):
    return pltpu.roll(t, HD, 1)


def dup_low(t):
    return jnp.where(low_lanes(t.shape[0]), t, swap(t))


def dup_high(t):
    return jnp.where(low_lanes(t.shape[0]), swap(t), t)


def halves(t):
    high = t.astype(bf16)
    return high, (t - high.astype(f32)).astype(bf16)


def mixed(t):
    high = t.astype(bf16).astype(f32)
    return jnp.where(low_lanes(t.shape[0]), high, t - high).astype(bf16)


def high_only(t):
    return jnp.where(low_lanes(t.shape[0]), t, 0.0).astype(bf16)


def left_stack(t):
    m = mixed(t)
    return jnp.concatenate([m, m], axis=1)


def right_stack(t):
    high, low = halves(t)
    return jnp.concatenate([high, low], axis=1)


def normalize(values):
    mean = jnp.sum(values, axis=-1, keepdims=True) * (1.0 / D)
    center = values - mean
    variance = jnp.sum(center * center, axis=-1, keepdims=True) * (1.0 / D)
    inverse = lax.rsqrt(variance + norm_eps)
    return center * inverse, inverse


def normalize_back(grad_out, normed, inverse, gain):
    scaled = grad_out * gain
    first = jnp.sum(scaled, axis=-1, keepdims=True) * (1.0 / D)
    second = jnp.sum(scaled * normed, axis=-1, keepdims=True) * (1.0 / D)
    grad_in = inverse * (scaled - first - normed * second)
    gain_grad = jnp.sum(grad_out * normed, axis=0, keepdims=True)
    shift_grad = jnp.sum(grad_out, axis=0, keepdims=True)
    return grad_in, gain_grad, shift_grad


def pack_reader(refs):
    return lambda r, k, lo, hi: refs[k][r, lo:hi, :]


def segment_row(seg_ref, chunk, span):
    return seg_ref[:, pl.ds(pl.multiple_of(chunk * span, span), span)].astype(f32)


def segment_column(seg_ref, chunk, span):
    return jnp.transpose(jnp.broadcast_to(segment_row(seg_ref, chunk, span), (TILE, span)))[:, 0:1]


def project_and_attend(c, h, wkv_ref, wqo_ref, seg_ref, kv_ref, qx_ref, att_ref, lse_ref):
    cols = h.shape[0]
    span = h.shape[1]
    wkv = wkv_ref[...]
    for j in range(cols):
        kv_ref[j * span:(j + 1) * span, :] = dot(h[j], wkv)
    h_own = h[0]
    qx_ref[...] = dot(h_own, wqo_ref[...])
    lane = lax.broadcasted_iota(jnp.int32, (span, TILE), 1)
    seg_row = jnp.concatenate([segment_row(seg_ref, c ^ k, span) for k in range(cols)], axis=1)
    allowed = segment_column(seg_ref, c, span) == seg_row
    lse_all = jnp.zeros((span, TILE), f32)
    for j in range(cols):
        tile = slice(j * TILE, (j + 1) * TILE)
        kv = kv_ref[:, tile]
        k_right = right_stack(dup_low(kv))
        v_dup = dup_high(kv)
        v_mix = mixed(v_dup)
        v_high = high_only(v_dup)
        q_left = left_stack(dup_low(qx_ref[:, tile]) * (HD ** -0.5))
        scores = jnp.where(allowed, dot1(q_left, k_right, NT), masked_score)
        top = jnp.max(scores, axis=-1, keepdims=True)
        raised = jnp.exp(scores - top)
        total = jnp.sum(raised, axis=-1, keepdims=True)
        p_high, p_low = halves(raised)
        out = dot1(p_high, v_mix) + dot1(p_low, v_high)
        out = (out + swap(out)) / total
        att_ref[:, tile] = jnp.where(low_lanes(span), 0.0, out)
        lse_all = jnp.where(lane == j, top + jnp.log(total), lse_all)
    lse_ref[...] = jnp.transpose(lse_all)[0:8, :]
    return dot(att_ref[...], wqo_ref[...], NT), h_own


def place_attention(rows, cols, block, at, wkv_ref, wqo_ref):
    for j in range(cols):
        for r in range(rows):
            piece = block(r, j, at, at + HD)
            wkv_ref[r * HD:(r + 1) * HD, j * TILE:(j + 1) * TILE] = piece[:, :TILE]
            wqo_ref[r * HD:(r + 1) * HD, j * TILE:(j + 1) * TILE] = piece[:, TILE:]


def place_feed(rows, cols, block, at, up_ref, dn_ref):
    for j in range(cols):
        for r in range(rows):
            to = (slice(r * HD, (r + 1) * HD), slice(j * 2 * TILE, (j + 1) * 2 * TILE))
            up_ref[to] = block(r, j, at, at + HD)
            dn_ref[to] = block(r, j, at + HD, at + 2 * HD)


def feed_forward(mid, up_ref, dn_ref, before_ref, act_ref):
    before = dot(mid, up_ref[...])
    before_ref[...] = before
    activated = 0.5 * before * (1.0 + lax.erf(before * 0.7071067811865476))
    act_ref[...] = activated
    return normalize(mid + dot(activated, dn_ref[...], NT))


def attention_kernel(rows, cols, idx_ref, seg_ref, *refs):
    c = idx_ref[0]
    packs, refs = refs[:cols], refs[cols:]
    h_out, wkv_out, wqo_out, kv_out, qx_out, att_out, lse_out, mid_out, n1_out, i1_out, params_out = refs
    block = pack_reader(packs)
    span = mid_out.shape[0]
    place_attention(rows, cols, block, 0, wkv_out, wqo_out)
    for j in range(cols):
        h_out[j] = jnp.transpose(
            jnp.concatenate([block(r, j, HD, 2 * HD) for r in range(rows)], axis=0)
        )
    tiles = []
    for t in range(rows // 2):
        a = block(2 * t, 0, 2 * HD, 2 * HD + 8)[:, 0:TILE]
        b = block(2 * t + 1, 0, 2 * HD, 2 * HD + 8)[:, 0:TILE]
        tiles.append(jnp.where(low_lanes(8), a, swap(b)))
    params_out[...] = jnp.concatenate(tiles, axis=1)
    branch, h_own = project_and_attend(
        c, h_out, wkv_out, wqo_out, seg_ref, kv_out, qx_out, att_out, lse_out
    )
    normed, inverse = normalize(h_own + branch)
    n1_out[...] = normed
    i1_out[...] = jnp.broadcast_to(inverse, (span, TILE))
    mid_out[...] = normed * params_out[0:1, :] + params_out[1:2, :]


def feed_kernel(rows, cols, mid_ref, ln_ref, *refs):
    packs, refs = refs[:cols], refs[cols:]
    h_out, up_out, dn_out, before_out, act_out, n2_out, i2_out = refs
    block = pack_reader(packs)
    place_feed(rows, cols, block, 0, up_out, dn_out)
    normed, inverse = feed_forward(mid_ref[...], up_out, dn_out, before_out, act_out)
    n2_out[...] = normed
    i2_out[...] = jnp.broadcast_to(inverse, i2_out.shape)
    h_out[...] = normed * ln_ref[2:3, :] + ln_ref[3:4, :]


def backward(
    c, dh, gains, seg_ref, wqo_ref, kv_ref, qx_ref, att_ref, lse_ref, n1, i1, up_ref, dn_ref,
    before_ref, n2, i2, dkv_ref, dqx_ref, dbef_ref, dv1_ref, dv2_ref, norm_ref
):
    span = n1.shape[0]
    cols = seg_ref.shape[1] // span
    dv2, gain2, shift2 = normalize_back(dh, n2, i2, gains[2])
    dv2_ref[...] = dv2
    d_act = dot(dv2, dn_ref[...])
    before = before_ref[...]
    slope = (
        0.5 * (1.0 + lax.erf(before * 0.7071067811865476))
        + before * jnp.exp(-0.5 * before * before) * 0.3989422804014327
    )
    dbef_ref[...] = d_act * slope
    d_mid = dv2 + dot(dbef_ref[...], up_ref[...], NT)
    dv1, gain1, shift1 = normalize_back(d_mid, n1, i1, gains[0])
    dv1_ref[...] = dv1
    norm_ref[...] = jnp.zeros_like(norm_ref)
    for k, row in enumerate((gain1, shift1, gain2, shift2)):
        norm_ref[k:k + 1, :] = row
    d_att = dot(dv1, wqo_ref[...])
    lane = lax.broadcasted_iota(jnp.int32, (span, TILE), 1)
    inner_all = jnp.zeros((span, TILE), f32)
    for j in range(cols):
        tile = slice(j * TILE, (j + 1) * TILE)
        inner = jnp.sum(d_att[:, tile] * att_ref[:, tile], axis=-1, keepdims=True)
        inner_all = jnp.where(lane == j, inner, inner_all)
    inner_rows = jnp.transpose(inner_all)
    seg_row = segment_row(seg_ref, c, span)
    seg_cols = [segment_column(seg_ref, c ^ b, span) for b in range(cols)]
    low = low_lanes(span)
    for j in range(cols):
        tile = slice(j * TILE, (j + 1) * TILE)
        q_dup = dup_low(qx_ref[:, tile]) * (HD ** -0.5)
        q_mix = mixed(q_dup)
        q_left = jnp.concatenate([q_mix, q_mix], axis=1)
        q_high = high_only(q_dup)
        do_dup = dup_high(d_att[:, tile])
        do_mix = mixed(do_dup)
        do_left = jnp.concatenate([do_mix, do_mix], axis=1)
        do_high = high_only(do_dup)
        lse_row = lse_ref[j:j + 1, :]
        inner_row = inner_rows[j:j + 1, :]
        dq_t = jnp.zeros((TILE, span), f32)
        for b in range(cols):
            keys = slice(b * span, (b + 1) * span)
            kv = kv_ref[keys, tile]
            k_dup = dup_low(kv)
            v_dup = dup_high(kv)
            scores = dot1(right_stack(k_dup), q_left, NT)
            shares = jnp.where(seg_cols[b] == seg_row, jnp.exp(scores - lse_row), 0.0)
            d_shares = dot1(right_stack(v_dup), do_left, NT)
            d_scores = shares * (d_shares - inner_row)
            p_high, p_low = halves(shares)
            s_high, s_low = halves(d_scores)
            dv = dot1(p_high, do_mix) + dot1(p_low, do_high)
            dk = dot1(s_high, q_mix) + dot1(s_low, q_high)
            dkv_ref[keys, tile] = jnp.where(low, dk + swap(dk), dv + swap(dv))
            k_t = jnp.transpose(k_dup)
            k_t_high = k_t.astype(bf16)
            upper = lax.broadcasted_iota(jnp.int32, (TILE, span), 0) < HD
            k_t_mix = jnp.where(upper, k_t_high.astype(f32), k_t - k_t_high.astype(f32)).astype(bf16)
            k_t_only = jnp.where(upper, k_t, 0.0).astype(bf16)
            dq_t = dq_t + dot1(k_t_mix, s_high) + dot1(k_t_only, s_low)
        dq = jnp.transpose(dq_t)
        dqx_ref[:, tile] = jnp.where(low, (dq + swap(dq)) * (HD ** -0.5), 0.0)


def input_gradient(wkv_ref, wqo_ref, dkv_ref, dqx_ref, dv1_ref, keep_out, send_out):
    span = dv1_ref.shape[0]
    wkv = wkv_ref[...]
    for k in (1, 3, 0, 2):
        part = dot(dkv_ref[k * span:(k + 1) * span, :], wkv, NT)
        if k == 0:
            part = part + dot(dqx_ref[...], wqo_ref[...], NT) + dv1_ref[...]
        (send_out if k % 2 else keep_out)[k // 2] = part


def weight_gradients(
    role, cols, h_ref, mid_ref, act_ref, att_ref, dkv_ref, dqx_ref, dbef_ref, dv1_ref, dv2_ref, norm_ref, grad_at
):
    span = dv1_ref.shape[0]

    @pl.when(role == 0)
    def _():
        mid = mid_ref[...]
        for k in range(cols):
            grad_at(k)[...] = dot(mid, dbef_ref[:, k * 2 * TILE:(k + 1) * 2 * TILE], TN)

    @pl.when(role == 1)
    def _():
        for k in range(cols):
            grad_at(k)[...] = dot(dv2_ref[...], act_ref[:, k * 2 * TILE:(k + 1) * 2 * TILE], TN)

    @pl.when(role == 2)
    def _():
        total = dot(h_ref[0], dkv_ref[0:span, :], TN)
        for b in range(1, cols):
            total += dot(h_ref[b], dkv_ref[b * span:(b + 1) * span, :], TN)
        for k in range(cols):
            grad_at(k)[:, 0:TILE] = total[:, k * TILE:(k + 1) * TILE]
            grad_at(k)[:, TILE:] = jnp.zeros((D, TILE), f32)

    @pl.when(role == 3)
    def _():
        total = dot(h_ref[0], dqx_ref[...], TN) + dot(dv1_ref[...], att_ref[...], TN)
        norms = jnp.transpose(norm_ref[...])
        for k in range(cols):
            grad_at(k)[:, 0:TILE] = total[:, k * TILE:(k + 1) * TILE]
            grad_at(k)[:, TILE:] = norms


def top_layer_kernel(rows, cols, idx_ref, ln_ref, seg_ref, *refs):
    c = idx_ref[0]
    packs, wide_packs, refs = refs[:cols], refs[cols:2 * cols], refs[2 * cols:]
    late_refs, h_refs, refs = refs[:rows], refs[rows:rows + cols], refs[rows + cols:]
    (out_ref, h_full, mid_ref, act_ref, att_ref, dkv_ref, dqx_ref, dbef_ref, dv1_ref, dv2_ref, norm_ref,
     keep_out, send_out, wkv_ref, wqo_ref, kv_ref, qx_ref, lse_ref, up_ref, dn_ref, before_ref) = refs
    place_attention(rows, cols, pack_reader(packs), 2 * HD, wkv_ref, wqo_ref)
    place_feed(rows, cols, pack_reader(wide_packs), 0, up_ref, dn_ref)
    for j in range(cols):
        h_full[j] = h_refs[j][...]
    gains = [ln_ref[k:k + 1, :] for k in range(4, 8)]
    branch, h_own = project_and_attend(
        c, h_full, wkv_ref, wqo_ref, seg_ref, kv_ref, qx_ref, att_ref, lse_ref
    )
    n1, i1 = normalize(h_own + branch)
    mid_ref[...] = n1 * gains[0] + gains[1]
    n2, i2 = feed_forward(mid_ref[...], up_ref, dn_ref, before_ref, act_ref)
    out_ref[...] = n2 * gains[2] + gains[3]
    dh = jnp.transpose(jnp.concatenate([ref[2 * HD:, :] for ref in late_refs], axis=0))
    backward(
        c, dh, gains, seg_ref, wqo_ref, kv_ref, qx_ref, att_ref, lse_ref, n1, i1, up_ref, dn_ref,
        before_ref, n2, i2, dkv_ref, dqx_ref, dbef_ref, dv1_ref, dv2_ref, norm_ref
    )
    input_gradient(wkv_ref, wqo_ref, dkv_ref, dqx_ref, dv1_ref, keep_out, send_out)


def add_moment(idx_ref, late_refs, big, at):
    first = 0 if big else HD

    @pl.when(idx_ref[2] == 0)
    def _():
        for r, ref in enumerate(late_refs):
            at[r * HD:(r + 1) * HD, :] += ref[first:first + HD, :]


def top_gradients_kernel(rows, cols, idx_ref, *refs):
    z = idx_ref[1]
    late_refs, refs = refs[:rows], refs[rows:]
    keep_out, send_out = refs[-2:]
    weight_gradients(z, cols, *refs[:-2], lambda k: (send_out if k % 2 else keep_out).at[k // 2])
    for big in (True, False):

        @pl.when((z < 2) == big)
        def _():
            add_moment(idx_ref, late_refs, big, keep_out.at[0])


def low_layer_kernel(rows, cols, idx_ref, ln_ref, seg_ref, *refs):
    late_refs, refs = refs[:rows], refs[rows:]
    z = idx_ref[1]
    (dh_keep, dh_got, dh_across, h_ref, mid_ref, act_ref, wqo_ref, kv_ref, qx_ref, att_ref, lse_ref, n1_ref,
     i1_ref, up_ref, dn_ref, before_ref, n2_ref, i2_ref, keep_out, send_out, dkv_ref, dqx_ref, dv1_ref,
     dbef_ref, dv2_ref, norm_ref) = refs
    dh = dh_keep[0] + dh_got[0] + dh_across[...]
    gains = [ln_ref[k:k + 1, :] for k in range(4)]
    backward(
        idx_ref[0], dh, gains, seg_ref, wqo_ref, kv_ref, qx_ref, att_ref, lse_ref, n1_ref[...],
        i1_ref[:, 0:1], up_ref, dn_ref, before_ref, n2_ref[...], i2_ref[:, 0:1], dkv_ref, dqx_ref, dbef_ref,
        dv1_ref, dv2_ref, norm_ref
    )
    weight_gradients(
        z ^ 2, cols, h_ref, mid_ref, act_ref, att_ref, dkv_ref, dqx_ref, dbef_ref, dv1_ref, dv2_ref, norm_ref,
        lambda k: (send_out if k % 2 else keep_out).at[k // 2]
    )
    for big in (True, False):

        @pl.when((z >= 2) == big)
        def _():
            add_moment(idx_ref, late_refs, big, keep_out.at[0])


def low_input_kernel(*refs):
    input_gradient(*refs)


def symmetric(high, low, dims):
    return dot1(high, high, dims) + (dot1(high, low, dims) + dot1(low, high, dims))


def newton_schulz(blocks, wanted):
    sizes = [jnp.sum(x * x, keepdims=True) for x in blocks]
    blocks = [x / (jnp.sqrt(s) + frob_eps) for x, s in zip(blocks, sizes)]
    for step in range(NS_STEPS):
        parts = [halves(x) for x in blocks]
        grams = [symmetric(h, l, NT) for h, l in parts]
        squares = [symmetric(*halves(a), NN) for a in grams]
        polys = [halves(newton_coefs[1] * a + newton_coefs[2] * s) for a, s in zip(grams, squares)]
        if step == NS_STEPS - 1:
            blocks = [x[:, :n] for x, n in zip(blocks, wanted)]
            parts = [(h[:, :n], l[:, :n]) for (h, l), n in zip(parts, wanted)]
        blocks = [
            newton_coefs[0] * x + (dot1(ph, h) + dot1(ph, l) + dot1(pl_, h))
            for x, (h, l), (ph, pl_) in zip(blocks, parts, polys)
        ]
    return blocks


def orthogonal_kernel(cols, idx_ref, *refs):
    z = idx_ref[1]
    top_refs, low_refs = refs[:cols], refs[cols:2 * cols]
    big_out, small_out, big, small = refs[2 * cols:]

    @pl.when(z < 2)
    def _():
        for k in range(cols):
            big[:, k * 2 * TILE:(k + 1) * 2 * TILE] = top_refs[k][...]
            small[:, k * TILE:(k + 1) * TILE] = low_refs[k][:, 0:TILE]

    @pl.when(z >= 2)
    def _():
        for k in range(cols):
            big[:, k * 2 * TILE:(k + 1) * 2 * TILE] = low_refs[k][...]
            small[:, k * TILE:(k + 1) * TILE] = top_refs[k][:, 0:TILE]

    low = low_lanes(D)
    lefts, rights = [], []
    for t in range(cols // 2):
        a = small[:, 2 * t * TILE:(2 * t + 1) * TILE]
        b = small[:, (2 * t + 1) * TILE:(2 * t + 2) * TILE]
        lefts.append(jnp.where(low, a, swap(b)))
        rights.append(jnp.where(low, swap(a), b))
    wide, left, right = newton_schulz(
        [big[...], jnp.concatenate(lefts, axis=1), jnp.concatenate(rights, axis=1)], (2 * TILE, TILE, TILE)
    )
    big_out[...] = wide * math.sqrt(FF)
    small_out[...] = jnp.where(low, left, swap(right)) * math.sqrt(D)


def first_pack_kernel(heads_hbm, outs_hbm, x_hbm, params_hbm, shard_out, heads_ref, outs_ref, params_ref, sems):
    shard_out[2 * HD:, :] = jnp.zeros((8, 2 * TILE), f32)
    copies = [
        pltpu.make_async_copy(source, target, sems.at[i])
        for i, (source, target) in enumerate(
            (
                (heads_hbm.at[0], heads_ref),
                (outs_hbm.at[0], outs_ref),
                (params_hbm, params_ref),
                (x_hbm, shard_out.at[pl.ds(HD, HD)]),
            )
        )
    ]
    for copy in copies:
        copy.start()
    for copy in copies:
        copy.wait()
    shard_out[0:HD, 0:HD] = heads_ref[1]
    shard_out[0:HD, HD:TILE] = heads_ref[2]
    shard_out[0:HD, TILE:TILE + HD] = heads_ref[0]
    shard_out[0:HD, TILE + HD:] = jnp.transpose(outs_ref[...])
    shard_out[2 * HD:, 0:HD] = params_ref[...]


def pack_kernel(
    rows, idx_ref, heads_ref, outs_ref, up_ref, dn_ref, og_ref, mh_ref, mo_ref, mu_ref, md_ref, f_out, b_out, *refs
):
    z = idx_ref[1]
    late_outs, moments = refs[:rows], refs[rows]
    f_out[0:HD, :] = up_ref[0]
    f_out[HD:2 * HD, :] = dn_ref[0]
    f_out[2 * HD:, 0:HD] = heads_ref[1, 1]
    f_out[2 * HD:, HD:TILE] = heads_ref[1, 2]
    f_out[2 * HD:, TILE:TILE + HD] = heads_ref[1, 0]
    f_out[2 * HD:, TILE + HD:] = jnp.transpose(outs_ref[1])
    b_out[0:HD, :] = up_ref[1]
    b_out[HD:2 * HD, :] = dn_ref[1]
    b_out[2 * HD:, :] = og_ref[...]
    for l in range(LAYERS):
        large, small = (0, 2) if l else (2, 0)
        moments[large, 0:HD, :] = mu_ref[l] * muon_decay
        moments[large + 1, 0:HD, :] = md_ref[l] * muon_decay
        moments[small, HD:, 0:HD] = mh_ref[l, 1] * muon_decay
        moments[small, HD:, HD:TILE] = mh_ref[l, 2] * muon_decay
        moments[small + 1, HD:, 0:HD] = mh_ref[l, 0] * muon_decay
        moments[small + 1, HD:, HD:TILE] = jnp.transpose(mo_ref[l]) * muon_decay
    for r in range(rows):
        moments[r, HD:, TILE:] = jnp.zeros((HD, TILE), f32)
    for k in range(rows):
        late_outs[k][...] = moments[z ^ k]


def update_kernel(
    rows, idx_ref, heads_ref, outs_ref, up_ref, dn_ref, params_ref, first_ref, second_ref, *refs
):
    z = idx_ref[1]
    mom_refs, step_refs, refs = refs[:rows], refs[rows:2 * rows], refs[2 * rows:]
    (heads_out, outs_out, up_out, dn_out, mh_out, mo_out, mu_out, md_out, first_out, second_out, params_out,
     mom, step) = refs
    for k in range(rows):
        mom[z ^ k] = mom_refs[k][...]
        step[z ^ k] = step_refs[k][...] * muon_rate
    for l in range(LAYERS):
        large, small = (0, 2) if l else (2, 0)
        mu_out[l] = mom[large, 0:HD, :]
        md_out[l] = mom[large + 1, 0:HD, :]
        up_out[l] = up_ref[l] - D ** -0.5 * step[large, :, 0:2 * TILE]
        dn_out[l] = dn_ref[l] - FF ** -0.5 * step[large + 1, :, 0:2 * TILE]
        kv, qo = mom[small, HD:, 0:TILE], mom[small + 1, HD:, 0:TILE]
        mh_out[l, 0] = qo[:, 0:HD]
        mh_out[l, 1] = kv[:, 0:HD]
        mh_out[l, 2] = swap(kv)[:, 0:HD]
        mo_out[l] = jnp.transpose(swap(qo))[0:HD, :]
        kv, qo = step[small, :, 2 * TILE:], step[small + 1, :, 2 * TILE:]
        heads_out[l, 0] = heads_ref[l, 0] - D ** -0.5 * qo[:, 0:HD]
        heads_out[l, 1] = heads_ref[l, 1] - D ** -0.5 * kv[:, 0:HD]
        heads_out[l, 2] = heads_ref[l, 2] - D ** -0.5 * swap(kv)[:, 0:HD]
        outs_out[l] = outs_ref[l] - (D // 16) ** -0.5 * jnp.transpose(swap(qo))[0:HD, :]
        grad = jnp.transpose(mom[small + 1, HD:, TILE:])[0:4, :]
        first = adam_first * first_ref[l] + (1.0 - adam_first) * grad
        second = adam_second * second_ref[l] + (1.0 - adam_second) * grad * grad
        first_out[l] = first
        second_out[l] = second
        params_out[l] = params_ref[l] - adam_rate * (first / (1.0 - adam_first**STEP)) / (
            jnp.sqrt(second / (1.0 - adam_second**STEP)) + adam_eps
        )


def call(body, operands, outs, scratch=(), flops=0, vmem=50):
    specs = [pl.BlockSpec(memory_space=pltpu.SMEM if x.ndim == 1 else pltpu.VMEM) for x in operands]
    moved = sum(4 * math.prod(x.shape) for x in operands) + sum(4 * math.prod(s) for s in outs)
    return pl.pallas_call(
        body,
        out_shape=[jax.ShapeDtypeStruct(s, f32) for s in outs],
        in_specs=specs,
        out_specs=[pl.BlockSpec(memory_space=pltpu.VMEM) for _ in outs],
        scratch_shapes=[pltpu.VMEM(s, f32) for s in scratch],
        compiler_params=pltpu.CompilerParams(vmem_limit_bytes=vmem * 2**20),
        cost_estimate=pl.CostEstimate(flops=flops, bytes_accessed=moved if flops else 0, transcendentals=0),
    )(*operands)


def fetched_call(body, idx, operands, outs, scratch):
    count, given = len(operands), len(outs) + len(scratch)

    def kernel(idx_ref, *refs):
        sources, rest, held, sems = refs[:count], refs[count:count + given], refs[count + given:-1], refs[-1]
        copies = [pltpu.make_async_copy(a, b, sems.at[i]) for i, (a, b) in enumerate(zip(sources, held))]
        for copy in copies:
            copy.start()
        for copy in copies:
            copy.wait()
        body(idx_ref, *held, *rest)

    return pl.pallas_call(
        kernel,
        out_shape=[jax.ShapeDtypeStruct(s, f32) for s in outs],
        in_specs=[pl.BlockSpec(memory_space=pltpu.SMEM)] + [pl.BlockSpec(memory_space=pltpu.HBM)] * count,
        out_specs=[pl.BlockSpec(memory_space=pltpu.VMEM) for _ in outs],
        scratch_shapes=[pltpu.VMEM(s, f32) for s in scratch]
        + [pltpu.VMEM(x.shape, f32) for x in operands] + [pltpu.SemaphoreType.DMA((count,))],
        compiler_params=pltpu.CompilerParams(vmem_limit_bytes=56 * 2**20),
    )(idx, *operands)


def on_device(
    layer_input,
    segment_ids,
    head_projection_weights,
    output_projection_weights,
    up_projection_weights,
    down_projection_weights,
    head_moment,
    out_moment,
    up_moment,
    down_moment,
    norm_params,
    norm_first,
    norm_second,
    output_grad,
):
    row = lax.axis_index("row").astype(jnp.int32)
    col = lax.axis_index("col").astype(jnp.int32)
    rows = lax.axis_size("row")
    cols = lax.axis_size("col")
    dps = lax.axis_size("dp")
    span = layer_input.shape[1]
    length = span * cols
    idx = jnp.stack([col, row, lax.axis_index("dp").astype(jnp.int32)])
    swap2 = lambda x: jnp.swapaxes(x, -1, -2)

    def perm(x, axis, bit):
        return lax.ppermute(x, axis, [(i, i ^ bit) for i in range(lax.axis_size(axis))])

    def spread_cols(x):
        across = perm(x, "col", 2)
        return [x, perm(x, "col", 1), across, perm(across, "col", 1)]

    def spread_rows(parts):
        return [parts[0]] + [perm(parts[k], "row", k) for k in range(1, rows)]

    heads, outs, ups = head_projection_weights, output_projection_weights, up_projection_weights
    downs = swap2(down_projection_weights)
    shard_a = pl.pallas_call(
        first_pack_kernel,
        out_shape=jax.ShapeDtypeStruct((2 * HD + 8, D), f32),
        in_specs=[pl.BlockSpec(memory_space=pltpu.HBM)] * 4,
        out_specs=pl.BlockSpec(memory_space=pltpu.VMEM),
        scratch_shapes=[
            pltpu.VMEM((3, HD, HD), f32), pltpu.VMEM((HD, HD), f32), pltpu.VMEM((8, HD), f32), pltpu.SemaphoreType.DMA((4,)),
        ],
        compiler_params=pltpu.CompilerParams(vmem_limit_bytes=60 * 2**20),
    )(heads, outs, swap2(layer_input[0]), norm_params.reshape(8, HD))
    shard_f, shard_b, *moments = fetched_call(
        functools.partial(pack_kernel, rows),
        idx, [heads, outs, ups, downs, swap2(output_grad[0]), head_moment, out_moment, up_moment, swap2(down_moment)],
        [(3 * HD, D), (3 * HD, D)] + [(2 * HD, D)] * rows, [(rows, 2 * HD, D)],
    )
    pieces = spread_rows([shard_a] * rows)
    *pieces, shard_f = lax.optimization_barrier((*pieces, shard_f))
    mine_a = jnp.stack(pieces)
    across_a, core_a = perm(mine_a, "col", 2), perm(mine_a, "col", 1)
    shard_f, _ = lax.optimization_barrier((shard_f, core_a))
    pieces_f = spread_rows([shard_f] * rows)
    mine_f = jnp.stack(pieces_f)
    across_a, mine_f = lax.optimization_barrier((across_a, mine_f))
    packs_a = [mine_a, core_a, across_a, perm(across_a, "col", 1)]
    across_f = perm(mine_f, "col", 2)
    shard_b, _ = lax.optimization_barrier((shard_b, pieces_f[1]))
    pieces_b = spread_rows([shard_b] * rows)

    full = (cols, span, D)
    pair = (2, span, D)
    own = (span, D)
    wide = (span, FF)
    half = (D, cols * TILE)
    keys = (length, cols * TILE)
    queries = (span, cols * TILE)
    one = (span, TILE)
    stats = (8, span)
    norms = (TILE, D)
    segs = [segment_ids]

    h_full, wkv, wqo, kv, qx, att, lse, mid, n1, i1, ln = call(
        functools.partial(attention_kernel, rows, cols),
        [idx] + segs + packs_a,
        [full, half, half, keys, queries, queries, stats, own, own, one, (8, D)], flops=5 * 10**9, vmem=12,
    )
    mid, across_f, *rest = lax.optimization_barrier((mid, across_f, *moments, *pieces_b))
    moments, pieces_b = rest[:rows], rest[rows:]
    packs_f = [mine_f, perm(mine_f, "col", 1), across_f, perm(across_f, "col", 1)]
    moments = spread_rows(moments)
    h_own, up, dn, before, act, n2, i2 = call(
        functools.partial(feed_kernel, rows, cols),
        [mid, ln] + packs_f,
        [own, (D, FF), (D, FF), wide, wide, own, one], flops=2 * 10**9, vmem=8,
    )
    hidden = spread_cols(h_own)
    mine_b = jnp.stack([x[:2 * HD] for x in pieces_b])
    across_b = perm(mine_b, "col", 2)
    across_b, hidden[2], *moments = lax.optimization_barrier((across_b, hidden[2], *moments))
    packs_b = [mine_b, perm(mine_b, "col", 1), across_b, perm(across_b, "col", 1)]
    top, *saved, keep, send = call(
        functools.partial(top_layer_kernel, rows, cols),
        [idx, ln] + segs + packs_f + packs_b + pieces_b + hidden,
        [own, full, own, wide, queries, keys, queries, wide, own, own, norms, pair, pair],
        [half, half, keys, queries, stats, (D, FF), (D, FF), wide], flops=20 * 10**9, vmem=18,
    )
    layer_output = top[:, :HD][None]

    def fold_core(keep, send):
        got = perm(send, "col", 1)
        return got, perm(keep[1] + got[1], "col", 2)

    got, across = fold_core(keep, send)
    keep_t, send_t = call(
        functools.partial(top_gradients_kernel, rows, cols), [idx] + moments + saved, [pair, pair],
        flops=2 * 10**9, vmem=6,
    )
    got_t = perm(send_t, "col", 1)
    half_t = keep_t[1] + got_t[1]
    got, half_t = lax.optimization_barrier((got, half_t))
    across_t = perm(half_t, "col", 2)
    keep_g, send_g, dkv, dqx, dv1 = call(
        functools.partial(low_layer_kernel, rows, cols),
        [idx, ln] + segs + moments
        + [keep, got, across, h_full, mid, act, wqo, kv, qx, att, lse, n1, i1, up, dn, before, n2, i2],
        [pair, pair, keys, queries, own], [wide, own, norms], flops=12 * 10**9, vmem=12,
    )
    send_g, across_t = lax.optimization_barrier((send_g, across_t))
    got, across = fold_core(keep_g, send_g)
    mine = keep_g[0] + got[0] + across
    top = keep_t[0] + got_t[0] + across_t
    top, mine = [
        lax.optimization_barrier(x + perm(x, "dp", 1) if dps == 2 else lax.psum(x, "dp")) for x in (top, mine)
    ]
    keep, send = call(
        low_input_kernel, [wkv, wqo, dkv, dqx, dv1], [pair, pair], flops=2 * 10**9, vmem=6,
    )
    got, across = fold_core(keep, send)
    input_grad = (keep[0] + got[0] + across)[:, :HD][None]

    tops, parts = spread_cols(top), spread_cols(mine)
    large, small = jnp.where(row < 2, top, mine), jnp.where(row < 2, mine, top)
    moms = jnp.concatenate([large.reshape(rows, HD, D), small.reshape(rows, HD, D)], axis=1)
    moms = spread_rows([moms[k] for k in range(rows)])
    large, small = call(
        functools.partial(orthogonal_kernel, cols), [idx] + tops + parts, [own, (D, TILE)],
        [(D, FF), (D, cols * TILE)], flops=8 * 10**9, vmem=16,
    )
    steps = jnp.concatenate([large.reshape(rows, HD, D), small.reshape(rows, HD, TILE)], axis=2)
    steps = spread_rows([steps[k] for k in range(rows)])
    three = (LAYERS, 4, HD)
    updates = list(call(
        functools.partial(update_kernel, rows),
        [idx, heads, outs, ups, downs, norm_params, norm_first, norm_second] + moms + steps,
        [heads.shape, outs.shape, ups.shape, downs.shape] * 2 + [three] * 3,
        [(rows, 2 * HD, D), (rows, HD, D + TILE)], vmem=8,
    ))
    for at in (3, 7):
        updates[at] = swap2(updates[at])
    return (layer_output, input_grad, *updates)


def solution(mesh):
    placed = (
        P("dp", "col", "row"),
        P("dp", None),
        P(None, None, "row", "col"),
        P(None, "col", "row"),
        P(None, "row", "col"),
        P(None, "col", "row"),
        P(None, None, "row", "col"),
        P(None, "col", "row"),
        P(None, "row", "col"),
        P(None, "col", "row"),
        P(None, None, "row"),
        P(None, None, "row"),
        P(None, None, "row"),
        P("dp", "col", "row"),
    )
    return jax.shard_map(
        on_device,
        mesh=mesh,
        in_specs=placed,
        out_specs=(
            P("dp", "col", "row"),
            P("dp", "col", "row"),
            P(None, None, "row", "col"),
            P(None, "col", "row"),
            P(None, "row", "col"),
            P(None, "col", "row"),
            P(None, None, "row", "col"),
            P(None, "col", "row"),
            P(None, "row", "col"),
            P(None, "col", "row"),
            P(None, None, "row"),
            P(None, None, "row"),
            P(None, None, "row"),
        ),
        check_vma=False,
    )
```

```python
import functools
import math

import jax
import jax.numpy as jnp
from jax import lax
from jax.experimental import pallas as pl
from jax.experimental.pallas import tpu as pltpu
from jax.sharding import PartitionSpec as P

D = 256
FF = 1024
LAYERS = 2
NS_STEPS = 5
STEP = 10
HD = 64
TILE = 128

norm_eps = 1e-05
newton_coefs = (3.4445, -4.775, 2.0315)
frob_eps = 1e-07
muon_decay = 0.95
muon_rate = 0.5
adam_first = 0.9
adam_second = 0.999
adam_eps = 1e-08
adam_rate = 0.2
masked_score = -1e30

f32 = jnp.float32
bf16 = jnp.bfloat16

NN = (((1,), (0,)), ((), ()))
NT = (((1,), (1,)), ((), ()))
TN = (((0,), (0,)), ((), ()))


def dot(a, b, dims=NN):
    return lax.dot_general(a, b, dims, precision=lax.Precision.HIGH, preferred_element_type=f32)


def dot1(a, b, dims=NN):
    return lax.dot_general(a, b, dims, preferred_element_type=f32)


def low_lanes(rows):
    return lax.broadcasted_iota(jnp.int32, (rows, TILE), 1) < HD


def swap(t):
    return pltpu.roll(t, HD, 1)


def dup_low(t):
    return jnp.where(low_lanes(t.shape[0]), t, swap(t))


def dup_high(t):
    return jnp.where(low_lanes(t.shape[0]), swap(t), t)


def halves(t):
    high = t.astype(bf16)
    return high, (t - high.astype(f32)).astype(bf16)


def mixed(t):
    high = t.astype(bf16).astype(f32)
    return jnp.where(low_lanes(t.shape[0]), high, t - high).astype(bf16)


def high_only(t):
    return jnp.where(low_lanes(t.shape[0]), t, 0.0).astype(bf16)


def left_stack(t):
    m = mixed(t)
    return jnp.concatenate([m, m], axis=1)


def right_stack(t):
    high, low = halves(t)
    return jnp.concatenate([high, low], axis=1)


def normalize(values):
    mean = jnp.sum(values, axis=-1, keepdims=True) * (1.0 / D)
    center = values - mean
    variance = jnp.sum(center * center, axis=-1, keepdims=True) * (1.0 / D)
    inverse = lax.rsqrt(variance + norm_eps)
    return center * inverse, inverse


def normalize_back(grad_out, normed, inverse, gain):
    scaled = grad_out * gain
    first = jnp.sum(scaled, axis=-1, keepdims=True) * (1.0 / D)
    second = jnp.sum(scaled * normed, axis=-1, keepdims=True) * (1.0 / D)
    grad_in = inverse * (scaled - first - normed * second)
    gain_grad = jnp.sum(grad_out * normed, axis=0, keepdims=True)
    shift_grad = jnp.sum(grad_out, axis=0, keepdims=True)
    return grad_in, gain_grad, shift_grad


def pack_reader(refs):
    return lambda r, k, lo, hi: refs[k][r, lo:hi, :]


def segment_row(seg_ref, chunk, span):
    return seg_ref[:, pl.ds(pl.multiple_of(chunk * span, span), span)].astype(f32)


def segment_column(seg_ref, chunk, span):
    return jnp.transpose(jnp.broadcast_to(segment_row(seg_ref, chunk, span), (TILE, span)))[:, 0:1]


def project_and_attend(c, h, wkv_ref, wqo_ref, seg_ref, kv_ref, qx_ref, att_ref, lse_ref):
    cols = h.shape[0]
    span = h.shape[1]
    wkv = wkv_ref[...]
    for j in range(cols):
        kv_ref[j * span:(j + 1) * span, :] = dot(h[j], wkv)
    h_own = h[0]
    qx_ref[...] = dot(h_own, wqo_ref[...])
    lane = lax.broadcasted_iota(jnp.int32, (span, TILE), 1)
    seg_row = jnp.concatenate([segment_row(seg_ref, c ^ k, span) for k in range(cols)], axis=1)
    allowed = segment_column(seg_ref, c, span) == seg_row
    lse_all = jnp.zeros((span, TILE), f32)
    for j in range(cols):
        tile = slice(j * TILE, (j + 1) * TILE)
        kv = kv_ref[:, tile]
        k_right = right_stack(dup_low(kv))
        v_dup = dup_high(kv)
        v_mix = mixed(v_dup)
        v_high = high_only(v_dup)
        q_left = left_stack(dup_low(qx_ref[:, tile]) * (HD ** -0.5))
        scores = jnp.where(allowed, dot1(q_left, k_right, NT), masked_score)
        top = jnp.max(scores, axis=-1, keepdims=True)
        raised = jnp.exp(scores - top)
        total = jnp.sum(raised, axis=-1, keepdims=True)
        p_high, p_low = halves(raised)
        out = dot1(p_high, v_mix) + dot1(p_low, v_high)
        out = (out + swap(out)) / total
        att_ref[:, tile] = jnp.where(low_lanes(span), 0.0, out)
        lse_all = jnp.where(lane == j, top + jnp.log(total), lse_all)
    lse_ref[...] = jnp.transpose(lse_all)[0:8, :]
    return dot(att_ref[...], wqo_ref[...], NT), h_own


def place_attention(rows, cols, block, at, wkv_ref, wqo_ref):
    for j in range(cols):
        for r in range(rows):
            piece = block(r, j, at, at + HD)
            wkv_ref[r * HD:(r + 1) * HD, j * TILE:(j + 1) * TILE] = piece[:, :TILE]
            wqo_ref[r * HD:(r + 1) * HD, j * TILE:(j + 1) * TILE] = piece[:, TILE:]


def place_feed(rows, cols, block, at, up_ref, dn_ref):
    for j in range(cols):
        for r in range(rows):
            to = (slice(r * HD, (r + 1) * HD), slice(j * 2 * TILE, (j + 1) * 2 * TILE))
            up_ref[to] = block(r, j, at, at + HD)
            dn_ref[to] = block(r, j, at + HD, at + 2 * HD)


def feed_forward(mid, up_ref, dn_ref, before_ref, act_ref):
    before = dot(mid, up_ref[...])
    before_ref[...] = before
    activated = 0.5 * before * (1.0 + lax.erf(before * 0.7071067811865476))
    act_ref[...] = activated
    return normalize(mid + dot(activated, dn_ref[...], NT))


def attention_kernel(rows, cols, idx_ref, seg_ref, *refs):
    c = idx_ref[0]
    packs, refs = refs[:cols], refs[cols:]
    h_out, wkv_out, wqo_out, kv_out, qx_out, att_out, lse_out, mid_out, n1_out, i1_out, params_out = refs
    block = pack_reader(packs)
    span = mid_out.shape[0]
    place_attention(rows, cols, block, 0, wkv_out, wqo_out)
    for j in range(cols):
        h_out[j] = jnp.transpose(
            jnp.concatenate([block(r, j, HD, 2 * HD) for r in range(rows)], axis=0)
        )
    tiles = []
    for t in range(rows // 2):
        a = block(2 * t, 0, 2 * HD, 2 * HD + 8)[:, 0:TILE]
        b = block(2 * t + 1, 0, 2 * HD, 2 * HD + 8)[:, 0:TILE]
        tiles.append(jnp.where(low_lanes(8), a, swap(b)))
    params_out[...] = jnp.concatenate(tiles, axis=1)
    branch, h_own = project_and_attend(
        c, h_out, wkv_out, wqo_out, seg_ref, kv_out, qx_out, att_out, lse_out
    )
    normed, inverse = normalize(h_own + branch)
    n1_out[...] = normed
    i1_out[...] = jnp.broadcast_to(inverse, (span, TILE))
    mid_out[...] = normed * params_out[0:1, :] + params_out[1:2, :]


def feed_kernel(rows, cols, mid_ref, ln_ref, *refs):
    packs, refs = refs[:cols], refs[cols:]
    h_out, up_out, dn_out, before_out, act_out, n2_out, i2_out = refs
    block = pack_reader(packs)
    place_feed(rows, cols, block, 0, up_out, dn_out)
    normed, inverse = feed_forward(mid_ref[...], up_out, dn_out, before_out, act_out)
    n2_out[...] = normed
    i2_out[...] = jnp.broadcast_to(inverse, i2_out.shape)
    h_out[...] = normed * ln_ref[2:3, :] + ln_ref[3:4, :]


def backward(
    c, dh, gains, seg_ref, wqo_ref, kv_ref, qx_ref, att_ref, lse_ref, n1, i1, up_ref, dn_ref,
    before_ref, n2, i2, dkv_ref, dqx_ref, dbef_ref, dv1_ref, dv2_ref, norm_ref
):
    span = n1.shape[0]
    cols = seg_ref.shape[1] // span
    dv2, gain2, shift2 = normalize_back(dh, n2, i2, gains[2])
    dv2_ref[...] = dv2
    d_act = dot(dv2, dn_ref[...])
    before = before_ref[...]
    slope = (
        0.5 * (1.0 + lax.erf(before * 0.7071067811865476))
        + before * jnp.exp(-0.5 * before * before) * 0.3989422804014327
    )
    dbef_ref[...] = d_act * slope
    d_mid = dv2 + dot(dbef_ref[...], up_ref[...], NT)
    dv1, gain1, shift1 = normalize_back(d_mid, n1, i1, gains[0])
    dv1_ref[...] = dv1
    norm_ref[...] = jnp.zeros_like(norm_ref)
    for k, row in enumerate((gain1, shift1, gain2, shift2)):
        norm_ref[k:k + 1, :] = row
    d_att = dot(dv1, wqo_ref[...])
    lane = lax.broadcasted_iota(jnp.int32, (span, TILE), 1)
    inner_all = jnp.zeros((span, TILE), f32)
    for j in range(cols):
        tile = slice(j * TILE, (j + 1) * TILE)
        inner = jnp.sum(d_att[:, tile] * att_ref[:, tile], axis=-1, keepdims=True)
        inner_all = jnp.where(lane == j, inner, inner_all)
    inner_rows = jnp.transpose(inner_all)
    seg_row = segment_row(seg_ref, c, span)
    seg_cols = [segment_column(seg_ref, c ^ b, span) for b in range(cols)]
    low = low_lanes(span)
    for j in range(cols):
        tile = slice(j * TILE, (j + 1) * TILE)
        q_dup = dup_low(qx_ref[:, tile]) * (HD ** -0.5)
        q_mix = mixed(q_dup)
        q_left = jnp.concatenate([q_mix, q_mix], axis=1)
        q_high = high_only(q_dup)
        do_dup = dup_high(d_att[:, tile])
        do_mix = mixed(do_dup)
        do_left = jnp.concatenate([do_mix, do_mix], axis=1)
        do_high = high_only(do_dup)
        lse_row = lse_ref[j:j + 1, :]
        inner_row = inner_rows[j:j + 1, :]
        dq_t = jnp.zeros((TILE, span), f32)
        for b in range(cols):
            keys = slice(b * span, (b + 1) * span)
            kv = kv_ref[keys, tile]
            k_dup = dup_low(kv)
            v_dup = dup_high(kv)
            scores = dot1(right_stack(k_dup), q_left, NT)
            shares = jnp.where(seg_cols[b] == seg_row, jnp.exp(scores - lse_row), 0.0)
            d_shares = dot1(right_stack(v_dup), do_left, NT)
            d_scores = shares * (d_shares - inner_row)
            p_high, p_low = halves(shares)
            s_high, s_low = halves(d_scores)
            dv = dot1(p_high, do_mix) + dot1(p_low, do_high)
            dk = dot1(s_high, q_mix) + dot1(s_low, q_high)
            dkv_ref[keys, tile] = jnp.where(low, dk + swap(dk), dv + swap(dv))
            k_t = jnp.transpose(k_dup)
            k_t_high = k_t.astype(bf16)
            upper = lax.broadcasted_iota(jnp.int32, (TILE, span), 0) < HD
            k_t_mix = jnp.where(upper, k_t_high.astype(f32), k_t - k_t_high.astype(f32)).astype(bf16)
            k_t_only = jnp.where(upper, k_t, 0.0).astype(bf16)
            dq_t = dq_t + dot1(k_t_mix, s_high) + dot1(k_t_only, s_low)
        dq = jnp.transpose(dq_t)
        dqx_ref[:, tile] = jnp.where(low, (dq + swap(dq)) * (HD ** -0.5), 0.0)


def input_gradient(wkv_ref, wqo_ref, dkv_ref, dqx_ref, dv1_ref, keep_out, send_out):
    span = dv1_ref.shape[0]
    wkv = wkv_ref[...]
    for k in (1, 3, 0, 2):
        part = dot(dkv_ref[k * span:(k + 1) * span, :], wkv, NT)
        if k == 0:
            part = part + dot(dqx_ref[...], wqo_ref[...], NT) + dv1_ref[...]
        (send_out if k % 2 else keep_out)[k // 2] = part


def weight_gradients(
    role, cols, h_ref, mid_ref, act_ref, att_ref, dkv_ref, dqx_ref, dbef_ref, dv1_ref, dv2_ref, norm_ref, grad_at
):
    span = dv1_ref.shape[0]

    @pl.when(role == 0)
    def _():
        mid = mid_ref[...]
        for k in range(cols):
            grad_at(k)[...] = dot(mid, dbef_ref[:, k * 2 * TILE:(k + 1) * 2 * TILE], TN)

    @pl.when(role == 1)
    def _():
        for k in range(cols):
            grad_at(k)[...] = dot(dv2_ref[...], act_ref[:, k * 2 * TILE:(k + 1) * 2 * TILE], TN)

    @pl.when(role == 2)
    def _():
        total = dot(h_ref[0], dkv_ref[0:span, :], TN)
        for b in range(1, cols):
            total += dot(h_ref[b], dkv_ref[b * span:(b + 1) * span, :], TN)
        for k in range(cols):
            grad_at(k)[:, 0:TILE] = total[:, k * TILE:(k + 1) * TILE]
            grad_at(k)[:, TILE:] = jnp.zeros((D, TILE), f32)

    @pl.when(role == 3)
    def _():
        total = dot(h_ref[0], dqx_ref[...], TN) + dot(dv1_ref[...], att_ref[...], TN)
        norms = jnp.transpose(norm_ref[...])
        for k in range(cols):
            grad_at(k)[:, 0:TILE] = total[:, k * TILE:(k + 1) * TILE]
            grad_at(k)[:, TILE:] = norms


def top_layer_kernel(rows, cols, idx_ref, ln_ref, seg_ref, *refs):
    c = idx_ref[0]
    packs, wide_packs, refs = refs[:cols], refs[cols:2 * cols], refs[2 * cols:]
    late_refs, h_refs, refs = refs[:rows], refs[rows:rows + cols], refs[rows + cols:]
    (out_ref, h_full, mid_ref, act_ref, att_ref, dkv_ref, dqx_ref, dbef_ref, dv1_ref, dv2_ref, norm_ref,
     keep_out, send_out, wkv_ref, wqo_ref, kv_ref, qx_ref, lse_ref, up_ref, dn_ref, before_ref) = refs
    place_attention(rows, cols, pack_reader(packs), 2 * HD, wkv_ref, wqo_ref)
    place_feed(rows, cols, pack_reader(wide_packs), 0, up_ref, dn_ref)
    for j in range(cols):
        h_full[j] = h_refs[j][...]
    gains = [ln_ref[k:k + 1, :] for k in range(4, 8)]
    branch, h_own = project_and_attend(
        c, h_full, wkv_ref, wqo_ref, seg_ref, kv_ref, qx_ref, att_ref, lse_ref
    )
    n1, i1 = normalize(h_own + branch)
    mid_ref[...] = n1 * gains[0] + gains[1]
    n2, i2 = feed_forward(mid_ref[...], up_ref, dn_ref, before_ref, act_ref)
    out_ref[...] = n2 * gains[2] + gains[3]
    dh = jnp.transpose(jnp.concatenate([ref[2 * HD:, :] for ref in late_refs], axis=0))
    backward(
        c, dh, gains, seg_ref, wqo_ref, kv_ref, qx_ref, att_ref, lse_ref, n1, i1, up_ref, dn_ref,
        before_ref, n2, i2, dkv_ref, dqx_ref, dbef_ref, dv1_ref, dv2_ref, norm_ref
    )
    input_gradient(wkv_ref, wqo_ref, dkv_ref, dqx_ref, dv1_ref, keep_out, send_out)


def add_moment(idx_ref, late_refs, big, at):
    first = 0 if big else HD

    @pl.when(idx_ref[2] == 0)
    def _():
        for r, ref in enumerate(late_refs):
            at[r * HD:(r + 1) * HD, :] += ref[first:first + HD, :]


def top_gradients_kernel(rows, cols, idx_ref, *refs):
    z = idx_ref[1]
    late_refs, refs = refs[:rows], refs[rows:]
    keep_out, send_out = refs[-2:]
    weight_gradients(z, cols, *refs[:-2], lambda k: (send_out if k % 2 else keep_out).at[k // 2])
    for big in (True, False):

        @pl.when((z < 2) == big)
        def _():
            add_moment(idx_ref, late_refs, big, keep_out.at[0])


def low_layer_kernel(rows, cols, idx_ref, ln_ref, seg_ref, *refs):
    late_refs, refs = refs[:rows], refs[rows:]
    z = idx_ref[1]
    (dh_keep, dh_got, dh_across, h_ref, mid_ref, act_ref, wqo_ref, kv_ref, qx_ref, att_ref, lse_ref, n1_ref,
     i1_ref, up_ref, dn_ref, before_ref, n2_ref, i2_ref, keep_out, send_out, dkv_ref, dqx_ref, dv1_ref,
     dbef_ref, dv2_ref, norm_ref) = refs
    dh = dh_keep[0] + dh_got[0] + dh_across[...]
    gains = [ln_ref[k:k + 1, :] for k in range(4)]
    backward(
        idx_ref[0], dh, gains, seg_ref, wqo_ref, kv_ref, qx_ref, att_ref, lse_ref, n1_ref[...],
        i1_ref[:, 0:1], up_ref, dn_ref, before_ref, n2_ref[...], i2_ref[:, 0:1], dkv_ref, dqx_ref, dbef_ref,
        dv1_ref, dv2_ref, norm_ref
    )
    weight_gradients(
        z ^ 2, cols, h_ref, mid_ref, act_ref, att_ref, dkv_ref, dqx_ref, dbef_ref, dv1_ref, dv2_ref, norm_ref,
        lambda k: (send_out if k % 2 else keep_out).at[k // 2]
    )
    for big in (True, False):

        @pl.when((z >= 2) == big)
        def _():
            add_moment(idx_ref, late_refs, big, keep_out.at[0])


def low_input_kernel(*refs):
    input_gradient(*refs)


def symmetric(high, low, dims):
    return dot1(high, high, dims) + (dot1(high, low, dims) + dot1(low, high, dims))


def newton_schulz(blocks, wanted):
    sizes = [jnp.sum(x * x, keepdims=True) for x in blocks]
    blocks = [x / (jnp.sqrt(s) + frob_eps) for x, s in zip(blocks, sizes)]
    for step in range(NS_STEPS):
        parts = [halves(x) for x in blocks]
        grams = [symmetric(h, l, NT) for h, l in parts]
        squares = [symmetric(*halves(a), NN) for a in grams]
        polys = [halves(newton_coefs[1] * a + newton_coefs[2] * s) for a, s in zip(grams, squares)]
        if step == NS_STEPS - 1:
            blocks = [x[:, :n] for x, n in zip(blocks, wanted)]
            parts = [(h[:, :n], l[:, :n]) for (h, l), n in zip(parts, wanted)]
        blocks = [
            newton_coefs[0] * x + (dot1(ph, h) + dot1(ph, l) + dot1(pl_, h))
            for x, (h, l), (ph, pl_) in zip(blocks, parts, polys)
        ]
    return blocks


def orthogonal_kernel(cols, idx_ref, *refs):
    z = idx_ref[1]
    top_refs, low_refs = refs[:cols], refs[cols:2 * cols]
    big_out, small_out, big, small = refs[2 * cols:]

    @pl.when(z < 2)
    def _():
        for k in range(cols):
            big[:, k * 2 * TILE:(k + 1) * 2 * TILE] = top_refs[k][...]
            small[:, k * TILE:(k + 1) * TILE] = low_refs[k][:, 0:TILE]

    @pl.when(z >= 2)
    def _():
        for k in range(cols):
            big[:, k * 2 * TILE:(k + 1) * 2 * TILE] = low_refs[k][...]
            small[:, k * TILE:(k + 1) * TILE] = top_refs[k][:, 0:TILE]

    low = low_lanes(D)
    lefts, rights = [], []
    for t in range(cols // 2):
        a = small[:, 2 * t * TILE:(2 * t + 1) * TILE]
        b = small[:, (2 * t + 1) * TILE:(2 * t + 2) * TILE]
        lefts.append(jnp.where(low, a, swap(b)))
        rights.append(jnp.where(low, swap(a), b))
    wide, left, right = newton_schulz(
        [big[...], jnp.concatenate(lefts, axis=1), jnp.concatenate(rights, axis=1)], (2 * TILE, TILE, TILE)
    )
    big_out[...] = wide * math.sqrt(FF)
    small_out[...] = jnp.where(low, left, swap(right)) * math.sqrt(D)


def first_pack_kernel(heads_hbm, outs_hbm, x_hbm, params_hbm, shard_out, heads_ref, outs_ref, params_ref, sems):
    shard_out[2 * HD:, :] = jnp.zeros((8, 2 * TILE), f32)
    copies = [
        pltpu.make_async_copy(source, target, sems.at[i])
        for i, (source, target) in enumerate(
            (
                (heads_hbm.at[0], heads_ref),
                (outs_hbm.at[0], outs_ref),
                (params_hbm, params_ref),
                (x_hbm, shard_out.at[pl.ds(HD, HD)]),
            )
        )
    ]
    for copy in copies:
        copy.start()
    for copy in copies:
        copy.wait()
    shard_out[0:HD, 0:HD] = heads_ref[1]
    shard_out[0:HD, HD:TILE] = heads_ref[2]
    shard_out[0:HD, TILE:TILE + HD] = heads_ref[0]
    shard_out[0:HD, TILE + HD:] = jnp.transpose(outs_ref[...])
    shard_out[2 * HD:, 0:HD] = params_ref[...]


def pack_kernel(
    rows, idx_ref, heads_ref, outs_ref, up_ref, dn_ref, og_ref, mh_ref, mo_ref, mu_ref, md_ref, f_out, b_out, *refs
):
    z = idx_ref[1]
    late_outs, moments = refs[:rows], refs[rows]
    f_out[0:HD, :] = up_ref[0]
    f_out[HD:2 * HD, :] = dn_ref[0]
    f_out[2 * HD:, 0:HD] = heads_ref[1, 1]
    f_out[2 * HD:, HD:TILE] = heads_ref[1, 2]
    f_out[2 * HD:, TILE:TILE + HD] = heads_ref[1, 0]
    f_out[2 * HD:, TILE + HD:] = jnp.transpose(outs_ref[1])
    b_out[0:HD, :] = up_ref[1]
    b_out[HD:2 * HD, :] = dn_ref[1]
    b_out[2 * HD:, :] = og_ref[...]
    for l in range(LAYERS):
        large, small = (0, 2) if l else (2, 0)
        moments[large, 0:HD, :] = mu_ref[l] * muon_decay
        moments[large + 1, 0:HD, :] = md_ref[l] * muon_decay
        moments[small, HD:, 0:HD] = mh_ref[l, 1] * muon_decay
        moments[small, HD:, HD:TILE] = mh_ref[l, 2] * muon_decay
        moments[small + 1, HD:, 0:HD] = mh_ref[l, 0] * muon_decay
        moments[small + 1, HD:, HD:TILE] = jnp.transpose(mo_ref[l]) * muon_decay
    for r in range(rows):
        moments[r, HD:, TILE:] = jnp.zeros((HD, TILE), f32)
    for k in range(rows):
        late_outs[k][...] = moments[z ^ k]


def update_kernel(
    rows, idx_ref, heads_ref, outs_ref, up_ref, dn_ref, params_ref, first_ref, second_ref, *refs
):
    z = idx_ref[1]
    mom_refs, step_refs, refs = refs[:rows], refs[rows:2 * rows], refs[2 * rows:]
    (heads_out, outs_out, up_out, dn_out, mh_out, mo_out, mu_out, md_out, first_out, second_out, params_out,
     mom, step) = refs
    for k in range(rows):
        mom[z ^ k] = mom_refs[k][...]
        step[z ^ k] = step_refs[k][...] * muon_rate
    for l in range(LAYERS):
        large, small = (0, 2) if l else (2, 0)
        mu_out[l] = mom[large, 0:HD, :]
        md_out[l] = mom[large + 1, 0:HD, :]
        up_out[l] = up_ref[l] - D ** -0.5 * step[large, :, 0:2 * TILE]
        dn_out[l] = dn_ref[l] - FF ** -0.5 * step[large + 1, :, 0:2 * TILE]
        kv, qo = mom[small, HD:, 0:TILE], mom[small + 1, HD:, 0:TILE]
        mh_out[l, 0] = qo[:, 0:HD]
        mh_out[l, 1] = kv[:, 0:HD]
        mh_out[l, 2] = swap(kv)[:, 0:HD]
        mo_out[l] = jnp.transpose(swap(qo))[0:HD, :]
        kv, qo = step[small, :, 2 * TILE:], step[small + 1, :, 2 * TILE:]
        heads_out[l, 0] = heads_ref[l, 0] - D ** -0.5 * qo[:, 0:HD]
        heads_out[l, 1] = heads_ref[l, 1] - D ** -0.5 * kv[:, 0:HD]
        heads_out[l, 2] = heads_ref[l, 2] - D ** -0.5 * swap(kv)[:, 0:HD]
        outs_out[l] = outs_ref[l] - (D // 16) ** -0.5 * jnp.transpose(swap(qo))[0:HD, :]
        grad = jnp.transpose(mom[small + 1, HD:, TILE:])[0:4, :]
        first = adam_first * first_ref[l] + (1.0 - adam_first) * grad
        second = adam_second * second_ref[l] + (1.0 - adam_second) * grad * grad
        first_out[l] = first
        second_out[l] = second
        params_out[l] = params_ref[l] - adam_rate * (first / (1.0 - adam_first**STEP)) / (
            jnp.sqrt(second / (1.0 - adam_second**STEP)) + adam_eps
        )


def call(body, operands, outs, scratch=(), flops=0, vmem=50):
    specs = [pl.BlockSpec(memory_space=pltpu.SMEM if x.ndim == 1 else pltpu.VMEM) for x in operands]
    moved = sum(4 * math.prod(x.shape) for x in operands) + sum(4 * math.prod(s) for s in outs)
    return pl.pallas_call(
        body,
        out_shape=[jax.ShapeDtypeStruct(s, f32) for s in outs],
        in_specs=specs,
        out_specs=[pl.BlockSpec(memory_space=pltpu.VMEM) for _ in outs],
        scratch_shapes=[pltpu.VMEM(s, f32) for s in scratch],
        compiler_params=pltpu.CompilerParams(vmem_limit_bytes=vmem * 2**20),
        cost_estimate=pl.CostEstimate(flops=flops, bytes_accessed=moved if flops else 0, transcendentals=0),
    )(*operands)


def fetched_call(body, idx, operands, outs, scratch):
    count, given = len(operands), len(outs) + len(scratch)

    def kernel(idx_ref, *refs):
        sources, rest, held, sems = refs[:count], refs[count:count + given], refs[count + given:-1], refs[-1]
        copies = [pltpu.make_async_copy(a, b, sems.at[i]) for i, (a, b) in enumerate(zip(sources, held))]
        for copy in copies:
            copy.start()
        for copy in copies:
            copy.wait()
        body(idx_ref, *held, *rest)

    return pl.pallas_call(
        kernel,
        out_shape=[jax.ShapeDtypeStruct(s, f32) for s in outs],
        in_specs=[pl.BlockSpec(memory_space=pltpu.SMEM)] + [pl.BlockSpec(memory_space=pltpu.HBM)] * count,
        out_specs=[pl.BlockSpec(memory_space=pltpu.VMEM) for _ in outs],
        scratch_shapes=[pltpu.VMEM(s, f32) for s in scratch]
        + [pltpu.VMEM(x.shape, f32) for x in operands] + [pltpu.SemaphoreType.DMA((count,))],
        compiler_params=pltpu.CompilerParams(vmem_limit_bytes=56 * 2**20),
    )(idx, *operands)


def on_device(
    layer_input,
    segment_ids,
    head_projection_weights,
    output_projection_weights,
    up_projection_weights,
    down_projection_weights,
    head_moment,
    out_moment,
    up_moment,
    down_moment,
    norm_params,
    norm_first,
    norm_second,
    output_grad,
):
    row = lax.axis_index("row").astype(jnp.int32)
    col = lax.axis_index("col").astype(jnp.int32)
    rows = lax.axis_size("row")
    cols = lax.axis_size("col")
    dps = lax.axis_size("dp")
    span = layer_input.shape[1]
    length = span * cols
    idx = jnp.stack([col, row, lax.axis_index("dp").astype(jnp.int32)])
    swap2 = lambda x: jnp.swapaxes(x, -1, -2)

    def perm(x, axis, bit):
        return lax.ppermute(x, axis, [(i, i ^ bit) for i in range(lax.axis_size(axis))])

    def spread_cols(x):
        across = perm(x, "col", 2)
        return [x, perm(x, "col", 1), across, perm(across, "col", 1)]

    def spread_rows(parts):
        return [parts[0]] + [perm(parts[k], "row", k) for k in range(1, rows)]

    heads, outs, ups = head_projection_weights, output_projection_weights, up_projection_weights
    downs = swap2(down_projection_weights)
    shard_a = pl.pallas_call(
        first_pack_kernel,
        out_shape=jax.ShapeDtypeStruct((2 * HD + 8, D), f32),
        in_specs=[pl.BlockSpec(memory_space=pltpu.HBM)] * 4,
        out_specs=pl.BlockSpec(memory_space=pltpu.VMEM),
        scratch_shapes=[
            pltpu.VMEM((3, HD, HD), f32), pltpu.VMEM((HD, HD), f32), pltpu.VMEM((8, HD), f32), pltpu.SemaphoreType.DMA((4,)),
        ],
        compiler_params=pltpu.CompilerParams(vmem_limit_bytes=60 * 2**20),
    )(heads, outs, swap2(layer_input[0]), norm_params.reshape(8, HD))
    shard_f, shard_b, *moments = fetched_call(
        functools.partial(pack_kernel, rows),
        idx, [heads, outs, ups, downs, swap2(output_grad[0]), head_moment, out_moment, up_moment, swap2(down_moment)],
        [(3 * HD, D), (3 * HD, D)] + [(2 * HD, D)] * rows, [(rows, 2 * HD, D)],
    )
    pieces = spread_rows([shard_a] * rows)
    *pieces, shard_f = lax.optimization_barrier((*pieces, shard_f))
    mine_a = jnp.stack(pieces)
    across_a, core_a = perm(mine_a, "col", 2), perm(mine_a, "col", 1)
    shard_f, _ = lax.optimization_barrier((shard_f, core_a))
    pieces_f = spread_rows([shard_f] * rows)
    mine_f = jnp.stack(pieces_f)
    across_a, mine_f = lax.optimization_barrier((across_a, mine_f))
    packs_a = [mine_a, core_a, across_a, perm(across_a, "col", 1)]
    across_f = perm(mine_f, "col", 2)
    shard_b, _ = lax.optimization_barrier((shard_b, pieces_f[1]))
    pieces_b = spread_rows([shard_b] * rows)

    full = (cols, span, D)
    pair = (2, span, D)
    own = (span, D)
    wide = (span, FF)
    half = (D, cols * TILE)
    keys = (length, cols * TILE)
    queries = (span, cols * TILE)
    one = (span, TILE)
    stats = (8, span)
    norms = (TILE, D)
    segs = [segment_ids]

    h_full, wkv, wqo, kv, qx, att, lse, mid, n1, i1, ln = call(
        functools.partial(attention_kernel, rows, cols),
        [idx] + segs + packs_a,
        [full, half, half, keys, queries, queries, stats, own, own, one, (8, D)], flops=5 * 10**9, vmem=12,
    )
    mid, across_f, *rest = lax.optimization_barrier((mid, across_f, *moments, *pieces_b))
    moments, pieces_b = rest[:rows], rest[rows:]
    packs_f = [mine_f, perm(mine_f, "col", 1), across_f, perm(across_f, "col", 1)]
    moments = spread_rows(moments)
    h_own, up, dn, before, act, n2, i2 = call(
        functools.partial(feed_kernel, rows, cols),
        [mid, ln] + packs_f,
        [own, (D, FF), (D, FF), wide, wide, own, one], flops=2 * 10**9, vmem=8,
    )
    hidden = spread_cols(h_own)
    mine_b = jnp.stack([x[:2 * HD] for x in pieces_b])
    across_b = perm(mine_b, "col", 2)
    across_b, hidden[2], *moments = lax.optimization_barrier((across_b, hidden[2], *moments))
    packs_b = [mine_b, perm(mine_b, "col", 1), across_b, perm(across_b, "col", 1)]
    top, *saved, keep, send = call(
        functools.partial(top_layer_kernel, rows, cols),
        [idx, ln] + segs + packs_f + packs_b + pieces_b + hidden,
        [own, full, own, wide, queries, keys, queries, wide, own, own, norms, pair, pair],
        [half, half, keys, queries, stats, (D, FF), (D, FF), wide], flops=20 * 10**9, vmem=18,
    )
    layer_output = top[:, :HD][None]

    def fold_core(keep, send):
        got = perm(send, "col", 1)
        return got, perm(keep[1] + got[1], "col", 2)

    got, across = fold_core(keep, send)
    keep_t, send_t = call(
        functools.partial(top_gradients_kernel, rows, cols), [idx] + moments + saved, [pair, pair],
        flops=2 * 10**9, vmem=6,
    )
    got_t = perm(send_t, "col", 1)
    half_t = keep_t[1] + got_t[1]
    got, half_t = lax.optimization_barrier((got, half_t))
    across_t = perm(half_t, "col", 2)
    keep_g, send_g, dkv, dqx, dv1 = call(
        functools.partial(low_layer_kernel, rows, cols),
        [idx, ln] + segs + moments
        + [keep, got, across, h_full, mid, act, wqo, kv, qx, att, lse, n1, i1, up, dn, before, n2, i2],
        [pair, pair, keys, queries, own], [wide, own, norms], flops=12 * 10**9, vmem=12,
    )
    send_g, across_t = lax.optimization_barrier((send_g, across_t))
    got, across = fold_core(keep_g, send_g)
    mine = keep_g[0] + got[0] + across
    top = keep_t[0] + got_t[0] + across_t
    top, mine = [
        lax.optimization_barrier(x + perm(x, "dp", 1) if dps == 2 else lax.psum(x, "dp")) for x in (top, mine)
    ]
    keep, send = call(
        low_input_kernel, [wkv, wqo, dkv, dqx, dv1], [pair, pair], flops=2 * 10**9, vmem=6,
    )
    got, across = fold_core(keep, send)
    input_grad = (keep[0] + got[0] + across)[:, :HD][None]

    tops, parts = spread_cols(top), spread_cols(mine)
    large, small = jnp.where(row < 2, top, mine), jnp.where(row < 2, mine, top)
    moms = jnp.concatenate([large.reshape(rows, HD, D), small.reshape(rows, HD, D)], axis=1)
    moms = spread_rows([moms[k] for k in range(rows)])
    parts[2], moms[1] = lax.optimization_barrier((parts[2], moms[1]))
    parts[3] = perm(parts[2], "col", 1)
    large, small = call(
        functools.partial(orthogonal_kernel, cols), [idx] + tops + parts, [own, (D, TILE)],
        [(D, FF), (D, cols * TILE)], flops=8 * 10**9, vmem=16,
    )
    steps = jnp.concatenate([large.reshape(rows, HD, D), small.reshape(rows, HD, TILE)], axis=2)
    steps = spread_rows([steps[k] for k in range(rows)])
    three = (LAYERS, 4, HD)
    updates = list(call(
        functools.partial(update_kernel, rows),
        [idx, heads, outs, ups, downs, norm_params, norm_first, norm_second] + moms + steps,
        [heads.shape, outs.shape, ups.shape, downs.shape] * 2 + [three] * 3,
        [(rows, 2 * HD, D), (rows, HD, D + TILE)], vmem=8,
    ))
    for at in (3, 7):
        updates[at] = swap2(updates[at])
    return (layer_output, input_grad, *updates)


def solution(mesh):
    placed = (
        P("dp", "col", "row"),
        P("dp", None),
        P(None, None, "row", "col"),
        P(None, "col", "row"),
        P(None, "row", "col"),
        P(None, "col", "row"),
        P(None, None, "row", "col"),
        P(None, "col", "row"),
        P(None, "row", "col"),
        P(None, "col", "row"),
        P(None, None, "row"),
        P(None, None, "row"),
        P(None, None, "row"),
        P("dp", "col", "row"),
    )
    return jax.shard_map(
        on_device,
        mesh=mesh,
        in_specs=placed,
        out_specs=(
            P("dp", "col", "row"),
            P("dp", "col", "row"),
            P(None, None, "row", "col"),
            P(None, "col", "row"),
            P(None, "row", "col"),
            P(None, "col", "row"),
            P(None, None, "row", "col"),
            P(None, "col", "row"),
            P(None, "row", "col"),
            P(None, "col", "row"),
            P(None, None, "row"),
            P(None, None, "row"),
            P(None, None, "row"),
        ),
        check_vma=False,
    )
```
